32 devices in a mesh: dp: 8 (over z, x), tensor: 4 (over y, core).
Axes of the slice: x: 2, y: 2, z: 4, core: 2. Of those that a mesh axis runs over, the one named last changes fastest.
Arguments:
- target: bfloat16 [16384, 768], P('dp'), may hold values from -6 to 6
- memory: bfloat16 [16384, 768], P('dp'), may hold values from -6 to 6
- cotangent: bfloat16 [16384, 768], P('dp'), may hold values from -6 to 6
- tgt_seg: int32 [16, 1024], P('dp'), may hold values from 0 to 3, never falling along the last dimension, each value on 1 to 512 neighbouring positions
- mem_seg: int32 [16, 1024], P('dp'), may hold values from 0 to 3, never falling along the last dimension, each value on 1 to 512 neighbouring positions
- pad_len: int32 [16], P('dp'), may hold values from 0 to 128
- step_count: int32 [], replicated, may hold values from 2 to 20
- self_in: float32 [3, 768, 768], P(None, 'dp', 'tensor'), may hold values from -0.21875 to 0.21875
- self_in_first: float32 [3, 768, 768], P(None, 'dp', 'tensor'), may hold values from -0.00021362305 to 0.00021362305
- self_in_second: float32 [3, 768, 768], P(None, 'dp', 'tensor'), may hold values from 1.059121e-10 to 4.236484e-10
- self_out: float32 [768, 768], P('tensor', 'dp'), may hold values from -1.75 to 1.75
- self_out_first: float32 [768, 768], P('tensor', 'dp'), may hold values from -5.340576e-05 to 5.340576e-05
- self_out_second: float32 [768, 768], P('tensor', 'dp'), may hold values from 6.619506e-12 to 2.6478025e-11
- cross_in: float32 [3, 768, 768], P(None, 'dp', 'tensor'), may hold values from -0.21875 to 0.21875
- cross_in_first: float32 [3, 768, 768], P(None, 'dp', 'tensor'), may hold values from -0.00021362305 to 0.00021362305
- cross_in_second: float32 [3, 768, 768], P(None, 'dp', 'tensor'), may hold values from 1.059121e-10 to 4.236484e-10
- cross_out: float32 [768, 768], P('tensor', 'dp'), may hold values from -1.75 to 1.75
- cross_out_first: float32 [768, 768], P('tensor', 'dp'), may hold values from -2.2888184e-05 to 2.2888184e-05
- cross_out_second: float32 [768, 768], P('tensor', 'dp'), may hold values from 1.059121e-12 to 4.236484e-12
- ffn_in: float32 [768, 3072], P('dp', 'tensor'), may hold values from -0.21875 to 0.21875
- ffn_in_first: float32 [768, 3072], P('dp', 'tensor'), may hold values from -0.00021362305 to 0.00021362305
- ffn_in_second: float32 [768, 3072], P('dp', 'tensor'), may hold values from 1.059121e-10 to 4.236484e-10
- ffn_out: float32 [3072, 768], P('tensor', 'dp'), may hold values from -0.28867513 to 0.28867513
- ffn_out_first: float32 [3072, 768], P('tensor', 'dp'), may hold values from -0.00021362305 to 0.00021362305
- ffn_out_second: float32 [3072, 768], P('tensor', 'dp'), may hold values from 1.059121e-10 to 4.236484e-10
- norm_params: float32 [6, 768], P(None, 'dp'), may hold values from -0.8 to 3.6, as said below
- norm_params_first: float32 [6, 768], P(None, 'dp'), may hold values from -0.00061035156 to 0.00061035156
- norm_params_second: float32 [6, 768], P(None, 'dp'), may hold values from 9.532088e-10 to 3.8128354e-09
Outputs:
- global_norm: float32 [], replicated
- block_out: float32 [16384, 768], P('dp')
- grad_target: float32 [16384, 768], P('dp')
- grad_memory: float32 [16384, 768], P('dp')
- self_in_new: float32 [3, 768, 768], P(None, 'dp', 'tensor')
- self_in_copy: bfloat16 [3, 768, 768], P(None, 'dp', 'tensor')
- self_in_first_new: float32 [3, 768, 768], P(None, 'dp', 'tensor')
- self_in_second_new: float32 [3, 768, 768], P(None, 'dp', 'tensor')
- self_out_new: float32 [768, 768], P('tensor', 'dp')
- self_out_copy: bfloat16 [768, 768], P('tensor', 'dp')
- self_out_first_new: float32 [768, 768], P('tensor', 'dp')
- self_out_second_new: float32 [768, 768], P('tensor', 'dp')
- cross_in_new: float32 [3, 768, 768], P(None, 'dp', 'tensor')
- cross_in_copy: bfloat16 [3, 768, 768], P(None, 'dp', 'tensor')
- cross_in_first_new: float32 [3, 768, 768], P(None, 'dp', 'tensor')
- cross_in_second_new: float32 [3, 768, 768], P(None, 'dp', 'tensor')
- cross_out_new: float32 [768, 768], P('tensor', 'dp')
- cross_out_copy: bfloat16 [768, 768], P('tensor', 'dp')
- cross_out_first_new: float32 [768, 768], P('tensor', 'dp')
- cross_out_second_new: float32 [768, 768], P('tensor', 'dp')
- ffn_in_new: float32 [768, 3072], P('dp', 'tensor')
- ffn_in_copy: bfloat16 [768, 3072], P('dp', 'tensor')
- ffn_in_first_new: float32 [768, 3072], P('dp', 'tensor')
- ffn_in_second_new: float32 [768, 3072], P('dp', 'tensor')
- ffn_out_new: float32 [3072, 768], P('tensor', 'dp')
- ffn_out_copy: bfloat16 [3072, 768], P('tensor', 'dp')
- ffn_out_first_new: float32 [3072, 768], P('tensor', 'dp')
- ffn_out_second_new: float32 [3072, 768], P('tensor', 'dp')
- norm_params_new: float32 [6, 768], P(None, 'dp')
- norm_params_copy: bfloat16 [6, 768], P(None, 'dp')
- norm_params_first_new: float32 [6, 768], P(None, 'dp')
- norm_params_second_new: float32 [6, 768], P(None, 'dp')
The draws below stay inside these ranges and needn't reach their ends.
Inputs may be any that keep to these rules, and one draw needn't show every extreme that they name: `tgt_seg`: in each row the ids never fall and each of the 4 ids occurs. `mem_seg`: in each row the ids never fall and each of the 4 ids occurs. `norm_params`: rows 0 to 2 are positive gains, rows 3 to 5 shifts.
All inputs are finite; a program needn't handle non-finite values.
Results may differ from the reference program's by a relative error of at most 0.039.
Values may be sent and summed in bfloat16 or wider, within the bound.
A program may use at most 192 MiB of HBM per device.

```python
import math
import jax
import jax.numpy as jnp
import numpy as np
from jax import lax

D = 768
HD = 64
FF = 3072
LEN = 1024
MLEN = 1024
DOCS = 4
ROWS = 16
TOKENS = 16384
MTOKENS = 16384
PARAMS = 9441792
N_TENSOR = 4


def draw_norm_params(key, part):
    key = jax.random.fold_in(key, 11)
    normal_part = jnp.clip(jax.random.normal(key, (6, D), jnp.float32), -4.0, 4.0)
    row_index = jnp.arange(6)[:, None]
    ramp = jnp.exp(jnp.linspace(jnp.log(0.6), jnp.log(1.8), D, dtype=jnp.float32))
    return jnp.where(row_index < 3, (1.0 + 0.1 * normal_part) * ramp[None, :], 0.2 * normal_part)


def draw_ffn_out(key, part):
    key = jax.random.fold_in(key, 23)
    normal_part = jnp.clip(jax.random.normal(key, (FF, D), jnp.float32), -4.0, 4.0)
    ramp = jnp.exp(jnp.linspace(jnp.log(0.55), jnp.log(1.65), FF, dtype=jnp.float32))
    return normal_part * ramp[:, None] * (4.0 / FF) ** 0.5


def touch_ends(drawn, rng, low, high):
    shape = drawn.shape
    spot = [jax.random.randint(jax.random.fold_in(rng, axis), (), 0, shape[axis]) for axis in range(len(shape))]
    drawn = drawn.at[tuple(spot)].set(low)
    longest = shape.index(max(shape))
    spot[longest] = (spot[longest] + 1) % shape[longest]
    return drawn.at[tuple(spot)].set(high)


def block_levels(own_key, extent, cuts, smallest, top_value):
    def one(dim, blocks):
        steps = jax.random.uniform(jax.random.fold_in(jax.random.fold_in(own_key, 6), dim), (blocks,), jnp.float32, smallest / len(cuts), top_value / len(cuts))
        return jnp.repeat(jnp.exp(steps), extent[dim] // blocks).reshape((-1,) + (1,) * (len(extent) - dim - 1))

    loudness = one(*cuts[0])
    for cut in cuts[1:]:
        loudness = loudness * one(*cut)
    return loudness


def profile(amount, total, reach, slope):
    portions = [(1 << 20) // math.isqrt(standing ** slope) + 1 for standing in range(2, amount + 1)]
    spare, counts = total - reach - (amount - 1), [1] * (amount - 1)
    while spare > 0:
        candidates = [i for i in range(amount - 1) if counts[i] < reach]
        whole, budget = sum([portions[i] for i in candidates]), spare
        for i in candidates:
            addition = min(reach - counts[i], max(1, budget * portions[i] // whole), spare)
            counts[i] = counts[i] + addition
            spare = spare - addition
    return np.array([reach] + counts)


def ragged(own_key, number_of, total, reach, slope):
    if number_of == 2:
        one = jax.random.randint(own_key, (), max(1, total - reach), min(reach, total - 1) + 1)
        return jnp.stack([one, total - one])
    lengths = jnp.asarray(profile(number_of, total, reach, slope), jnp.int32)
    pairs = (number_of - 1) // 2
    donor, taker = lengths[1:1 + 2 * pairs:2], lengths[2:2 + 2 * pairs:2]
    margin = jnp.minimum(donor - 1, reach - taker)
    moved = jax.random.randint(jax.random.fold_in(own_key, 1), (pairs,), 0, 1 << 20) % (margin + 1)
    lengths = lengths.at[1:1 + 2 * pairs:2].set(donor - moved).at[2:2 + 2 * pairs:2].set(taker + moved)
    return lengths[jax.random.permutation(jax.random.fold_in(own_key, 2), number_of)]


def normal_values(key, dims, scale, reach, split=(), held_as=jnp.bfloat16):
    drawn = scale * jax.random.normal(key, dims, jnp.float32)
    if split:
        drawn = drawn * block_levels(key, dims, split, -0.22, 0.18)
    return jnp.clip(drawn, -reach, reach).astype(held_as)


def setup_inputs(seed: int = 0) -> dict:
    arg_keys = jax.random.split(jax.random.key(seed), 29)
    target = normal_values(arg_keys[0], (TOKENS, D), 1.0, 6.0, ((0, 8),))
    memory = normal_values(arg_keys[1], (MTOKENS, D), 1.0, 6.0, ((0, 8),))
    cotangent = normal_values(arg_keys[2], (TOKENS, D), 1.0, 6.0, ((0, 8),))
    tgt_seg = jax.vmap(lambda own: jnp.searchsorted(jnp.cumsum(ragged(own, DOCS, LEN, LEN // 2, 1)), jnp.arange(LEN), side="right"))(jax.random.split(arg_keys[3], ROWS)).reshape((ROWS, LEN)).astype(jnp.int32)
    mem_seg = jax.vmap(lambda own: jnp.searchsorted(jnp.cumsum(ragged(own, DOCS, MLEN, MLEN // 2, 1)), jnp.arange(MLEN), side="right"))(jax.random.split(arg_keys[4], ROWS)).reshape((ROWS, MLEN)).astype(jnp.int32)
    pad_len = touch_ends(jax.random.randint(arg_keys[5], (ROWS,), 0, LEN // 8 + 1), jax.random.fold_in(arg_keys[5], 1), 0, (LEN // 8 + 1) - 1).astype(jnp.int32)
    step_count = jax.random.randint(arg_keys[6], (), 2, 21).astype(jnp.int32)
    self_in = normal_values(arg_keys[7], (3, D, D), D ** -0.5, 0.21875, ((1, 8), (2, 4)), jnp.float32)
    self_in_first = normal_values(arg_keys[8], (3, D, D), (0.111 / PARAMS ** 0.5), 0.00021362305, ((1, 8), (2, 4)), jnp.float32)
    self_in_second = jnp.clip(jnp.exp(math.log(4.236483941433278e-10) - 1.3862944 * jax.random.uniform(arg_keys[9], (3, D, D), jnp.float32) ** block_levels(arg_keys[9], (3, D, D), ((1, 8), (2, 4)), -0.2, 0.2)), 1.0591209853583194e-10, 4.236483941433278e-10)
    self_out = normal_values(arg_keys[10], (D, D), (D // 64) ** -0.5, 1.75, ((0, 4), (1, 8)), jnp.float32)
    self_out_first = normal_values(arg_keys[11], (D, D), (0.028 / PARAMS ** 0.5), 5.340576171875e-05, ((0, 4), (1, 8)), jnp.float32)
    self_out_second = jnp.clip(jnp.exp(math.log(2.6478024633957986e-11) - 1.3862944 * jax.random.uniform(arg_keys[12], (D, D), jnp.float32) ** block_levels(arg_keys[12], (D, D), ((0, 4), (1, 8)), -0.2, 0.2)), 6.6195061584894965e-12, 2.6478024633957986e-11)
    cross_in = normal_values(arg_keys[13], (3, D, D), D ** -0.5, 0.21875, ((1, 8), (2, 4)), jnp.float32)
    cross_in_first = normal_values(arg_keys[14], (3, D, D), (0.111 / PARAMS ** 0.5), 0.00021362305, ((1, 8), (2, 4)), jnp.float32)
    cross_in_second = jnp.clip(jnp.exp(math.log(4.236483941433278e-10) - 1.3862944 * jax.random.uniform(arg_keys[15], (3, D, D), jnp.float32) ** block_levels(arg_keys[15], (3, D, D), ((1, 8), (2, 4)), -0.2, 0.2)), 1.0591209853583194e-10, 4.236483941433278e-10)
    cross_out = normal_values(arg_keys[16], (D, D), (D // 64) ** -0.5, 1.75, ((0, 4), (1, 8)), jnp.float32)
    cross_out_first = normal_values(arg_keys[17], (D, D), (0.0111 / PARAMS ** 0.5), 2.288818359375e-05, ((0, 4), (1, 8)), jnp.float32)
    cross_out_second = jnp.clip(jnp.exp(math.log(4.236483993474982e-12) - 1.3862944 * jax.random.uniform(arg_keys[18], (D, D), jnp.float32) ** block_levels(arg_keys[18], (D, D), ((0, 4), (1, 8)), -0.2, 0.2)), 1.0591209983687455e-12, 4.236483993474982e-12)
    ffn_in = normal_values(arg_keys[19], (D, FF), D ** -0.5, 0.21875, ((0, 8), (1, 4)), jnp.float32)
    ffn_in_first = normal_values(arg_keys[20], (D, FF), (0.111 / PARAMS ** 0.5), 0.00021362305, ((0, 8), (1, 4)), jnp.float32)
    ffn_in_second = jnp.clip(jnp.exp(math.log(4.236483941433278e-10) - 1.3862944 * jax.random.uniform(arg_keys[21], (D, FF), jnp.float32) ** block_levels(arg_keys[21], (D, FF), ((0, 8), (1, 4)), -0.2, 0.2)), 1.0591209853583194e-10, 4.236483941433278e-10)
    ffn_out = draw_ffn_out(jax.random.fold_in(arg_keys[28], 71), 0)
    ffn_out_first = normal_values(arg_keys[23], (FF, D), (0.111 / PARAMS ** 0.5), 0.00021362305, ((0, 4), (1, 8)), jnp.float32)
    ffn_out_second = jnp.clip(jnp.exp(math.log(4.236483941433278e-10) - 1.3862944 * jax.random.uniform(arg_keys[24], (FF, D), jnp.float32) ** block_levels(arg_keys[24], (FF, D), ((0, 4), (1, 8)), -0.2, 0.2)), 1.0591209853583194e-10, 4.236483941433278e-10)
    norm_params = draw_norm_params(jax.random.fold_in(arg_keys[28], 71), 0)
    norm_params_first = normal_values(arg_keys[26], (6, D), (0.333 / PARAMS ** 0.5), 0.00061035156, ((1, 8),), jnp.float32)
    norm_params_second = jnp.clip(jnp.exp(math.log(3.812835380756496e-09) - 1.3862944 * jax.random.uniform(arg_keys[27], (6, D), jnp.float32) ** block_levels(arg_keys[27], (6, D), ((1, 8),), -0.2, 0.2)), 9.53208845189124e-10, 3.812835380756496e-09)
    return {"target": target, "memory": memory, "cotangent": cotangent, "tgt_seg": tgt_seg, "mem_seg": mem_seg, "pad_len": pad_len, "step_count": step_count, "self_in": self_in, "self_in_first": self_in_first, "self_in_second": self_in_second, "self_out": self_out, "self_out_first": self_out_first, "self_out_second": self_out_second, "cross_in": cross_in, "cross_in_first": cross_in_first, "cross_in_second": cross_in_second, "cross_out": cross_out, "cross_out_first": cross_out_first, "cross_out_second": cross_out_second, "ffn_in": ffn_in, "ffn_in_first": ffn_in_first, "ffn_in_second": ffn_in_second, "ffn_out": ffn_out, "ffn_out_first": ffn_out_first, "ffn_out_second": ffn_out_second, "norm_params": norm_params, "norm_params_first": norm_params_first, "norm_params_second": norm_params_second}


@jax.custom_vjp
def low(v):
    return lax.optimization_barrier(v.astype(jnp.bfloat16)).astype(jnp.float32)

@jax.custom_vjp
def low_back(v):
    return v

def low_keep(v):
    return (low(v), None)

def low_pass(kept, grad):
    return (grad,)

def back_keep(v):
    return (v, None)

def back_low(kept, grad):
    return (low(grad),)
low.defvjp(low_keep, low_pass)
low_back.defvjp(back_keep, back_low)
EPS_NORM = 1e-05
NEG_FILL = -1000000000.0
BETA_ONE = 0.9
BETA_TWO = 0.999
EPS_ADAM = 1e-08
RATE_MATRIX = 0.05
RATE_OUTPUT = 0.25
RATE_NORMS = 0.75
DECAY_RATE = 0.1
CLIP_LIMIT = 1.0
GELU_COEF = 0.044715
HIGHEST = lax.Precision.HIGHEST

def matmul(left_side, right_side):
    return jnp.dot(left_side, right_side, precision=HIGHEST, preferred_element_type=jnp.float32)

def gelu_tanh(values):
    inner = math.sqrt(2.0 / math.pi) * (values + GELU_COEF * values * values * values)
    return 0.5 * values * (1.0 + jnp.tanh(inner))

def layer_norm(values, norm_gain, norm_shift):
    centre = values - lax.optimization_barrier(jnp.mean(values, -1, keepdims=True))
    spread = lax.optimization_barrier(jnp.mean(centre * centre, -1, keepdims=True))
    return centre * lax.rsqrt(spread + EPS_NORM) * norm_gain + norm_shift

def attend(query_rows, key_rows, value_rows, allowed):
    head_count = query_rows.shape[1] // HD
    query_heads = query_rows.reshape(query_rows.shape[0], head_count, HD)
    key_heads = key_rows.reshape(key_rows.shape[0], head_count, HD)
    value_heads = value_rows.reshape(value_rows.shape[0], head_count, HD)
    scores = jnp.einsum('qhd,khd->hqk', query_heads, key_heads, precision=HIGHEST) * (1.0 / math.sqrt(HD))
    scores = low_back(scores)
    scores = jnp.where(allowed[None], scores, NEG_FILL)
    shifted = jnp.exp(scores - lax.optimization_barrier(jnp.max(scores, -1, keepdims=True)))
    attn_weights = shifted / lax.optimization_barrier(jnp.sum(shifted, -1, keepdims=True))
    attended = jnp.einsum('hqk,khd->qhd', low(attn_weights), value_heads, precision=HIGHEST)
    return attended.reshape(query_rows.shape[0], head_count * HD)

def attention_branch(source, memory_src, proj_in, proj_out, allowed):
    col_width = D // N_TENSOR
    summed = jnp.zeros((source.shape[0], D), jnp.float32)
    for head_group in range(N_TENSOR):
        col_slice = slice(head_group * col_width, (head_group + 1) * col_width)
        query_in = low_back(source)
        if memory_src is None:
            keys_in = query_in
        else:
            keys_in = low_back(memory_src)
        query_rows = low_back(low(matmul(query_in, proj_in[0][:, col_slice])))
        key_rows = low_back(low(matmul(keys_in, proj_in[1][:, col_slice])))
        value_rows = low_back(low(matmul(keys_in, proj_in[2][:, col_slice])))
        attended = low_back(low(attend(query_rows, key_rows, value_rows, allowed)))
        summed = summed + low(matmul(attended, proj_out[col_slice, :]))
    return low_back(summed)

def feed_forward(source, proj_up, proj_down):
    hidden_width = FF // N_TENSOR
    summed = jnp.zeros((source.shape[0], D), jnp.float32)
    for head_group in range(N_TENSOR):
        hid_slice = slice(head_group * hidden_width, (head_group + 1) * hidden_width)
        pre_act = low_back(matmul(low_back(source), proj_up[:, hid_slice]))
        hidden = low(gelu_tanh(pre_act))
        summed = summed + low(matmul(hidden, proj_down[hid_slice, :]))
    return low_back(summed)

def row_forward(params, target_row, memory_row, tgt_ids, mem_ids, valid_len):
    copies = [low(weight) for weight in params]
    proj_self_in, proj_self_out, proj_cross_in, proj_cross_out, proj_up, proj_down, norm_copy = copies
    positions = jnp.arange(LEN)
    causal = positions[None, :] <= positions[:, None]
    same_doc = tgt_ids[:, None] == tgt_ids[None, :]
    live_key = (positions[None, :] < valid_len) | (positions[None, :] == positions[:, None])
    self_allowed = causal & same_doc & live_key
    cross_allowed = tgt_ids[:, None] == mem_ids[None, :]
    normed_one = low(layer_norm(target_row, norm_copy[0], norm_copy[3]))
    hidden_one = target_row + attention_branch(normed_one, None, proj_self_in, proj_self_out, self_allowed)
    normed_two = low(layer_norm(hidden_one, norm_copy[1], norm_copy[4]))
    hidden_two = hidden_one + attention_branch(normed_two, memory_row, proj_cross_in, proj_cross_out, cross_allowed)
    normed_three = low(layer_norm(hidden_two, norm_copy[2], norm_copy[5]))
    return hidden_two + feed_forward(normed_three, proj_up, proj_down)

def adam_update(weight, gradient, first, second, clip_factor, step_float, rate, decay):
    scaled = gradient * clip_factor
    first_new = BETA_ONE * first + (1.0 - BETA_ONE) * scaled
    second_new = BETA_TWO * second + (1.0 - BETA_TWO) * scaled * scaled
    first_hat = first_new / (1.0 - jnp.power(BETA_ONE, step_float))
    second_hat = second_new / (1.0 - jnp.power(BETA_TWO, step_float))
    weight_new = weight - rate * (first_hat / (jnp.sqrt(second_hat) + EPS_ADAM) + decay * weight)
    return (weight_new, weight_new.astype(jnp.bfloat16), first_new, second_new)

def reference(target, memory, cotangent, tgt_seg, mem_seg, pad_len, step_count, self_in, self_in_first, self_in_second, self_out, self_out_first, self_out_second, cross_in, cross_in_first, cross_in_second, cross_out, cross_out_first, cross_out_second, ffn_in, ffn_in_first, ffn_in_second, ffn_out, ffn_out_first, ffn_out_second, norm_params, norm_params_first, norm_params_second):
    params = (self_in, self_out, cross_in, cross_out, ffn_in, ffn_out, norm_params)
    target_rows = target.astype(jnp.float32).reshape(ROWS, LEN, D)
    memory_rows = memory.astype(jnp.float32).reshape(ROWS, MLEN, D)
    cot_rows = cotangent.astype(jnp.float32).reshape(ROWS, LEN, D)
    valid_lens = LEN - pad_len

    def one_row(totals, inputs):
        target_row, memory_row, cot_row, tgt_ids, mem_ids, valid_len = inputs

        def forward(weights, target_in, memory_in):
            return row_forward(weights, target_in, memory_in, tgt_ids, mem_ids, valid_len)
        block_row, pullback = jax.vjp(forward, params, target_row, memory_row)
        weight_grads, target_grad, memory_grad = pullback(cot_row)
        totals = tuple((running + extra for running, extra in zip(totals, weight_grads)))
        return (totals, (block_row, target_grad, memory_grad))
    start_totals = tuple((jnp.zeros_like(weight) for weight in params))
    totals, outputs = lax.scan(one_row, start_totals, (target_rows, memory_rows, cot_rows, tgt_seg, mem_seg, valid_lens))
    block_rows, target_grads, memory_grads = outputs
    squares = jnp.zeros((), jnp.float32)
    for gradient in totals:
        squares = squares + jnp.sum(gradient * gradient)
    global_norm = jnp.sqrt(squares)
    clip_factor = CLIP_LIMIT / jnp.maximum(global_norm, CLIP_LIMIT)
    step_float = step_count.astype(jnp.float32)
    sin_new, sin_copy, sin_first, sin_second = adam_update(self_in, totals[0], self_in_first, self_in_second, clip_factor, step_float, RATE_MATRIX, DECAY_RATE)
    sout_new, sout_copy, sout_first, sout_second = adam_update(self_out, totals[1], self_out_first, self_out_second, clip_factor, step_float, RATE_OUTPUT, DECAY_RATE)
    cin_new, cin_copy, cin_first, cin_second = adam_update(cross_in, totals[2], cross_in_first, cross_in_second, clip_factor, step_float, RATE_MATRIX, DECAY_RATE)
    cout_new, cout_copy, cout_first, cout_second = adam_update(cross_out, totals[3], cross_out_first, cross_out_second, clip_factor, step_float, RATE_OUTPUT, DECAY_RATE)
    fin_new, fin_copy, fin_first, fin_second = adam_update(ffn_in, totals[4], ffn_in_first, ffn_in_second, clip_factor, step_float, RATE_MATRIX, DECAY_RATE)
    fout_new, fout_copy, fout_first, fout_second = adam_update(ffn_out, totals[5], ffn_out_first, ffn_out_second, clip_factor, step_float, RATE_MATRIX, DECAY_RATE)
    norm_new, norm_copy, norm_first, norm_second = adam_update(norm_params, totals[6], norm_params_first, norm_params_second, clip_factor, step_float, RATE_NORMS, 0.0)
    return (global_norm, block_rows.reshape(TOKENS, D), target_grads.reshape(TOKENS, D), memory_grads.reshape(MTOKENS, D), sin_new, sin_copy, sin_first, sin_second, sout_new, sout_copy, sout_first, sout_second, cin_new, cin_copy, cin_first, cin_second, cout_new, cout_copy, cout_first, cout_second, fin_new, fin_copy, fin_first, fin_second, fout_new, fout_copy, fout_first, fout_second, norm_new, norm_copy, norm_first, norm_second)
```

```python
from functools import partial
import math

import jax
import jax.numpy as jnp
from jax import lax
from jax.experimental import pallas as pl
from jax.experimental.pallas import tpu as pltpu
from jax.sharding import Mesh, PartitionSpec as P

HD = 64
EPS_NORM = 1e-05
NEG_FILL = -1000000000.0
BETA_ONE = 0.9
BETA_TWO = 0.999
EPS_ADAM = 1e-08
RATE_MATRIX = 0.05
RATE_OUTPUT = 0.25
RATE_NORMS = 0.75
DECAY_RATE = 0.1
CLIP_LIMIT = 1.0
GELU_COEF = 0.044715

BF = jnp.bfloat16
F32 = jnp.float32
RB = 256
PW = 768
MESH_ID = pl.DeviceIdType.MESH
VMEM_LIMIT = 60 * 1024 * 1024


def nn(a, b):
    return lax.dot_general(a, b, (((1,), (0,)), ((), ())), preferred_element_type=F32)


def nt(a, b):
    return lax.dot_general(a, b, (((1,), (1,)), ((), ())), preferred_element_type=F32)


def vm(n=1):
    return [pl.BlockSpec(memory_space=pltpu.VMEM)] * n


def anym(n=1):
    return [pl.BlockSpec(memory_space=pl.ANY)] * n


def sds(shape, dtype):
    return jax.ShapeDtypeStruct(shape, dtype)


def params(**kw):
    return pltpu.CompilerParams(vmem_limit_bytes=VMEM_LIMIT, **kw)


def block(i, size=RB):
    return pl.ds(pl.multiple_of(i * size, size), size)


def gelu_with_slope(values):
    root = math.sqrt(2.0 / math.pi)
    square = values * values
    tangent = jnp.tanh(values * (root + (root * GELU_COEF) * square))
    half = 0.5 + 0.5 * tangent
    output = values * half
    slope = half + 0.5 * output * (1.0 - tangent) * (2.0 * root + (6.0 * root * GELU_COEF) * square)
    return output, slope


def norm_stats(values):
    centre = values - jnp.mean(values, -1, keepdims=True)
    inverse = lax.rsqrt(jnp.mean(centre * centre, -1, keepdims=True) + EPS_NORM)
    return centre * inverse, inverse


def norm_forward(values, gain, shift):
    scaled, _ = norm_stats(values)
    return (scaled * gain + shift).astype(BF)


def norm_backward(upstream, values, gain):
    scaled, inverse = norm_stats(values)
    weighted = upstream * gain
    product = upstream * scaled
    result = inverse * (
        weighted
        - jnp.mean(weighted, -1, keepdims=True)
        - scaled * jnp.mean(weighted * scaled, -1, keepdims=True)
    )
    return result, jnp.sum(product, 0, keepdims=True), jnp.sum(upstream, 0, keepdims=True)


def fetch_row(src, dst, sem):
    rows = dst.shape[0]
    start = lax.axis_index("ta") * rows
    return pltpu.make_async_copy(src.at[pl.ds(start, rows)], dst, sem)


def join_groups(packed, joined):
    depth, width = packed.shape[1], packed.shape[2] // 4

    @pl.loop(0, depth // 128)
    def _(i):
        first, second = packed[0, block(i, 128), :], packed[1, block(i, 128), :]
        pieces = []
        for s in range(4):
            pieces += [first[:, s * width : (s + 1) * width], second[:, s * width : (s + 1) * width]]
        joined[block(i, 128), :] = jnp.concatenate(pieces, axis=1)


def split_groups(joined_rows, packed, rows):
    width = joined_rows.shape[1] // 8
    for t in range(2):
        packed[t, rows, :] = jnp.concatenate(
            [joined_rows[:, (2 * s + t) * width : (2 * s + t + 1) * width] for s in range(4)], axis=1
        ).astype(BF)


def transpose_into(src, dst):
    @pl.loop(0, src.shape[0] // RB)
    def _(i):
        dst[:, block(i)] = src[block(i), :].T


def head_masks(rows):
    lane = lax.broadcasted_iota(jnp.int32, (rows, 2 * HD), 1)
    return lane < HD


def keep_half(values, low_half, head):
    zero = jnp.zeros_like(values)
    return jnp.where(low_half, values, zero) if head == 0 else jnp.where(low_half, zero, values)


def attend(qkv, bias_of, causal, out, logsum, bias):
    rows, cols = out.shape
    pairs = cols // (2 * HD)

    def one(q_rows, keys, pair):
        lanes = block(pair, 2 * HD)
        k_lanes = pl.ds(pl.multiple_of(cols + pair * 2 * HD, 2 * HD), 2 * HD)
        v_lanes = pl.ds(pl.multiple_of(2 * cols + pair * 2 * HD, 2 * HD), 2 * HD)
        query, key, value = qkv[q_rows, lanes], qkv[0:keys, k_lanes], qkv[0:keys, v_lanes]
        low_half = head_masks(RB)
        outs, sums = [], []
        for head in range(2):
            scores = nt(keep_half(query, low_half, head), key) + bias[:, 0:keys]
            peak = jnp.max(scores, -1, keepdims=True)
            shifted = jnp.exp(scores - peak)
            total = jnp.sum(shifted, -1, keepdims=True)
            outs.append(nn(shifted.astype(BF), value) / total)
            sums.append(peak + jnp.log(total))
        out[q_rows, lanes] = jnp.where(low_half, outs[0], outs[1]).astype(BF)
        both = jnp.where(low_half, sums[0], sums[1]).T
        logsum[pair, :, q_rows] = jnp.concatenate([both[0:1], both[HD : HD + 1]], axis=0)

    if causal:
        for i in range(rows // RB):
            keys = (i + 1) * RB
            bias[:, 0:keys] = bias_of(i, keys)
            pl.loop(0, pairs)(partial(one, pl.ds(i * RB, RB), keys))
    else:

        @pl.loop(0, rows // RB)
        def _(i):
            bias[...] = bias_of(i, rows)
            pl.loop(0, pairs)(partial(one, block(i), rows))


def attend_back(qkv, attended, grad, logsum, bias_of, causal, dqkv, dk_sum, dv_sum, bias):
    rows, cols = attended.shape
    pairs = cols // (2 * HD)
    dk_sum[...] = jnp.zeros_like(dk_sum)
    dv_sum[...] = jnp.zeros_like(dv_sum)

    def one(q_rows, keys, pair):
        lanes = block(pair, 2 * HD)
        k_lanes = pl.ds(pl.multiple_of(cols + pair * 2 * HD, 2 * HD), 2 * HD)
        v_lanes = pl.ds(pl.multiple_of(2 * cols + pair * 2 * HD, 2 * HD), 2 * HD)
        query, key, value = qkv[q_rows, lanes], qkv[0:keys, k_lanes], qkv[0:keys, v_lanes]
        out_grad = grad[q_rows, lanes]
        low_half = head_masks(RB)
        low_keys = head_masks(keys)
        product = (out_grad.astype(F32) * attended[q_rows, lanes].astype(F32)).T
        dq = dk = dv = None
        for head in range(2):
            inner = jnp.sum(product[head * HD : (head + 1) * HD], 0, keepdims=True)
            q_head = keep_half(query, low_half, head)
            g_head = keep_half(out_grad, low_half, head)
            scores = nt(key, q_head) + bias[0:keys, :]
            weights = jnp.exp(scores - logsum[pair, head : head + 1, q_rows])
            weight_grad = nt(value, g_head)
            score_grad = (weights * (weight_grad - inner)).astype(BF)
            dv_part = nn(weights.astype(BF), g_head)
            dk_part = nn(score_grad, q_head)
            dq_part = nn(score_grad.T, keep_half(key, low_keys, head))
            dv = dv_part if dv is None else dv + dv_part
            dk = dk_part if dk is None else dk + dk_part
            dq = dq_part if dq is None else dq + dq_part
        dqkv[q_rows, lanes] = (dq * (1.0 / math.sqrt(HD))).astype(BF)
        dk_sum[0:keys, lanes] += dk
        dv_sum[0:keys, lanes] += dv

    if causal:
        for i in range(rows // RB):
            keys = (i + 1) * RB
            bias[0:keys, :] = bias_of(i, keys)
            pl.loop(0, pairs)(partial(one, pl.ds(i * RB, RB), keys))
    else:

        @pl.loop(0, rows // RB)
        def _(i):
            bias[...] = bias_of(i, rows)
            pl.loop(0, pairs)(partial(one, block(i), rows))

    @pl.loop(0, rows // RB)
    def _(i):
        dqkv[block(i), cols : 2 * cols] = dk_sum[block(i), :].astype(BF)
        dqkv[block(i), 2 * cols : 3 * cols] = dv_sum[block(i), :].astype(BF)


def self_bias(q_ids, k_ids, i, keys):
    same = q_ids[block(i), :] == k_ids[:, 0:keys]
    if not isinstance(i, int):
        raise ValueError("static block")
    q_pos = i * RB + lax.broadcasted_iota(jnp.int32, (RB, keys), 0)
    k_pos = lax.broadcasted_iota(jnp.int32, (RB, keys), 1)
    allowed = (same & (k_pos < q_pos)) | (k_pos == q_pos)
    return jnp.where(allowed, 0.0, NEG_FILL)


def self_bias_turned(q_ids, k_ids, i, keys):
    same = k_ids[0:keys, :] == q_ids[:, i * RB : (i + 1) * RB]
    q_pos = i * RB + lax.broadcasted_iota(jnp.int32, (keys, RB), 1)
    k_pos = lax.broadcasted_iota(jnp.int32, (keys, RB), 0)
    allowed = (same & (k_pos < q_pos)) | (k_pos == q_pos)
    return jnp.where(allowed, 0.0, NEG_FILL)


def cross_bias(q_ids, k_ids, i, keys):
    return jnp.where(q_ids[block(i), :] == k_ids[:, 0:keys], 0.0, NEG_FILL)


def cross_bias_turned(q_ids, k_ids, i, keys):
    return jnp.where(k_ids[0:keys, :] == q_ids[:, block(i)], 0.0, NEG_FILL)


def self_forward_kernel(
    target, packed, norms, q_ids, k_ids, part, qkv, normed, out, logsum, row, weights, bias, sem
):
    fetch = fetch_row(target, row, sem)
    fetch.start()
    join_groups(packed, weights)
    fetch.wait()
    cols = out.shape[1]

    @pl.loop(0, row.shape[0] // RB)
    def _(i):
        n = norm_forward(row[block(i), :].astype(F32), norms[0:1, :], norms[3:4, :])
        normed[block(i), :] = n
        projected = nn(n, weights[:, 0 : 3 * cols])
        qkv[block(i), 0:cols] = (projected[:, 0:cols].astype(BF).astype(F32) * (1.0 / math.sqrt(HD))).astype(BF)
        qkv[block(i), cols : 3 * cols] = projected[:, cols : 3 * cols].astype(BF)

    attend(qkv, partial(self_bias, q_ids, k_ids), True, out, logsum, bias)

    @pl.loop(0, row.shape[0] // RB)
    def _(i):
        part[block(i), :] = nt(out[block(i), :], weights[:, 3 * cols : 4 * cols]).astype(BF)


def cross_forward_kernel(
    target, own, other, memory, packed, norms, q_ids, k_ids,
    hidden, part, qkv, normed, out, logsum,
    row, mem_row, weights, bias, sem,
):
    fetch, fetch_mem = fetch_row(target, row, sem.at[0]), fetch_row(memory, mem_row, sem.at[1])
    fetch.start()
    fetch_mem.start()
    join_groups(packed, weights)
    fetch.wait()
    fetch_mem.wait()
    cols = out.shape[1]

    @pl.loop(0, row.shape[0] // RB)
    def _(i):
        h = row[block(i), :].astype(F32) + (own[block(i), :].astype(F32) + other[block(i), :].astype(F32))
        hidden[block(i), :] = h
        n = norm_forward(h, norms[1:2, :], norms[4:5, :])
        normed[block(i), :] = n
        q = nn(n, weights[:, 0:cols]).astype(BF).astype(F32) * (1.0 / math.sqrt(HD))
        qkv[block(i), 0:cols] = q.astype(BF)
        qkv[block(i), cols : 3 * cols] = nn(mem_row[block(i), :], weights[:, cols : 3 * cols]).astype(BF)

    attend(qkv, partial(cross_bias, q_ids, k_ids), False, out, logsum, bias)

    @pl.loop(0, row.shape[0] // RB)
    def _(i):
        part[block(i), :] = nt(out[block(i), :], weights[:, 3 * cols : 4 * cols]).astype(BF)


def feed_forward_kernel(
    hidden, own, other, cotangent, up, down, norms,
    hidden_two, part, grad_part, grad_up, grad_down,
    cot, normed, active, pre_grad, turned, sem,
):
    fetch = fetch_row(cotangent, cot, sem)
    fetch.start()
    fetch.wait()

    @pl.loop(0, hidden.shape[0] // RB)
    def _(i):
        h = hidden[block(i), :] + (own[block(i), :].astype(F32) + other[block(i), :].astype(F32))
        hidden_two[block(i), :] = h
        n = norm_forward(h, norms[2:3, :], norms[5:6, :])
        normed[block(i), :] = n
        e = cot[block(i), :]
        total = grad_total = None
        for t in range(2):
            activated, slope = gelu_with_slope(nn(n, up[t]))
            activated = activated.astype(BF)
            du = (nn(e, down[t]) * slope).astype(BF)
            active[t, block(i), :] = activated
            pre_grad[t, block(i), :] = du
            one, two = nt(activated, down[t]), nt(du, up[t])
            total = one if total is None else total + one
            grad_total = two if grad_total is None else grad_total + two
        part[block(i), :] = total.astype(BF)
        grad_part[block(i), :] = grad_total.astype(BF)

    for src, rhs, dst in ((normed, pre_grad, grad_up), (cot, active, grad_down)):
        transpose_into(src, turned)

        @pl.loop(0, turned.shape[0] // RB)
        def _(i):
            for t in range(2):
                dst[t, block(i), :] = nn(turned[block(i), :], rhs[t]).astype(BF)


def back_in(upstream_a, upstream_b, values, gain, residual, sums, rows):
    upstream = upstream_a[rows, :].astype(F32) + upstream_b[rows, :].astype(F32)
    delta, gain_part, shift_part = norm_backward(upstream, values, gain)
    sums[0:1, :] += gain_part
    sums[1:2, :] += shift_part
    return residual + delta


def cross_backward_kernel(
    hidden, own, other, cotangent, attended, qkv, logsum, normed, memory, packed, norms, q_ids, k_ids,
    residual, grads, part, mem_part, norm_sums,
    cot, mem_row, weights, low, grad, dqkv, dk_sum, dv_sum, bias, turned, joined, sem,
):
    fetch, fetch_mem = fetch_row(cotangent, cot, sem.at[0]), fetch_row(memory, mem_row, sem.at[1])
    fetch.start()
    fetch_mem.start()
    join_groups(packed, weights)
    norm_sums[...] = jnp.zeros_like(norm_sums)
    fetch.wait()
    fetch_mem.wait()
    cols = attended.shape[1]
    blocks = hidden.shape[0] // RB

    @pl.loop(0, blocks)
    def _(i):
        e = back_in(
            own, other, hidden[block(i), :], norms[2:3, :], cot[block(i), :].astype(F32), norm_sums, block(i)
        )
        residual[block(i), :] = e
        low[block(i), :] = e.astype(BF)
        grad[block(i), :] = nn(e.astype(BF), weights[:, 3 * cols : 4 * cols]).astype(BF)

    attend_back(
        qkv, attended, grad, logsum, partial(cross_bias_turned, q_ids, k_ids), False, dqkv, dk_sum, dv_sum, bias
    )

    @pl.loop(0, blocks)
    def _(i):
        part[block(i), :] = nt(dqkv[block(i), 0:cols], weights[:, 0:cols]).astype(BF)
        mem_part[block(i), :] = nt(dqkv[block(i), cols : 3 * cols], weights[:, cols : 3 * cols]).astype(BF)

    for src, rhs, first, last in ((normed, dqkv, 0, 1), (mem_row, dqkv, 1, 3), (low, attended, 3, 4)):
        transpose_into(src, turned)
        rhs_cols = slice(0, cols) if rhs is attended else slice(first * cols, last * cols)

        @pl.loop(0, turned.shape[0] // RB)
        def _(i):
            joined[block(i), first * cols : last * cols] = nn(turned[block(i), :], rhs[:, rhs_cols])

    @pl.loop(0, turned.shape[0] // RB)
    def _(i):
        split_groups(joined[block(i), :], grads, block(i))


def self_backward_kernel(
    hidden, own, other, residual, attended, qkv, logsum, normed, packed, norms, q_ids, k_ids,
    residual_out, grads, part, norm_sums,
    weights, low, grad, dqkv, dk_sum, dv_sum, bias, turned, joined,
):
    join_groups(packed, weights)
    norm_sums[...] = jnp.zeros_like(norm_sums)
    cols = attended.shape[1]
    blocks = hidden.shape[0] // RB

    @pl.loop(0, blocks)
    def _(i):
        e = back_in(own, other, hidden[block(i), :], norms[1:2, :], residual[block(i), :], norm_sums, block(i))
        residual_out[block(i), :] = e
        low[block(i), :] = e.astype(BF)
        grad[block(i), :] = nn(e.astype(BF), weights[:, 3 * cols : 4 * cols]).astype(BF)

    attend_back(
        qkv, attended, grad, logsum, partial(self_bias_turned, q_ids, k_ids), True, dqkv, dk_sum, dv_sum, bias
    )

    @pl.loop(0, blocks)
    def _(i):
        part[block(i), :] = nt(dqkv[block(i), :], weights[:, 0 : 3 * cols]).astype(BF)

    for src, rhs, first, last in ((normed, dqkv, 0, 3), (low, attended, 3, 4)):
        transpose_into(src, turned)

        @pl.loop(0, turned.shape[0] // RB)
        def _(i):
            joined[block(i), first * cols : last * cols] = nn(turned[block(i), :], rhs[...])

    @pl.loop(0, turned.shape[0] // RB)
    def _(i):
        split_groups(joined[block(i), :], grads, block(i))


def last_norm_kernel(target, own, other, residual, norms, grad_row, norm_sums, row, sem):
    fetch = fetch_row(target, row, sem)
    fetch.start()
    norm_sums[...] = jnp.zeros_like(norm_sums)
    fetch.wait()

    @pl.loop(0, row.shape[0] // RB)
    def _(i):
        grad_row[block(i), :] = back_in(
            own, other, row[block(i), :].astype(F32), norms[0:1, :], residual[block(i), :], norm_sums, block(i)
        )


def places():
    dp, ta = lax.axis_index("dp"), lax.axis_index("ta")
    return lax.div(dp, 2), lax.rem(dp, 2), ta


class Peers:
    def __init__(self, nz):
        self.nz = nz
        self.z, self.x, self.ta = places()
        self.ox, self.ot = 1 - self.x, 1 - self.ta
        self.x_peer = {"dp": self.z * 2 + self.ox}
        self.y_peer = {"ta": self.ot}
        self.core_peer = {"tb": 1 - lax.axis_index("tb")}

    def up(self, j):
        return lax.rem(self.z + j, self.nz)

    def down(self, j):
        return lax.rem(self.z + (self.nz - j), self.nz)

    def z_peer(self, j):
        return {"dp": self.up(j) * 2 + self.x}

    def greet(self, core=False):
        barrier = pltpu.get_barrier_semaphore()
        others = [self.z_peer(j) for j in range(1, self.nz)] + [self.x_peer, self.y_peer]
        others += [self.core_peer] if core else []
        for other in others:
            pl.semaphore_signal(barrier, inc=1, device_id=other, device_id_type=MESH_ID)
        pl.semaphore_wait(barrier, len(others))


def gather_copies(nz):
    return (nz - 1) + 2 * nz + nz


class Gather:
    def __init__(self, peers, out, send, recv):
        self.p, self.out, self.send, self.recv = peers, out, send, recv
        nz = peers.nz
        self.half = nz // 2
        self.first_x, self.first_y, self.first_d = nz - 1, 2 * nz - 1, 3 * nz - 1

    def copy(self, t, d, index, peer):
        slot = self.out.at[t, d]
        return pltpu.make_async_remote_copy(
            src_ref=slot, dst_ref=slot, send_sem=self.send.at[index], recv_sem=self.recv.at[index],
            device_id=peer, device_id_type=MESH_ID,
        )

    def mine(self, j, turn_x=False, turn_t=False):
        p = self.p
        return (p.ot if turn_t else p.ta), p.down(j) * 2 + (p.ox if turn_x else p.x)

    def start(self):
        p = self.p
        t, d = self.mine(0)
        for j in range(1, p.nz):
            self.copy(t, d, j - 1, p.z_peer(j)).start()
        self.plane(0)

    def plane(self, j):
        t, d = self.mine(j)
        self.copy(t, d, self.first_x + j, self.p.x_peer).start()
        self.copy(t, d, self.first_y + j, self.p.y_peer).start()

    def after_z(self, j):
        t, d = self.mine(j)
        self.copy(t, d, j - 1, self.p.x_peer).wait_recv()
        self.plane(j)

    def after_plane(self, j):
        t, d = self.mine(j, turn_x=True)
        self.copy(t, d, self.first_x + j, self.p.x_peer).wait_recv()
        if j < self.half:
            self.copy(t, d, self.first_d + j, self.p.y_peer).start()
        t, d = self.mine(j, turn_t=True)
        self.copy(t, d, self.first_y + j, self.p.y_peer).wait_recv()
        if j >= self.half:
            self.copy(t, d, self.first_d + j, self.p.x_peer).start()

    def finish(self):
        p = self.p
        for j in range(p.nz):
            t, d = self.mine(j, turn_x=True, turn_t=True)
            self.copy(t, d, self.first_d + j, p.x_peer).wait_recv()
        for index in range(gather_copies(p.nz)):
            t, d = self.mine(0)
            self.copy(t, d, index, p.x_peer).wait_send()


def gather_kernel(nz, count, *refs):
    shards, outs, sems = refs[:count], refs[count : 2 * count], refs[2 * count :]
    peers = Peers(nz)
    peers.greet()
    works = []
    for k in range(count):
        out = outs[k]
        out[peers.ta, peers.z * 2 + peers.x] = shards[k][...]
        works.append(Gather(peers, out, sems[0].at[k], sems[1].at[k]))
        works[k].start()
    for k in range(count):
        for j in range(1, nz):
            works[k].after_z(j)
    for k in range(count):
        for j in range(nz):
            works[k].after_plane(j)
    for k in range(count):
        works[k].finish()


def gather_all(shards, dp_size):
    nz = dp_size // 2
    count = len(shards)
    copies = gather_copies(nz)
    return pl.pallas_call(
        partial(gather_kernel, nz, count),
        name="gather_weights",
        out_shape=[sds((2, dp_size) + s.shape, s.dtype) for s in shards],
        in_specs=vm(count),
        out_specs=vm(count),
        scratch_shapes=[pltpu.SemaphoreType.DMA((count, copies)), pltpu.SemaphoreType.DMA((count, copies))],
        compiler_params=params(collective_id=0, has_side_effects=True),
    )(*shards)


class Reduce:
    def __init__(self, peers, part, landing, relay, send, recv):
        self.p, self.part, self.landing, self.relay, self.send, self.recv = peers, part, landing, relay, send, recv
        nz = peers.nz
        self.half = nz // 2
        self.first_x, self.first_y, self.first_z = nz, 2 * nz, 3 * nz

    def slot(self, j, turn_x=False, turn_t=False):
        p = self.p
        return self.part.at[(p.ot if turn_t else p.ta), p.up(j) * 2 + (p.ox if turn_x else p.x)]

    def copy(self, src, index, peer):
        return pltpu.make_async_remote_copy(
            src_ref=src, dst_ref=self.landing.at[index], send_sem=self.send.at[index], recv_sem=self.recv.at[index],
            device_id=peer, device_id_type=MESH_ID,
        )

    def arrived(self, index):
        self.copy(self.slot(0), index, self.p.x_peer).wait_recv()
        return self.landing[index].astype(F32)

    def start(self):
        p = self.p
        for j in range(p.nz):
            diagonal = self.slot(j, turn_x=True, turn_t=True)
            self.copy(diagonal, j, p.x_peer if j < self.half else p.y_peer).start()
        for j in range(p.nz):
            if j < self.half:
                self.copy(self.slot(j, turn_x=True), self.first_x + j, p.x_peer).start()
            else:
                self.copy(self.slot(j, turn_t=True), self.first_y + j, p.y_peer).start()

    def pass_on(self, j):
        p = self.p
        kwargs = {"turn_t": True} if j < self.half else {"turn_x": True}
        slot = self.relay.at[j]
        slot[...] = (self.slot(j, **kwargs)[...].astype(F32) + self.arrived(j)).astype(slot.dtype)
        if j < self.half:
            self.copy(slot, self.first_y + j, p.y_peer).start()
        else:
            self.copy(slot, self.first_x + j, p.x_peer).start()

    def along_z(self, j):
        total = self.slot(j)[...].astype(F32) + self.arrived(self.first_x + j) + self.arrived(self.first_y + j)
        if j == 0:
            return total
        slot = self.relay.at[self.p.nz + j - 1]
        slot[...] = total.astype(slot.dtype)
        self.copy(slot, self.first_z + j - 1, self.p.z_peer(j)).start()
        return None

    def finish(self, total):
        for j in range(1, self.p.nz):
            total = total + self.arrived(self.first_z + j - 1)
        for index in range(gather_copies(self.p.nz)):
            self.copy(self.slot(0), index, self.p.x_peer).wait_send()
        return total


def reduce_kernel(nz, count, tensor_size, norm_index, *refs):
    parts, outs, norm_out = refs[:count], refs[count : 2 * count], refs[2 * count]
    rest = refs[2 * count + 1 :]
    landings, relays = rest[:count], rest[count : 2 * count]
    stage, heard, send, recv, sends, recvs = rest[2 * count :]
    peers = Peers(nz)
    peers.greet(core=True)
    works = [Reduce(peers, parts[k], landings[k], relays[k], send.at[k], recv.at[k]) for k in range(count)]
    for w in works:
        w.start()
    for w in works:
        for j in range(nz):
            w.pass_on(j)
    for w in works:
        for j in range(1, nz):
            w.along_z(j)
    squares = jnp.zeros((1, 1), F32)
    for k, w in enumerate(works):
        total = w.finish(w.along_z(0))
        outs[k][...] = total
        share = jnp.sum(jnp.sum(total * total, -1, keepdims=True), 0, keepdims=True)
        squares = squares + (share / tensor_size if k == norm_index else share)

    def swap(step, peer, value):
        stage[step] = value
        copy = pltpu.make_async_remote_copy(
            src_ref=stage.at[step], dst_ref=heard.at[step], send_sem=sends.at[step], recv_sem=recvs.at[step],
            device_id=peer, device_id_type=MESH_ID,
        )
        copy.start()
        copy.wait()
        return value + heard[step]

    value = jnp.broadcast_to(squares, (8, 128))
    for step, peer in enumerate((peers.core_peer, peers.x_peer, peers.y_peer)):
        value = swap(step, peer, value)
    heard[3 + peers.z] = value
    copies = []
    for j in range(1, nz):
        copies.append(
            pltpu.make_async_remote_copy(
                src_ref=heard.at[3 + peers.z], dst_ref=heard.at[3 + peers.z], send_sem=sends.at[2 + j],
                recv_sem=recvs.at[2 + j], device_id=peers.z_peer(j), device_id_type=MESH_ID,
            )
        )
        copies[-1].start()
    for j in range(1, nz):
        pltpu.make_async_remote_copy(
            src_ref=heard.at[3 + peers.z], dst_ref=heard.at[3 + peers.down(j)], send_sem=sends.at[2 + j],
            recv_sem=recvs.at[2 + j], device_id=peers.z_peer(j), device_id_type=MESH_ID,
        ).wait_recv()
    for copy in copies:
        copy.wait_send()
    total = heard[3]
    for k in range(1, nz):
        total = total + heard[3 + k]
    norm_out[...] = total


def reduce_all(parts, dp_size, tensor_size, norm_index):
    nz = dp_size // 2
    count = len(parts)
    copies = gather_copies(nz)
    shard = [p.shape[2:] for p in parts]
    return pl.pallas_call(
        partial(reduce_kernel, nz, count, tensor_size, norm_index),
        name="reduce_gradients",
        out_shape=[sds(s, F32) for s in shard] + [sds((8, 128), F32)],
        in_specs=vm(count),
        out_specs=vm(count + 1),
        scratch_shapes=[pltpu.VMEM((copies,) + s, BF) for s in shard]
        + [pltpu.VMEM((2 * nz - 1,) + s, BF) for s in shard]
        + [
            pltpu.VMEM((3, 8, 128), F32),
            pltpu.VMEM((3 + nz, 8, 128), F32),
            pltpu.SemaphoreType.DMA((count, copies)),
            pltpu.SemaphoreType.DMA((count, copies)),
            pltpu.SemaphoreType.DMA((2 + nz,)),
            pltpu.SemaphoreType.DMA((2 + nz,)),
        ],
        compiler_params=params(collective_id=1, has_side_effects=True),
    )(*parts)


def adam_update(weight, gradient, first, second, clip_factor, bias_one, bias_two, rate, decay):
    scaled = gradient * clip_factor
    first_new = BETA_ONE * first + (1.0 - BETA_ONE) * scaled
    second_new = BETA_TWO * second + (1.0 - BETA_TWO) * scaled * scaled
    first_hat = first_new / bias_one
    second_hat = second_new / bias_two
    weight_new = weight - rate * (first_hat / (jnp.sqrt(second_hat) + EPS_ADAM) + decay * weight)
    return weight_new, weight_new.astype(BF), first_new, second_new


RATES = (
    (RATE_MATRIX, DECAY_RATE),
    (RATE_OUTPUT, DECAY_RATE),
    (RATE_MATRIX, DECAY_RATE),
    (RATE_OUTPUT, DECAY_RATE),
    (RATE_MATRIX, DECAY_RATE),
    (RATE_MATRIX, DECAY_RATE),
    (RATE_NORMS, 0.0),
)


def shard_gradients(reduced, width):
    g_self, g_cross, g_up, g_down, g_norms = reduced
    cut = [
        [g[:, s * width : (s + 1) * width] for s in range(4)] for g in (g_self, g_cross)
    ]
    return (cut[0][:3], cut[0][3].T, cut[1][:3], cut[1][3].T, g_up, g_down.T, g_norms)


def adam_kernel(*refs):
    reduced, squares, biases = refs[:5], refs[5], refs[6]
    state, norm_out, outs = refs[7:28], refs[28], refs[29:]
    width = state[3].shape[0]
    norm = jnp.sqrt(squares[...])
    norm_out[...] = norm
    clip = (CLIP_LIMIT / jnp.maximum(norm, CLIP_LIMIT))[0:1, 0:1]
    values = [r[...] for r in reduced]
    shape = state[18].shape
    values[4] = values[4][0 : shape[0], 0 : shape[1]]
    gradients = shard_gradients(values, width)
    for k, (rate, decay) in enumerate(RATES):
        weight, first, second = state[3 * k : 3 * k + 3]
        into = outs[4 * k : 4 * k + 4]
        if isinstance(gradients[k], list):
            for s in range(3):
                new = adam_update(
                    weight[s], gradients[k][s], first[s], second[s], clip, biases[0], biases[1], rate, decay
                )
                for ref, value in zip(into, new):
                    ref[s] = value
        else:
            new = adam_update(
                weight[...], gradients[k], first[...], second[...], clip, biases[0], biases[1], rate, decay
            )
            for ref, value in zip(into, new):
                ref[...] = value


def swap_core(value):
    return lax.ppermute(value, "tb", [(0, 1), (1, 0)])


def both_rows(row, ta, tb):
    half = row.shape[0] // 2
    mine = lax.dynamic_slice_in_dim(row, tb * half, half).astype(BF)
    got = lax.ppermute(mine, "ta", [(0, 1), (1, 0)])
    rest = swap_core(got)
    other = jnp.where(tb == 0, jnp.concatenate([got, rest]), jnp.concatenate([rest, got])).astype(F32)
    return jnp.where(ta == 0, jnp.concatenate([row, other]), jnp.concatenate([other, row]))


def body(target, memory, cotangent, tgt_seg, mem_seg, pad_len, step_count, *state):
    dp_size, tensor_size = lax.axis_size("dp"), lax.axis_size("ta") * lax.axis_size("tb")
    ta, tb = lax.axis_index("ta"), lax.axis_index("tb")
    self_in, self_out, cross_in, cross_out, ffn_in, ffn_out, norm_params = state[::3]
    length, depth = tgt_seg.shape[1], target.shape[1]
    mem_length = mem_seg.shape[1]
    width, span = self_out.shape
    cols = 2 * width
    own_transfers = span % 16 == 0

    def pack(w_in, w_out):
        return jnp.concatenate([w_in[0], w_in[1], w_in[2], w_out.T], axis=1).astype(BF)

    norm_shard = jnp.zeros((16, 128), BF).at[: norm_params.shape[0], :span].set(norm_params.astype(BF))
    shards = [pack(self_in, self_out), pack(cross_in, cross_out), ffn_in.astype(BF), ffn_out.T.astype(BF), norm_shard]
    if own_transfers:
        gathered = gather_all(shards, dp_size)
    else:
        gathered = [lax.all_gather(lax.all_gather(s, "dp", axis=0), "ta", axis=0) for s in shards]
    w_self, w_cross, w_up, w_down = [g.reshape(2, depth, g.shape[3]) for g in gathered[:4]]
    norms = gathered[4][0][:, :, :span].transpose(1, 0, 2).reshape(16, depth).astype(F32)

    tgt_ids = lax.dynamic_slice_in_dim(tgt_seg, ta, 1)
    mem_ids = lax.dynamic_slice_in_dim(mem_seg, ta, 1)
    pad = lax.dynamic_slice_in_dim(pad_len, ta, 1)
    key_ids = jnp.where(jnp.arange(length)[None, :] < length - pad[:, None], tgt_ids, -1)
    tgt_col, mem_col, key_col = tgt_ids.reshape(length, 1), mem_ids.reshape(mem_length, 1), key_ids.reshape(length, 1)

    row_bf, row_f32 = sds((length, depth), BF), sds((length, depth), F32)
    mem_bf = sds((mem_length, depth), BF)
    qkv_bf, att_bf = sds((length, 3 * cols), BF), sds((length, cols), BF)
    logsum = sds((cols // 128, 2, length), F32)
    grads = sds((2, depth, 4 * width), BF)
    sums = sds((8, depth), F32)
    v_row, v_att = pltpu.VMEM((length, depth), BF), pltpu.VMEM((length, cols), BF)
    v_mem = pltpu.VMEM((mem_length, depth), BF)
    v_joined = pltpu.VMEM((depth, 4 * cols), BF)
    v_sum = pltpu.VMEM((mem_length, cols), F32)

    def flops(macs, nbytes):
        return pl.CostEstimate(flops=2 * macs, bytes_accessed=nbytes, transcendentals=0)

    dense = length * depth

    def call(kernel, name, ins, outs, scratch, macs):
        arrays = [a for a, _ in ins]
        return pl.pallas_call(
            kernel,
            name=name,
            out_shape=outs,
            in_specs=[vm()[0] if spec else anym()[0] for _, spec in ins],
            out_specs=vm(len(outs)),
            scratch_shapes=scratch,
            compiler_params=params(),
            cost_estimate=flops(macs, 20 << 20),
        )(*arrays)

    part_one, qkv_one, normed_one, att_one, lse_one = call(
        self_forward_kernel,
        "self_forward",
        [(target, 0), (w_self, 1), (norms, 1), (tgt_col, 1), (key_ids, 1)],
        [row_bf, qkv_bf, row_bf, att_bf, logsum],
        [v_row, v_joined, pltpu.VMEM((RB, length), F32), pltpu.SemaphoreType.DMA],
        dense * 4 * cols * 2,
    )
    hidden_one, part_two, qkv_two, normed_two, att_two, lse_two = call(
        cross_forward_kernel,
        "cross_forward",
        [(target, 0), (part_one, 1), (swap_core(part_one), 1), (memory, 0), (w_cross, 1), (norms, 1)]
        + [(tgt_col, 1), (mem_ids, 1)],
        [row_f32, row_bf, qkv_bf, row_bf, att_bf, logsum],
        [v_row, v_mem, v_joined, pltpu.VMEM((RB, mem_length), F32), pltpu.SemaphoreType.DMA((2,))],
        dense * 4 * cols * 2,
    )
    hidden = w_up.shape[2]
    v_hidden = pltpu.VMEM((2, length, hidden), BF)
    hidden_two, part_three, grad_three, g_up, g_down = call(
        feed_forward_kernel,
        "feed_forward",
        [(hidden_one, 1), (part_two, 1), (swap_core(part_two), 1), (cotangent, 0), (w_up, 1), (w_down, 1), (norms, 1)],
        [row_f32, row_bf, row_bf, sds((2, depth, hidden), BF), sds((2, depth, hidden), BF)],
        [v_row, v_row, v_hidden, v_hidden, pltpu.VMEM((depth, length), BF), pltpu.SemaphoreType.DMA],
        dense * hidden * 12,
    )
    block_out = hidden_two + (part_three.astype(F32) + swap_core(part_three).astype(F32))
    residual_two, g_cross, grad_two, mem_part, sums_three = call(
        cross_backward_kernel,
        "cross_backward",
        [(hidden_two, 1), (grad_three, 1), (swap_core(grad_three), 1), (cotangent, 0), (att_two, 1), (qkv_two, 1)]
        + [(lse_two, 1), (normed_two, 1), (memory, 0), (w_cross, 1), (norms, 1), (tgt_ids, 1), (mem_col, 1)],
        [row_f32, grads, row_bf, mem_bf, sums],
        [v_row, v_mem, v_joined, v_row, v_att, pltpu.VMEM((length, 3 * cols), BF), v_sum, v_sum]
        + [pltpu.VMEM((mem_length, RB), F32), pltpu.VMEM((depth, length), BF), pltpu.VMEM((depth, 4 * cols), F32)]
        + [pltpu.SemaphoreType.DMA((2,))],
        dense * 4 * cols * 4,
    )
    grad_memory = mem_part.astype(F32) + swap_core(mem_part).astype(F32)
    residual_one, g_self, grad_one, sums_two = call(
        self_backward_kernel,
        "self_backward",
        [(hidden_one, 1), (grad_two, 1), (swap_core(grad_two), 1), (residual_two, 1), (att_one, 1), (qkv_one, 1)]
        + [(lse_one, 1), (normed_one, 1), (w_self, 1), (norms, 1), (tgt_ids, 1), (key_col, 1)],
        [row_f32, grads, row_bf, sums],
        [v_joined, v_row, v_att, pltpu.VMEM((length, 3 * cols), BF), v_sum, v_sum]
        + [pltpu.VMEM((length, RB), F32), pltpu.VMEM((depth, length), BF), pltpu.VMEM((depth, 4 * cols), F32)],
        dense * 4 * cols * 4,
    )
    grad_target, sums_one = call(
        last_norm_kernel,
        "last_norm",
        [(target, 0), (grad_one, 1), (swap_core(grad_one), 1), (residual_one, 1), (norms, 1)],
        [row_f32, sums],
        [v_row, pltpu.SemaphoreType.DMA],
        dense,
    )

    all_sums = jnp.stack([sums_one[0], sums_two[0], sums_three[0], sums_one[1], sums_two[1], sums_three[1]])
    norm_parts = all_sums.reshape(6, dp_size, span).transpose(1, 0, 2)
    norm_parts = jnp.zeros((dp_size, 16, 128), BF).at[:, :6, :span].set(norm_parts.astype(BF))
    norm_parts = jnp.broadcast_to(norm_parts[None], (2,) + norm_parts.shape)
    parts = [g.reshape(2, dp_size, span, g.shape[2]) for g in (g_self, g_cross, g_up, g_down)] + [norm_parts]
    step_float = step_count.astype(F32)
    biases = jnp.stack([1.0 - jnp.power(BETA_ONE, step_float), 1.0 - jnp.power(BETA_TWO, step_float)])
    if own_transfers:
        *reduced, squares = reduce_all(parts, dp_size, tensor_size, 4)
        updated = pl.pallas_call(
            adam_kernel,
            name="adam",
            out_shape=[sds((8, 128), F32)]
            + [sds(w.shape, dt) for w in state[::3] for dt in (F32, BF, F32, F32)],
            in_specs=vm(6) + [pl.BlockSpec(memory_space=pltpu.SMEM)] + vm(21),
            out_specs=vm(29),
            compiler_params=params(),
        )(*reduced, squares, biases, *state)
        global_norm, updated = updated[0][0, 0], updated[1:]
    else:
        reduced = [
            lax.psum_scatter(lax.psum_scatter(p.astype(F32), "ta", scatter_dimension=0), "dp", scatter_dimension=0)
            for p in parts
        ]
        reduced[4] = reduced[4][:6, :span]
        total = sum(jnp.sum(r * r) for r in reduced[:4]) + jnp.sum(reduced[4] * reduced[4]) / tensor_size
        global_norm = jnp.sqrt(lax.psum(total, ("dp", "ta", "tb")))
        clip = CLIP_LIMIT / jnp.maximum(global_norm, CLIP_LIMIT)
        updated = []
        for k, g in enumerate(shard_gradients(reduced, width)):
            g = jnp.stack(g) if isinstance(g, list) else g
            weight, first, second = state[3 * k : 3 * k + 3]
            updated += adam_update(weight, g, first, second, clip, biases[0], biases[1], *RATES[k])
    return (
        global_norm,
        both_rows(block_out, ta, tb),
        both_rows(grad_target, ta, tb),
        both_rows(grad_memory, ta, tb),
        *updated,
    )


def solution(mesh):
    dp_size, tensor_size = mesh.shape["dp"], mesh.shape["tensor"]
    grid = Mesh(mesh.devices.reshape(dp_size, 2, tensor_size // 2), ("dp", "ta", "tb"))
    tensor = ("ta", "tb")
    rows = P("dp", None)
    place = (
        P(None, "dp", tensor),
        P(tensor, "dp"),
        P(None, "dp", tensor),
        P(tensor, "dp"),
        P("dp", tensor),
        P(tensor, "dp"),
        P(None, "dp"),
    )
    return jax.shard_map(
        body,
        mesh=grid,
        in_specs=(rows,) * 5 + (P("dp"), P()) + tuple(p for p in place for _ in range(3)),
        out_specs=(P(), rows, rows, rows) + tuple(p for p in place for _ in range(4)),
        check_vma=False,
    )
```

```python
from functools import partial
import math
from types import SimpleNamespace

import jax
import jax.numpy as jnp
from jax import lax
from jax.experimental import pallas as pl
from jax.experimental.pallas import tpu as pltpu
from jax.sharding import Mesh, PartitionSpec as P

HD = 64
EPS_NORM = 1e-05
NEG_FILL = -1000000000.0
BETA_ONE = 0.9
BETA_TWO = 0.999
EPS_ADAM = 1e-08
RATE_MATRIX = 0.05
RATE_OUTPUT = 0.25
RATE_NORMS = 0.75
DECAY_RATE = 0.1
CLIP_LIMIT = 1.0
GELU_COEF = 0.044715

BF = jnp.bfloat16
F32 = jnp.float32
RB = 256
PW = 768
MESH_ID = pl.DeviceIdType.MESH
VMEM_LIMIT = 63 * 1024 * 1024


def nn(a, b):
    return lax.dot_general(a, b, (((1,), (0,)), ((), ())), preferred_element_type=F32)


def nt(a, b):
    return lax.dot_general(a, b, (((1,), (1,)), ((), ())), preferred_element_type=F32)


def vm(n=1):
    return [pl.BlockSpec(memory_space=pltpu.VMEM)] * n


def anym(n=1):
    return [pl.BlockSpec(memory_space=pl.ANY)] * n


def sds(shape, dtype):
    return jax.ShapeDtypeStruct(shape, dtype)


def params(**kw):
    return pltpu.CompilerParams(vmem_limit_bytes=VMEM_LIMIT, **kw)


def block(i, size=RB):
    return pl.ds(pl.multiple_of(i * size, size), size)


def gelu_with_slope(values):
    root = math.sqrt(2.0 / math.pi)
    square = values * values
    tangent = jnp.tanh(values * (root + (root * GELU_COEF) * square))
    half = 0.5 + 0.5 * tangent
    output = values * half
    slope = half + 0.5 * output * (1.0 - tangent) * (2.0 * root + (6.0 * root * GELU_COEF) * square)
    return output, slope


def norm_stats(values):
    centre = values - jnp.mean(values, -1, keepdims=True)
    inverse = lax.rsqrt(jnp.mean(centre * centre, -1, keepdims=True) + EPS_NORM)
    return centre * inverse, inverse


def norm_forward(values, gain, shift):
    scaled, _ = norm_stats(values)
    return (scaled * gain + shift).astype(BF)


def norm_backward(upstream, values, gain):
    scaled, inverse = norm_stats(values)
    weighted = upstream * gain
    product = upstream * scaled
    result = inverse * (
        weighted
        - jnp.mean(weighted, -1, keepdims=True)
        - scaled * jnp.mean(weighted * scaled, -1, keepdims=True)
    )
    return result, jnp.sum(product, 0, keepdims=True), jnp.sum(upstream, 0, keepdims=True)


def launch(kernel, name, ins, outs, scratch, macs=0, **compiler):
    names = list(ins) + list(outs) + list(scratch)

    def run(*refs):
        kernel(SimpleNamespace(**dict(zip(names, refs))))

    results = pl.pallas_call(
        run,
        name=name,
        out_shape=[sds(shape, dtype) for shape, dtype, _ in outs.values()],
        in_specs=[(vm() if inside else anym())[0] for _, inside in ins.values()],
        out_specs=[(vm() if inside else anym())[0] for _, _, inside in outs.values()],
        scratch_shapes=list(scratch.values()),
        compiler_params=params(**compiler),
        cost_estimate=pl.CostEstimate(flops=2 * macs, bytes_accessed=20 << 20, transcendentals=0),
    )(*[a for a, _ in ins.values()])
    return SimpleNamespace(**dict(zip(outs, results)))


class Local:
    def __init__(self, sems):
        self.sems, self.count, self.open = sems, 0, {}

    def start(self, name, src, dst):
        copy = pltpu.make_async_copy(src, dst, self.sems.at[self.count])
        self.count += 1
        copy.start()
        self.open[name] = copy

    def row(self, name, src, dst):
        rows = dst.shape[0]
        start = pl.multiple_of(lax.axis_index("ta") * rows, rows)
        self.start(name, src.at[pl.ds(start, rows)], dst)

    def wait(self, *names):
        for name in names:
            self.open.pop(name).wait()

    def drain(self):
        self.wait(*list(self.open))


class Steps:
    def __init__(self):
        self.todo = []

    def add(self, name, fn, *args, **kwargs):
        self.todo.append((name, partial(fn, *args, **kwargs)))

    def step(self, count=1):
        for _ in range(min(count, len(self.todo))):
            self.todo.pop(0)[1]()

    def until(self, name):
        while any(n == name for n, _ in self.todo):
            self.step()

    def drain(self):
        self.step(len(self.todo))


def join_groups(packed, joined):
    rows, width = packed.shape[2], packed.shape[3] // 4

    @pl.loop(0, packed.shape[1])
    def _(i):
        first, second = packed[0, i], packed[1, i]
        pieces = []
        for s in range(4):
            pieces += [first[:, s * width : (s + 1) * width], second[:, s * width : (s + 1) * width]]
        joined[block(i, rows), :] = jnp.concatenate(pieces, axis=1)


def gradient(turned, rhs, store):
    rows = turned.shape[0] // 4

    @pl.loop(0, 4)
    def _(i):
        product = nn(turned[block(i, rows), :], rhs())
        half = rows // 2
        for part in range(2):
            store(2 * i + part, product[part * half : (part + 1) * half])


def transpose_into(src, dst):
    @pl.loop(0, src.shape[0] // RB)
    def _(i):
        dst[:, block(i)] = src[block(i), :].T


def head_masks(rows):
    lane = lax.broadcasted_iota(jnp.int32, (rows, 2 * HD), 1)
    return lane < HD


def keep_half(values, low_half, head):
    zero = jnp.zeros_like(values)
    return jnp.where(low_half, values, zero) if head == 0 else jnp.where(low_half, zero, values)


def attend(qkv, bias_of, causal, out, logsum, bias, after):
    rows, cols = out.shape
    pairs = cols // (2 * HD)

    def one(q_rows, keys, pair):
        lanes = block(pair, 2 * HD)
        k_lanes = pl.ds(pl.multiple_of(cols + pair * 2 * HD, 2 * HD), 2 * HD)
        v_lanes = pl.ds(pl.multiple_of(2 * cols + pair * 2 * HD, 2 * HD), 2 * HD)
        query, key, value = qkv[q_rows, lanes], qkv[0:keys, k_lanes], qkv[0:keys, v_lanes]
        low_half = head_masks(RB)
        outs, sums = [], []
        for head in range(2):
            scores = nt(keep_half(query, low_half, head), key) + bias[:, 0:keys]
            peak = jnp.max(scores, -1, keepdims=True)
            shifted = jnp.exp(scores - peak)
            total = jnp.sum(shifted, -1, keepdims=True)
            outs.append(nn(shifted.astype(BF), value) / total)
            sums.append(peak + jnp.log(total))
        out[q_rows, lanes] = jnp.where(low_half, outs[0], outs[1]).astype(BF)
        both = jnp.where(low_half, sums[0], sums[1]).T
        logsum[pair, :, q_rows] = jnp.concatenate([both[0:1], both[HD : HD + 1]], axis=0)

    for i in range(rows // RB):
        keys = (i + 1) * RB if causal else bias.shape[1]
        bias[:, 0:keys] = bias_of(i, keys)
        pl.loop(0, pairs)(partial(one, pl.ds(i * RB, RB), keys))
        after(i)


def attend_back(qkv, attended, grad, logsum, bias_of, causal, dqkv, dk_sum, dv_sum, bias, after):
    rows, cols = attended.shape
    pairs = cols // (2 * HD)
    dk_sum[...] = jnp.zeros_like(dk_sum)
    dv_sum[...] = jnp.zeros_like(dv_sum)

    def one(q_rows, keys, pair):
        lanes = block(pair, 2 * HD)
        k_lanes = pl.ds(pl.multiple_of(cols + pair * 2 * HD, 2 * HD), 2 * HD)
        v_lanes = pl.ds(pl.multiple_of(2 * cols + pair * 2 * HD, 2 * HD), 2 * HD)
        query, key, value = qkv[q_rows, lanes], qkv[0:keys, k_lanes], qkv[0:keys, v_lanes]
        out_grad = grad[q_rows, lanes]
        low_half = head_masks(RB)
        low_keys = head_masks(keys)
        product = (out_grad.astype(F32) * attended[q_rows, lanes].astype(F32)).T
        dq = dk = dv = None
        for head in range(2):
            inner = jnp.sum(product[head * HD : (head + 1) * HD], 0, keepdims=True)
            q_head = keep_half(query, low_half, head)
            g_head = keep_half(out_grad, low_half, head)
            scores = nt(key, q_head) + bias[0:keys, :]
            weights = jnp.exp(scores - logsum[pair, head : head + 1, q_rows])
            weight_grad = nt(value, g_head)
            score_grad = (weights * (weight_grad - inner)).astype(BF)
            dv_part = nn(weights.astype(BF), g_head)
            dk_part = nn(score_grad, q_head)
            dq_part = nn(score_grad.T, keep_half(key, low_keys, head))
            dv = dv_part if dv is None else dv + dv_part
            dk = dk_part if dk is None else dk + dk_part
            dq = dq_part if dq is None else dq + dq_part
        dqkv[q_rows, lanes] = (dq * (1.0 / math.sqrt(HD))).astype(BF)
        dk_sum[0:keys, lanes] += dk
        dv_sum[0:keys, lanes] += dv

    def settle(key_rows):
        dqkv[key_rows, cols : 2 * cols] = dk_sum[key_rows, :].astype(BF)
        dqkv[key_rows, 2 * cols : 3 * cols] = dv_sum[key_rows, :].astype(BF)

    for i in reversed(range(rows // RB)):
        keys = (i + 1) * RB if causal else bias.shape[0]
        bias[0:keys, :] = bias_of(i, keys)
        pl.loop(0, pairs)(partial(one, pl.ds(i * RB, RB), keys))
        if causal:
            settle(pl.ds(i * RB, RB))
        after(i)
    if not causal:
        pl.loop(0, dk_sum.shape[0] // RB)(lambda i: settle(block(i)))


def self_bias(q_ids, k_ids, i, keys):
    same = q_ids[block(i), :] == k_ids[:, 0:keys]
    if not isinstance(i, int):
        raise ValueError("static block")
    q_pos = i * RB + lax.broadcasted_iota(jnp.int32, (RB, keys), 0)
    k_pos = lax.broadcasted_iota(jnp.int32, (RB, keys), 1)
    allowed = (same & (k_pos < q_pos)) | (k_pos == q_pos)
    return jnp.where(allowed, 0.0, NEG_FILL)


def self_bias_turned(q_ids, k_ids, i, keys):
    same = k_ids[0:keys, :] == q_ids[:, i * RB : (i + 1) * RB]
    q_pos = i * RB + lax.broadcasted_iota(jnp.int32, (keys, RB), 1)
    k_pos = lax.broadcasted_iota(jnp.int32, (keys, RB), 0)
    allowed = (same & (k_pos < q_pos)) | (k_pos == q_pos)
    return jnp.where(allowed, 0.0, NEG_FILL)


def cross_bias(q_ids, k_ids, i, keys):
    return jnp.where(q_ids[block(i), :] == k_ids[:, 0:keys], 0.0, NEG_FILL)


def cross_bias_turned(q_ids, k_ids, i, keys):
    return jnp.where(k_ids[0:keys, :] == q_ids[:, block(i)], 0.0, NEG_FILL)


def places():
    dp, ta = lax.axis_index("dp"), lax.axis_index("ta")
    return lax.div(dp, 2), lax.rem(dp, 2), ta


class Peers:
    def __init__(self, nz):
        self.nz = nz
        self.z, self.x, self.ta = places()
        self.ox, self.ot = 1 - self.x, 1 - self.ta
        self.x_peer = {"dp": self.z * 2 + self.ox}
        self.y_peer = {"ta": self.ot}
        self.core_peer = {"tb": 1 - lax.axis_index("tb")}

    def up(self, j):
        return lax.rem(self.z + j, self.nz)

    def down(self, j):
        return lax.rem(self.z + (self.nz - j), self.nz)

    def z_peer(self, j):
        return {"dp": self.up(j) * 2 + self.x}

    def greet(self, core=False, plane=True):
        barrier = pltpu.get_barrier_semaphore()
        others = [self.z_peer(j) for j in range(1, self.nz)] + [self.x_peer] if plane else []
        others += [self.y_peer] + ([self.core_peer] if core else [])
        for other in others:
            pl.semaphore_signal(barrier, inc=1, device_id=other, device_id_type=MESH_ID)
        pl.semaphore_wait(barrier, len(others))


def gather_copies(nz):
    return (nz - 1) + 2 * nz + nz


class Gather:
    def __init__(self, peers, out, send, recv, own=None):
        self.p, self.out, self.send, self.recv, self.own = peers, out, send, recv, own
        nz = peers.nz
        self.half = nz // 2
        self.first_x, self.first_y, self.first_d = nz - 1, 2 * nz - 1, 3 * nz - 1

    def copy(self, t, d, index, peer, own=False):
        slot = self.out.at[t, d]
        return pltpu.make_async_remote_copy(
            src_ref=self.own if own and self.own is not None else slot, dst_ref=slot, send_sem=self.send.at[index], recv_sem=self.recv.at[index],
            device_id=peer, device_id_type=MESH_ID,
        )

    def mine(self, j, turn_x=False, turn_t=False):
        p = self.p
        return (p.ot if turn_t else p.ta), p.down(j) * 2 + (p.ox if turn_x else p.x)

    def start(self):
        p = self.p
        t, d = self.mine(0)
        for j in range(1, p.nz):
            self.copy(t, d, j - 1, p.z_peer(j), own=True).start()
        self.plane(0)

    def plane(self, j):
        t, d = self.mine(j)
        self.copy(t, d, self.first_x + j, self.p.x_peer, own=j == 0).start()
        self.copy(t, d, self.first_y + j, self.p.y_peer, own=j == 0).start()

    def after_z(self, j):
        t, d = self.mine(j)
        self.copy(t, d, j - 1, self.p.x_peer).wait_recv()
        self.plane(j)

    def after_plane(self, j):
        t, d = self.mine(j, turn_x=True)
        self.copy(t, d, self.first_x + j, self.p.x_peer).wait_recv()
        if j < self.half:
            self.copy(t, d, self.first_d + j, self.p.y_peer).start()
        t, d = self.mine(j, turn_t=True)
        self.copy(t, d, self.first_y + j, self.p.y_peer).wait_recv()
        if j >= self.half:
            self.copy(t, d, self.first_d + j, self.p.x_peer).start()

    def finish(self):
        p = self.p
        for j in range(p.nz):
            t, d = self.mine(j, turn_x=True, turn_t=True)
            self.copy(t, d, self.first_d + j, p.x_peer).wait_recv()
        for index in range(gather_copies(p.nz)):
            t, d = self.mine(0)
            self.copy(t, d, index, p.x_peer).wait_send()


class Reduce:
    def __init__(self, peers, part, landing, relay, send, recv):
        self.p, self.part, self.landing, self.relay, self.send, self.recv = peers, part, landing, relay, send, recv
        nz = peers.nz
        self.half = nz // 2
        self.first_x, self.first_y, self.first_z = nz, 2 * nz, 3 * nz

    def slot(self, j, turn_x=False, turn_t=False):
        p = self.p
        return self.part.at[(p.ot if turn_t else p.ta), p.up(j) * 2 + (p.ox if turn_x else p.x)]

    def copy(self, src, index, peer):
        return pltpu.make_async_remote_copy(
            src_ref=src, dst_ref=self.landing.at[index], send_sem=self.send.at[index], recv_sem=self.recv.at[index],
            device_id=peer, device_id_type=MESH_ID,
        )

    def arrived(self, index):
        self.copy(self.slot(0), index, self.p.x_peer).wait_recv()
        return self.landing[index].astype(F32)

    def start(self):
        p = self.p
        for j in range(p.nz):
            diagonal = self.slot(j, turn_x=True, turn_t=True)
            self.copy(diagonal, j, p.x_peer if j < self.half else p.y_peer).start()
        for j in range(p.nz):
            if j < self.half:
                self.copy(self.slot(j, turn_x=True), self.first_x + j, p.x_peer).start()
            else:
                self.copy(self.slot(j, turn_t=True), self.first_y + j, p.y_peer).start()

    def pass_on(self, j):
        p = self.p
        kwargs = {"turn_t": True} if j < self.half else {"turn_x": True}
        slot = self.relay.at[j]
        slot[...] = (self.slot(j, **kwargs)[...].astype(F32) + self.arrived(j)).astype(slot.dtype)
        if j < self.half:
            self.copy(slot, self.first_y + j, p.y_peer).start()
        else:
            self.copy(slot, self.first_x + j, p.x_peer).start()

    def along_z(self, j):
        total = self.slot(j)[...].astype(F32) + self.arrived(self.first_x + j) + self.arrived(self.first_y + j)
        if j == 0:
            return total
        slot = self.relay.at[self.p.nz + j - 1]
        slot[...] = total.astype(slot.dtype)
        self.copy(slot, self.first_z + j - 1, self.p.z_peer(j)).start()
        return None

    def finish(self, total):
        for j in range(1, self.p.nz):
            total = total + self.arrived(self.first_z + j - 1)
        for index in range(gather_copies(self.p.nz)):
            self.copy(self.slot(0), index, self.p.x_peer).wait_send()
        return total


class Swap:
    def __init__(self, peers, src, dst, send, recv, rows=RB):
        self.peer, self.src, self.dst, self.send, self.recv, self.rows = peers.core_peer, src, dst, send, recv, rows

    def copy(self, i):
        rows = block(i, self.rows)
        return pltpu.make_async_remote_copy(
            src_ref=self.src.at[rows], dst_ref=self.dst.at[rows], send_sem=self.send.at[i], recv_sem=self.recv.at[i],
            device_id=self.peer, device_id_type=MESH_ID,
        )

    def start(self, i):
        self.copy(i).start()

    def arrived(self, i):
        self.copy(i).wait_recv()

    def drain(self):
        for i in range(self.src.shape[0] // self.rows):
            self.copy(i).wait_send()


class Spread:
    def __init__(self, peers, src, dst, send, recv):
        self.p, self.src, self.dst, self.send, self.recv = peers, src, dst, send, recv
        self.half = src.shape[0] // 2
        self.tb = lax.axis_index("tb")

    def copy(self, src, core, index, peer):
        rows = pl.ds(pl.multiple_of(core * self.half, self.half), self.half)
        return pltpu.make_async_remote_copy(
            src_ref=src.at[rows], dst_ref=self.dst.at[rows], send_sem=self.send.at[index], recv_sem=self.recv.at[index],
            device_id=peer, device_id_type=MESH_ID,
        )

    def start(self):
        self.copy(self.src, self.tb, 0, self.p.y_peer).start()

    def pass_on(self):
        self.copy(self.src, self.tb, 0, self.p.y_peer).wait_recv()
        self.copy(self.dst, self.tb, 1, self.p.core_peer).start()

    def finish(self):
        self.copy(self.dst, 1 - self.tb, 1, self.p.core_peer).wait_recv()
        self.copy(self.src, self.tb, 0, self.p.y_peer).wait_send()
        self.copy(self.dst, self.tb, 1, self.p.core_peer).wait_send()


def pack_rows(w_in, w_out):
    return jnp.concatenate([w_in[0], w_in[1], w_in[2], w_out[...].T], axis=1).astype(BF)


def add_gather_steps(steps, name, work, nz):
    for j in range(1, nz):
        steps.add(name, work.after_z, j)
    for j in range(nz):
        steps.add(name, work.after_plane, j)
    steps.add(name, work.finish)


def forward_kernel(nz, gathers, r):
    peers = Peers(nz)
    local = Local(r.local)
    local.row("x", r.target, r.x)
    local.row("mem", r.memory, r.mem)
    peers.greet(core=True, plane=gathers)
    steps = Steps()
    packs = (r.w_self, r.w_cross, r.w_up, r.w_down)
    if gathers:
        here = peers.ta, peers.z * 2 + peers.x
        works = [Gather(peers, g, r.g_send.at[k], r.g_recv.at[k], r.stage.at[k]) for k, g in enumerate(packs)]
        names = Gather(peers, r.n_all, r.g_send.at[4], r.g_recv.at[4])
        r.n_all[here] = jnp.zeros(r.n_all.shape[2:], BF)
        r.n_all[here[0], here[1], 0 : r.m_norm.shape[0], 0 : r.m_norm.shape[1]] = r.m_norm[...].astype(BF)
        names.start()
        r.stage[0] = pack_rows(r.m_self_in, r.m_self_out)
        works[0].start()
        local.start("own0", r.stage.at[0], packs[0].at[here])
        r.stage[1] = pack_rows(r.m_cross_in, r.m_cross_out)
        r.stage[2] = r.m_up[...].astype(BF)
        r.stage[3] = r.m_down[...].astype(BF)
        for k in range(1, 4):
            local.start("own%d" % k, r.stage.at[k], packs[k].at[here])
        for j in range(1, nz):
            names.after_z(j)
            works[0].after_z(j)
        for j in range(nz):
            names.after_plane(j)
        names.finish()
        span = r.m_norm.shape[1]
        feature = lax.broadcasted_iota(jnp.int32, (r.n_all.shape[3], r.x.shape[1]), 1)
        lane = lax.broadcasted_iota(jnp.int32, (r.n_all.shape[3], r.x.shape[1]), 0)
        norms = jnp.zeros((r.n_all.shape[2], r.x.shape[1]), F32)
        for d in range(2 * nz):
            norms += nn(r.n_all[0, d], ((feature == lane + d * span) & (lane < span)).astype(BF))
        r.norms[...] = norms
        works[1].start()
        steps_self = Steps()
        for j in range(nz):
            steps_self.add("self", works[0].after_plane, j)
        steps_self.add("self", works[0].finish)
        for name, k in (("cross", 1), ("up", 2), ("down", 3)):
            for j in range(1, nz):
                steps.add(name, works[k].after_z, j)
            if k < 3:
                steps.add(name, works[k + 1].start)
            for j in range(nz):
                steps.add(name, works[k].after_plane, j)
            steps.add(name, works[k].finish)
        norm_ref = r.norms
    else:
        steps_self = Steps()
        norm_ref = r.norms
    blocks = r.x.shape[0] // RB
    cols = r.att_a.shape[1]
    local.wait("x", "mem")

    @pl.loop(0, blocks)
    def _(i):
        r.n_a[block(i), :] = norm_forward(r.x[block(i), :].astype(F32), norm_ref[0:1, :], norm_ref[3:4, :])

    local.start("n_a", r.n_a, r.normed_one)
    steps_self.drain()
    if gathers:
        local.wait("own0")
    local.start("raw_a", packs[0], r.raw)
    local.wait("raw_a")
    join_groups(r.raw, r.wj_a)

    def project(normed, weights, qkv, i):
        q = nn(normed[block(i), :], weights[:, 0:cols]).astype(BF).astype(F32) * (1.0 / math.sqrt(HD))
        qkv[block(i), 0:cols] = q.astype(BF)

    def project_rest(source, weights, qkv, i):
        qkv[block(i), cols : 3 * cols] = nn(source[block(i), :], weights[:, cols : 3 * cols]).astype(BF)

    for i in range(blocks):
        project(r.n_a, r.wj_a, r.qkv_a, i)
        project_rest(r.n_a, r.wj_a, r.qkv_a, i)
        steps.step()
    local.start("qkv_a", r.qkv_a, r.qkv_one)
    swap_a = Swap(peers, r.own_a, r.other_a, r.s_send.at[0], r.s_recv.at[0])
    swap_b = Swap(peers, r.own_b, r.other_b, r.s_send.at[1], r.s_recv.at[1])

    def out_of(att, weights, own, swap, i):
        own[block(i), :] = nt(att[block(i), :], weights[:, 3 * cols : 4 * cols]).astype(BF)
        swap.start(i)
        steps.step(2)

    attend(
        r.qkv_a, partial(self_bias, r.q_ids, r.k_ids), True, r.att_a, r.lse_one, r.bias,
        partial(out_of, r.att_a, r.wj_a, r.own_a, swap_a),
    )
    local.start("att_a", r.att_a, r.att_one)
    steps.until("cross")
    if gathers:
        local.wait("own1")
    local.start("raw_b", packs[1], r.raw)
    local.wait("raw_b")
    join_groups(r.raw, r.wj_b)
    for i in range(blocks):
        project_rest(r.mem, r.wj_b, r.qkv_b, i)
        steps.step()
    for i in range(blocks):
        swap_a.arrived(i)
        h = r.x[block(i), :].astype(F32) + (r.own_a[block(i), :].astype(F32) + r.other_a[block(i), :].astype(F32))
        r.h_a[block(i), :] = h
        r.n_b[block(i), :] = norm_forward(h, norm_ref[1:2, :], norm_ref[4:5, :])
        project(r.n_b, r.wj_b, r.qkv_b, i)
    steps.step()
    local.start("h_a", r.h_a, r.hidden_one)
    local.start("n_b", r.n_b, r.normed_two)
    local.start("qkv_b", r.qkv_b, r.qkv_two)
    attend(
        r.qkv_b, partial(cross_bias, r.q_ids, r.m_ids), False, r.att_b, r.lse_two, r.bias,
        partial(out_of, r.att_b, r.wj_b, r.own_b, swap_b),
    )
    local.start("att_b", r.att_b, r.att_two)
    for i in range(blocks):
        swap_b.arrived(i)
        r.h_b[block(i), :] = r.h_a[block(i), :] + (
            r.own_b[block(i), :].astype(F32) + r.other_b[block(i), :].astype(F32)
        )
    local.start("h_b", r.h_b, r.hidden_two)
    swap_a.drain()
    swap_b.drain()
    steps.drain()
    local.drain()


def back_in(upstream, values, gain, residual, sums):
    delta, gain_part, shift_part = norm_backward(upstream, values, gain)
    sums[0:1, :] += gain_part
    sums[1:2, :] += shift_part
    return residual + delta


def store_joined(pack, first):
    def store(d, values):
        width = pack.shape[3] // 4
        for s in range(values.shape[1] // (2 * width)):
            for t in range(2):
                piece = values[:, (2 * s + t) * width : (2 * s + t + 1) * width].astype(BF)
                pack[t, d, :, (first + s) * width : (first + s + 1) * width] = piece

    return store


def reduce_steps(steps, name, work, nz):
    for j in range(nz):
        steps.add(name, work.pass_on, j)
    for j in range(1, nz):
        steps.add(name, work.along_z, j)


def middle_kernel(nz, reduces, r):
    peers = Peers(nz)
    local = Local(r.local)
    local.start("h", r.hidden_two, r.h)
    local.row("cot", r.cotangent, r.cot)
    local.start("up", r.w_up, r.up)
    local.start("down", r.w_down, r.down)
    local.start("n", r.normed_two, r.n_in)
    local.row("mem", r.memory, r.mem)
    peers.greet(core=True, plane=reduces)
    depth, blocks, cols = r.h.shape[1], r.h.shape[0] // RB, r.dk_sum.shape[1]
    qkv, att = r.active.at[:, 0 : 3 * cols], r.active.at[:, 3 * cols : 4 * cols]
    dqkv, grad = r.pre_grad.at[:, 0 : 3 * cols], r.pre_grad.at[:, 3 * cols : 4 * cols]
    hidden = r.active.shape[1] // 2
    row_low, own_q, own_m = r.n3, r.own_d, r.own_p
    steps = Steps()
    swap_p = Swap(peers, r.own_p, r.other_p, r.s_send.at[0], r.s_recv.at[0])
    swap_d = Swap(peers, r.own_d, r.other_d, r.s_send.at[1], r.s_recv.at[1])
    swap_q = Swap(peers, own_q, r.dn_other, r.s_send.at[2], r.s_recv.at[2])
    swap_m = Swap(peers, own_m, r.other_m, r.s_send.at[3], r.s_recv.at[3])
    spread = Spread(peers, row_low, r.block_other, r.y_send, r.y_recv)
    r.norm_sums[...] = jnp.zeros_like(r.norm_sums)
    local.wait("h", "cot", "up", "down")

    @pl.loop(0, blocks)
    def _(i):
        n = norm_forward(r.h[block(i), :], r.norms[2:3, :], r.norms[5:6, :])
        r.n3[block(i), :] = n
        e = r.cot[block(i), :]
        total = grad_total = None
        for t in range(2):
            up, down = r.up[t].reshape(depth, -1), r.down[t].reshape(depth, -1)
            activated, slope = gelu_with_slope(nn(n, up))
            activated = activated.astype(BF)
            du = (nn(e, down) * slope).astype(BF)
            r.active[block(i), t * hidden : (t + 1) * hidden] = activated
            r.pre_grad[block(i), t * hidden : (t + 1) * hidden] = du
            one, two = nt(activated, down), nt(du, up)
            total = one if total is None else total + one
            grad_total = two if grad_total is None else grad_total + two
        r.own_p[block(i), :] = total.astype(BF)
        swap_p.start(i)
        r.own_d[block(i), :] = grad_total.astype(BF)
        swap_d.start(i)

    def store_into(pack, t):
        def store(d, values):
            pack[t, d] = values.astype(BF)

        return store

    local.start("raw", r.w_cross, r.up)
    transpose_into(r.cot, r.turned)
    for t in range(2):
        gradient(r.turned, lambda: r.active[:, t * hidden : (t + 1) * hidden], store_into(r.p_down, t))
    local.start("qkv", r.qkv_two, qkv)
    local.start("att", r.att_two, att)
    works = []
    if reduces:
        works = [
            Reduce(peers, p, r.landing.at[k], r.relay.at[k], r.r_send.at[k], r.r_recv.at[k])
            for k, p in enumerate((r.p_down, r.p_up))
        ]
        works[0].start()
    transpose_into(r.n3, r.turned)
    for t in range(2):
        gradient(r.turned, lambda: r.pre_grad[:, t * hidden : (t + 1) * hidden], store_into(r.p_up, t))
    if reduces:
        works[1].start()
        for k in range(2):
            reduce_steps(steps, "ffn", works[k], nz)
    else:
        local.start("p_up", r.p_up, r.out_up)
        local.start("p_down", r.p_down, r.out_down)
    local.wait("raw")
    join_groups(r.up, r.wj)
    for i in range(blocks):
        swap_d.arrived(i)
        upstream = r.own_d[block(i), :].astype(F32) + r.other_d[block(i), :].astype(F32)
        e = back_in(upstream, r.h[block(i), :], r.norms[2:3, :], r.cot[block(i), :].astype(F32), r.norm_sums)
        r.e[block(i), :] = e
        r.low[block(i), :] = e.astype(BF)
        grad[block(i), :] = nn(e.astype(BF), r.wj[:, 3 * cols : 4 * cols]).astype(BF)
    local.start("e", r.e, r.residual)
    for i in range(blocks):
        swap_p.arrived(i)
        row = r.h[block(i), :] + (r.own_p[block(i), :].astype(F32) + r.other_p[block(i), :].astype(F32))
        r.h[block(i), :] = row
        row_low[block(i), :] = row.astype(BF)
    local.start("row", r.h, r.block_own)
    spread.start()
    steps.step()
    local.wait("qkv", "att", "n", "mem")

    swap_d.drain()

    def after(i):
        own_q[block(i), :] = nt(dqkv[block(i), 0:cols], r.wj[:, 0:cols]).astype(BF)
        swap_q.start(i)
        steps.step(2)

    transpose_into(r.low, r.turned)
    gradient(r.turned, lambda: att[...], store_joined(r.p_cross, 3))
    steps.step()
    attend_back(
        qkv, att, grad, r.lse_two, partial(cross_bias_turned, r.q_ids, r.m_ids), False, dqkv, r.dk_sum,
        r.dv_sum, r.bias, after,
    )
    spread.pass_on()
    swap_p.drain()
    for i in range(blocks):
        own_m[block(i), :] = nt(dqkv[block(i), cols : 3 * cols], r.wj[:, cols : 3 * cols]).astype(BF)
        swap_m.start(i)
    steps.step()
    transpose_into(r.n_in, r.turned)
    gradient(r.turned, lambda: dqkv[:, 0:cols], store_joined(r.p_cross, 0))
    transpose_into(r.mem, r.turned)
    gradient(r.turned, lambda: dqkv[:, cols : 3 * cols], store_joined(r.p_cross, 1))
    local.start("p_cross", r.p_cross, r.out_cross)
    local.start("own_q", own_q, r.dn_own)
    local.wait("e")
    for i in range(blocks):
        swap_m.arrived(i)
        r.e[block(i), :] = own_m[block(i), :].astype(F32) + r.other_m[block(i), :].astype(F32)
    local.start("mem_row", r.e, r.mem_own)
    for i in range(blocks):
        swap_q.arrived(i)
    steps.drain()
    if reduces:
        for k, out in enumerate((r.red_down, r.red_up)):
            out[...] = works[k].finish(works[k].along_z(0))
    spread.finish()
    for swap in (swap_q, swap_m):
        swap.drain()
    local.drain()


def last_kernel(nz, reduces, tensor_size, r):
    peers = Peers(nz)
    local = Local(r.local)
    if reduces:
        local.start("p_cross", r.g_cross, r.p_cross)
    local.start("e", r.residual, r.e)
    local.start("own_d", r.dn_own, r.own_d)
    local.start("other_d", r.dn_other, r.other_d)
    local.start("h", r.hidden_one, r.h)
    local.start("raw", r.w_self, r.raw)
    local.start("qkv", r.qkv_one, r.qkv)
    local.start("att", r.att_one, r.att)
    local.start("n", r.normed_one, r.n_in)
    local.row("x", r.target, r.x)
    local.start("mem", r.mem_own, r.mem_row)
    peers.greet(core=True, plane=reduces)
    blocks, cols = r.h.shape[0] // RB, r.att.shape[1]
    steps = Steps()
    swap_q = Swap(peers, r.own_q, r.other_q, r.s_send.at[0], r.s_recv.at[0])
    spread_m = Spread(peers, r.mem_low, r.mem_other, r.y_send.at[0], r.y_recv.at[0])
    spread_t = Spread(peers, r.row_low, r.target_other, r.y_send.at[1], r.y_recv.at[1])
    works = []
    if reduces:
        works = [
            Reduce(peers, p, r.landing.at[k], r.relay.at[k], r.r_send.at[k], r.r_recv.at[k])
            for k, p in enumerate((r.p_cross, r.p_self))
        ]
        works.append(Reduce(peers, r.p_norm, r.n_landing, r.n_relay, r.r_send.at[2], r.r_recv.at[2]))
        local.wait("p_cross")
        works[0].start()
        reduce_steps(steps, "cross", works[0], nz)
    r.norm_sums[...] = jnp.zeros_like(r.norm_sums)
    local.wait("raw")
    join_groups(r.raw, r.wj)
    local.wait("e", "own_d", "other_d", "h")
    for i in range(blocks):
        upstream = r.own_d[block(i), :].astype(F32) + r.other_d[block(i), :].astype(F32)
        e = back_in(upstream, r.h[block(i), :], r.norms[1:2, :], r.e[block(i), :], r.norm_sums)
        r.e[block(i), :] = e
        r.low[block(i), :] = e.astype(BF)
        r.grad[block(i), :] = nn(e.astype(BF), r.wj[:, 3 * cols : 4 * cols]).astype(BF)
    local.wait("mem")
    r.mem_low[...] = r.mem_row[...].astype(BF)
    spread_m.start()
    steps.step()
    local.wait("qkv", "att", "n", "x")
    transpose_into(r.low, r.turned)
    gradient(r.turned, lambda: r.att[...], store_joined(r.p_self, 3))
    steps.step()

    def after(i):
        r.own_q[block(i), :] = nt(r.dqkv[block(i), :], r.wj[:, 0 : 3 * cols]).astype(BF)
        swap_q.start(i)
        steps.step(2)

    attend_back(
        r.qkv, r.att, r.grad, r.lse_one, partial(self_bias_turned, r.q_ids, r.k_ids), True, r.dqkv, r.dk_sum, r.dv_sum,
        r.bias, after,
    )
    transpose_into(r.n_in, r.turned)
    gradient(r.turned, lambda: r.dqkv[...], store_joined(r.p_self, 0))
    steps.drain()
    if reduces:
        works[1].start()
        reduce_steps(steps, "self", works[1], nz)
    else:
        local.start("p_self", r.p_self, r.out_self)
    spread_m.pass_on()
    r.first_sums[...] = jnp.zeros_like(r.first_sums)
    for i in range(blocks):
        swap_q.arrived(i)
        upstream = r.own_q[block(i), :].astype(F32) + r.other_q[block(i), :].astype(F32)
        row = back_in(upstream, r.x[block(i), :].astype(F32), r.norms[0:1, :], r.e[block(i), :], r.first_sums)
        r.e[block(i), :] = row
        r.row_low[block(i), :] = row.astype(BF)
    local.start("row", r.e, r.target_own)
    spread_t.start()
    if reduces:
        depth, span = r.x.shape[1], r.x.shape[1] // (2 * nz)
        sums = jnp.concatenate(
            [r.first_sums[0:1], r.norm_sums[0:1], r.third_sums[0:1], r.first_sums[1:2], r.norm_sums[1:2]]
            + [r.third_sums[1:2], jnp.zeros((10, depth), F32)]
        ).astype(BF)
        feature = lax.broadcasted_iota(jnp.int32, (r.p_norm.shape[3], depth), 1)
        lane = lax.broadcasted_iota(jnp.int32, (r.p_norm.shape[3], depth), 0)
        for d in range(2 * nz):
            piece = nt(sums, ((feature == lane + d * span) & (lane < span)).astype(BF)).astype(BF)
            r.p_norm[0, d] = piece
            r.p_norm[1, d] = piece
        works[2].start()
        for j in range(nz):
            works[2].pass_on(j)
        for j in range(1, nz):
            works[2].along_z(j)
        steps.drain()
        squares = jnp.zeros((1, 1), F32)
        for k, out in enumerate((r.red_cross, r.red_self, r.red_norm)):
            total = works[k].finish(works[k].along_z(0))
            out[...] = total
            share = jnp.sum(jnp.sum(total * total, -1, keepdims=True), 0, keepdims=True)
            squares = squares + (share / tensor_size if k == 2 else share)
        for done in (r.red_up, r.red_down):
            squares = squares + jnp.sum(jnp.sum(done[...] * done[...], -1, keepdims=True), 0, keepdims=True)
        r.squares[...] = sum_everywhere(peers, squares, r.stage, r.heard, r.q_send, r.q_recv)
    spread_t.pass_on()
    spread_m.finish()
    spread_t.finish()
    swap_q.drain()
    local.drain()


def sum_everywhere(peers, value, stage, heard, send, recv):
    nz = peers.nz

    def copy(step, src, dst, peer):
        return pltpu.make_async_remote_copy(
            src_ref=src, dst_ref=dst, send_sem=send.at[step], recv_sem=recv.at[step], device_id=peer,
            device_id_type=MESH_ID,
        )

    value = jnp.broadcast_to(value, stage.shape[1:])
    for step, peer in enumerate((peers.core_peer, peers.x_peer, peers.y_peer)):
        stage[step] = value
        swap = copy(step, stage.at[step], heard.at[step], peer)
        swap.start()
        swap.wait()
        value = value + heard[step]
    mine = heard.at[3 + peers.z]
    mine[...] = value
    for j in range(1, nz):
        copy(2 + j, mine, mine, peers.z_peer(j)).start()
    for j in range(1, nz):
        copy(2 + j, mine, heard.at[3 + peers.down(j)], peers.z_peer(j)).wait_recv()
    for j in range(1, nz):
        copy(2 + j, mine, mine, peers.z_peer(j)).wait_send()
    total = heard[3]
    for k in range(1, nz):
        total = total + heard[3 + k]
    return total


def adam_update(weight, gradient, first, second, clip_factor, bias_one, bias_two, rate, decay):
    scaled = gradient * clip_factor
    first_new = BETA_ONE * first + (1.0 - BETA_ONE) * scaled
    second_new = BETA_TWO * second + (1.0 - BETA_TWO) * scaled * scaled
    first_hat = first_new / bias_one
    second_hat = second_new / bias_two
    weight_new = weight - rate * (first_hat / (jnp.sqrt(second_hat) + EPS_ADAM) + decay * weight)
    return weight_new, weight_new.astype(BF), first_new, second_new


RATES = (
    (RATE_MATRIX, DECAY_RATE),
    (RATE_OUTPUT, DECAY_RATE),
    (RATE_MATRIX, DECAY_RATE),
    (RATE_OUTPUT, DECAY_RATE),
    (RATE_MATRIX, DECAY_RATE),
    (RATE_MATRIX, DECAY_RATE),
    (RATE_NORMS, 0.0),
)


def shard_gradients(reduced, width):
    g_self, g_cross, g_up, g_down, g_norms = reduced
    cut = [
        [g[:, s * width : (s + 1) * width] for s in range(4)] for g in (g_self, g_cross)
    ]
    return (cut[0][:3], cut[0][3].T, cut[1][:3], cut[1][3].T, g_up, g_down.T, g_norms)


def adam_kernel(*refs):
    reduced, squares, biases = refs[:5], refs[5], refs[6]
    state, norm_out, outs = refs[7:28], refs[28], refs[29:]
    width = state[3].shape[0]
    norm = jnp.sqrt(squares[...])
    norm_out[...] = norm
    clip = (CLIP_LIMIT / jnp.maximum(norm, CLIP_LIMIT))[0:1, 0:1]
    values = [r[...] for r in reduced]
    shape = state[18].shape
    values[4] = values[4][0 : shape[0], 0 : shape[1]]
    gradients = list(shard_gradients(values, width))
    gradients[5] = values[3]
    for k, (rate, decay) in enumerate(RATES):
        weight, first, second = state[3 * k : 3 * k + 3]
        into = outs[4 * k : 4 * k + 4]
        if isinstance(gradients[k], list):
            for s in range(3):
                new = adam_update(
                    weight[s], gradients[k][s], first[s], second[s], clip, biases[0], biases[1], rate, decay
                )
                for ref, value in zip(into, new):
                    ref[s] = value
        else:
            new = adam_update(
                weight[...], gradients[k], first[...], second[...], clip, biases[0], biases[1], rate, decay
            )
            for ref, value in zip(into, new):
                ref[...] = value


def rows_kernel(place, *refs):
    own, other, outs = refs[0:3], refs[3:6], refs[6:9]
    half = pl.num_programs(0) // 2
    mine = pl.program_id(0) // half == place[0]

    @pl.when(mine)
    def _():
        for src, dst in zip(own, outs):
            dst[...] = src[...]

    @pl.when(jnp.logical_not(mine))
    def _():
        for src, dst in zip(other, outs):
            dst[...] = src[...].astype(F32)


def both_rows(own, other, ta):
    length, depth = own[0].shape
    blocks = length // RB

    def own_map(i, place):
        return jnp.where(i // blocks == place[0], i % blocks, 0), 0

    def other_map(i, place):
        return jnp.where(i // blocks == place[0], 0, i % blocks), 0

    return pl.pallas_call(
        rows_kernel,
        name="both_rows",
        out_shape=[sds((2 * length, depth), F32)] * 3,
        grid_spec=pltpu.PrefetchScalarGridSpec(
            num_scalar_prefetch=1,
            grid=(2 * blocks,),
            in_specs=[pl.BlockSpec((RB, depth), own_map)] * 3 + [pl.BlockSpec((RB, depth), other_map)] * 3,
            out_specs=[pl.BlockSpec((RB, depth), lambda i, place: (i, 0))] * 3,
        ),
        compiler_params=params(),
    )(ta.reshape(1).astype(jnp.int32), *own, *other)


def body(target, memory, cotangent, tgt_seg, mem_seg, pad_len, step_count, *state):
    dp_size, tensor_size = lax.axis_size("dp"), lax.axis_size("ta") * lax.axis_size("tb")
    ta = lax.axis_index("ta")
    self_in, self_out, cross_in, cross_out, ffn_in, ffn_out, norm_params = state[::3]
    length, depth = tgt_seg.shape[1], target.shape[1]
    mem_length = mem_seg.shape[1]
    width, span = self_out.shape
    cols, hidden = 2 * width, ffn_in.shape[1]
    fold = depth // 8
    own_transfers = dp_size == 8
    nz = dp_size // 2 if own_transfers else 1
    blocks = length // RB

    tgt_ids = lax.dynamic_slice_in_dim(tgt_seg, ta, 1)
    mem_ids = lax.dynamic_slice_in_dim(mem_seg, ta, 1)
    pad = lax.dynamic_slice_in_dim(pad_len, ta, 1)
    key_ids = jnp.where(jnp.arange(length)[None, :] < length - pad[:, None], tgt_ids, -1)
    tgt_col, mem_col, key_col = tgt_ids.reshape(length, 1), mem_ids.reshape(mem_length, 1), key_ids.reshape(length, 1)

    row, mem_row = (length, depth), (mem_length, depth)
    qkv, att, logsum = (length, 3 * cols), (length, cols), (cols // 128, 2, length)
    pack = (2, 8, fold, 4 * width)
    wide = (2, 8, fold, hidden)
    joined = (depth, 4 * cols)
    copies = gather_copies(nz)
    dma = pltpu.SemaphoreType.DMA

    def v(shape, dtype=BF):
        return pltpu.VMEM(shape, dtype)

    ins = dict(
        target=(target, 0), memory=(memory, 0), q_ids=(tgt_col, 1), k_ids=(key_ids, 1), m_ids=(mem_ids, 1)
    )
    outs = dict(
        hidden_one=(row, F32, 0), hidden_two=(row, F32, 0), normed_one=(row, BF, 0), normed_two=(row, BF, 0),
        qkv_one=(qkv, BF, 0), qkv_two=(qkv, BF, 0), att_one=(att, BF, 0), att_two=(att, BF, 0),
        lse_one=(logsum, F32, 1), lse_two=(logsum, F32, 1),
    )
    scratch = dict(
        x=v(row), mem=v(mem_row), raw=v(pack), wj_a=v(joined), wj_b=v(joined), n_a=v(row), n_b=v(row),
        qkv_a=v(qkv), qkv_b=v(qkv), att_a=v(att), att_b=v(att), h_a=v(row, F32), h_b=v(row, F32),
        own_a=v(row), other_a=v(row), own_b=v(row), other_b=v(row), bias=v((RB, max(length, mem_length)), F32),
        s_send=dma((2, blocks)), s_recv=dma((2, blocks)), local=dma((24,)),
    )
    if own_transfers:
        ins |= dict(
            m_self_in=(self_in, 1), m_self_out=(self_out, 1), m_cross_in=(cross_in, 1), m_cross_out=(cross_out, 1),
            m_up=(ffn_in, 1), m_down=(ffn_out.T, 1), m_norm=(norm_params, 1),
        )
        outs |= dict(
            w_self=(pack, BF, 0), w_cross=(pack, BF, 0), w_up=(wide, BF, 0), w_down=(wide, BF, 0),
            norms=((16, depth), F32, 1),
        )
        scratch |= dict(
            stage=v((4, fold, 4 * width)), n_all=v((2, dp_size, 16, 128)), g_send=dma((5, copies)),
            g_recv=dma((5, copies)),
        )
    else:
        norm_shard = jnp.zeros((16, span), BF).at[: norm_params.shape[0]].set(norm_params.astype(BF))
        shards = [
            jnp.concatenate([w_in[0], w_in[1], w_in[2], w_out.T], axis=1).astype(BF)
            for w_in, w_out in ((self_in, self_out), (cross_in, cross_out))
        ]
        shards += [ffn_in.astype(BF), ffn_out.T.astype(BF)]
        gathered = [
            lax.all_gather(lax.all_gather(s, "dp", axis=0, tiled=True), "ta", axis=0).reshape(2, 8, fold, s.shape[1])
            for s in shards
        ]
        norms = lax.all_gather(norm_shard, "dp", axis=1, tiled=True).astype(F32)
        ins |= dict(zip(("w_self", "w_cross", "w_up", "w_down"), ((g, 0) for g in gathered))) | dict(norms=(norms, 1))
    f = launch(
        partial(forward_kernel, nz, own_transfers), "forward", ins, outs, scratch, length * depth * 8 * cols,
        collective_id=0, has_side_effects=True,
    )
    if own_transfers:
        w_self, w_cross, w_up, w_down, norms = f.w_self, f.w_cross, f.w_up, f.w_down, f.norms
    else:
        w_self, w_cross, w_up, w_down = gathered

    ins = dict(
        hidden_two=(f.hidden_two, 0), cotangent=(cotangent, 0), w_up=(w_up, 0), w_down=(w_down, 0),
        w_cross=(w_cross, 0), qkv_two=(f.qkv_two, 0), att_two=(f.att_two, 0), normed_two=(f.normed_two, 0),
        memory=(memory, 0), lse_two=(f.lse_two, 1), norms=(norms, 1), q_ids=(tgt_ids, 1), m_ids=(mem_col, 1),
    )
    outs = dict(
        residual=(row, F32, 0), dn_own=(row, BF, 0), dn_other=(row, BF, 0), block_own=(row, F32, 0),
        block_other=(row, BF, 0), mem_own=(mem_row, F32, 0), out_cross=(pack, BF, 0), norm_sums=((8, depth), F32, 1),
    )
    back = dict(
        wj=v(joined), low=v(row), n_in=v(row), h=v(row, F32), e=v(row, F32), turned=v((depth, length)),
        own_d=v(row), other_d=v(row), local=dma((24,)), y_send=dma((2, 2)), y_recv=dma((2, 2)),
    )
    sums_m = dict(dk_sum=v((mem_length, cols), F32), dv_sum=v((mem_length, cols), F32), bias=v((mem_length, RB), F32))
    sums_s = dict(dk_sum=v((length, cols), F32), dv_sum=v((length, cols), F32), bias=v((length, RB), F32))
    reducing = dict(
        landing=v((2, copies, fold, 4 * width)), relay=v((2, 2 * nz - 1, fold, 4 * width)), r_send=dma((3, copies)),
        r_recv=dma((3, copies)),
    )
    scratch = back | sums_m | dict(
        mem=v(mem_row), up=v(wide), down=v(wide), cot=v(row), n3=v(row), active=v((length, 2 * hidden)),
        pre_grad=v((length, 2 * hidden)), own_p=v(row), other_p=v(row), other_m=v(mem_row),
        p_up=v(wide), p_down=v(wide), p_cross=v(pack), s_send=dma((4, blocks)), s_recv=dma((4, blocks)),
        y_send=dma((2,)), y_recv=dma((2,)),
    )
    if own_transfers:
        outs |= dict(red_down=((span, hidden), F32, 1), red_up=((span, hidden), F32, 1))
        scratch |= reducing
    else:
        outs |= dict(out_up=(wide, BF, 0), out_down=(wide, BF, 0))
    m = launch(
        partial(middle_kernel, nz, own_transfers), "middle", ins, outs, scratch, length * depth * (12 * hidden),
        collective_id=1, has_side_effects=True,
    )

    ins = dict(
        residual=(m.residual, 0), dn_own=(m.dn_own, 0), dn_other=(m.dn_other, 0), hidden_one=(f.hidden_one, 0),
        w_self=(w_self, 0), qkv_one=(f.qkv_one, 0), att_one=(f.att_one, 0), normed_one=(f.normed_one, 0),
        target=(target, 0), mem_own=(m.mem_own, 0), lse_one=(f.lse_one, 1), norms=(norms, 1), q_ids=(tgt_ids, 1),
        k_ids=(key_col, 1), third_sums=(m.norm_sums, 1),
    )
    outs = dict(
        target_own=(row, F32, 0), target_other=(row, BF, 0), mem_other=(mem_row, BF, 0),
        norm_sums=((8, depth), F32, 1), first_sums=((8, depth), F32, 1),
    )
    scratch = back | sums_s | dict(
        raw=v(pack), x=v(row), mem_row=v(mem_row, F32), mem_low=v(mem_row), other_q=v(row), p_self=v(pack), s_send=dma((1, blocks)),
        s_recv=dma((1, blocks)), qkv=v(qkv), att=v(att), dqkv=v(qkv), grad=v(att), row_low=v(row), own_q=v(row),
    )
    if own_transfers:
        ins |= dict(g_cross=(m.out_cross, 0), red_up=(m.red_up, 1), red_down=(m.red_down, 1))
        shard = ((span, 4 * width), F32, 1)
        outs |= dict(red_cross=shard, red_self=shard, red_norm=((16, 128), F32, 1), squares=((8, 128), F32, 1))
        scratch |= reducing | dict(
            p_cross=v(pack), p_norm=v((2, dp_size, 16, 128)), n_landing=v((copies, 16, 128)),
            n_relay=v((2 * nz - 1, 16, 128)), stage=v((3, 8, 128), F32), heard=v((3 + nz, 8, 128), F32),
            q_send=dma((2 + nz,)), q_recv=dma((2 + nz,)),
        )
    else:
        outs |= dict(out_self=(pack, BF, 0))
    b = launch(
        partial(last_kernel, nz, own_transfers, tensor_size), "last", ins, outs, scratch, length * depth * 16 * cols,
        collective_id=2, has_side_effects=True,
    )

    step_float = step_count.astype(F32)
    biases = jnp.stack([1.0 - jnp.power(BETA_ONE, step_float), 1.0 - jnp.power(BETA_TWO, step_float)])
    if own_transfers:
        turn = [a.T if 15 <= k < 18 else a for k, a in enumerate(state)]
        updated = pl.pallas_call(
            adam_kernel,
            name="adam",
            out_shape=[sds((8, 128), F32)]
            + [sds(w.shape, dt) for w in turn[::3] for dt in (F32, BF, F32, F32)],
            in_specs=vm(6) + [pl.BlockSpec(memory_space=pltpu.SMEM)] + vm(21),
            out_specs=vm(29),
            compiler_params=params(),
        )(b.red_self, b.red_cross, m.red_up, m.red_down, b.red_norm, b.squares, biases, *turn)
        global_norm, updated = updated[0][0, 0], list(updated[1:])
        updated[20:24] = [a.T for a in updated[20:24]]
    else:
        sums = (b.first_sums, b.norm_sums, m.norm_sums)
        all_sums = jnp.stack([s[k] for k in range(2) for s in sums]).astype(BF).astype(F32)
        norm_part = lax.psum_scatter(lax.psum(all_sums, "ta"), "dp", scatter_dimension=1, tiled=True)
        reduced = []
        for g in (b.out_self, m.out_cross, m.out_up, m.out_down):
            g = lax.psum_scatter(g.astype(F32), "ta", scatter_dimension=0).reshape(depth, g.shape[3])
            reduced.append(lax.psum_scatter(g, "dp", scatter_dimension=0, tiled=True))
        total = sum(jnp.sum(g * g) for g in reduced) + jnp.sum(norm_part * norm_part) / tensor_size
        global_norm = jnp.sqrt(lax.psum(total, ("dp", "ta", "tb")))
        clip = CLIP_LIMIT / jnp.maximum(global_norm, CLIP_LIMIT)
        updated = []
        for k, g in enumerate(shard_gradients(reduced + [norm_part], width)):
            g = jnp.stack(g) if isinstance(g, list) else g
            weight, first, second = state[3 * k : 3 * k + 3]
            updated += adam_update(weight, g, first, second, clip, biases[0], biases[1], *RATES[k])
    rows = both_rows(
        (m.block_own, b.target_own, m.mem_own), (m.block_other, b.target_other, b.mem_other), ta
    )
    return (global_norm, *rows, *updated)


def solution(mesh):
    dp_size, tensor_size = mesh.shape["dp"], mesh.shape["tensor"]
    grid = Mesh(mesh.devices.reshape(dp_size, 2, tensor_size // 2), ("dp", "ta", "tb"))
    tensor = ("ta", "tb")
    rows = P("dp", None)
    place = (
        P(None, "dp", tensor),
        P(tensor, "dp"),
        P(None, "dp", tensor),
        P(tensor, "dp"),
        P("dp", tensor),
        P(tensor, "dp"),
        P(None, "dp"),
    )
    return jax.shard_map(
        body,
        mesh=grid,
        in_specs=(rows,) * 5 + (P("dp"), P()) + tuple(p for p in place for _ in range(3)),
        out_specs=(P(), rows, rows, rows) + tuple(p for p in place for _ in range(4)),
        check_vma=False,
    )
```

```python
from functools import partial
import math
from types import SimpleNamespace

import jax
import jax.numpy as jnp
from jax import lax
from jax.experimental import pallas as pl
from jax.experimental.pallas import tpu as pltpu
from jax.sharding import Mesh, PartitionSpec as P

HD = 64
EPS_NORM = 1e-05
NEG_FILL = -1000000000.0
BETA_ONE = 0.9
BETA_TWO = 0.999
EPS_ADAM = 1e-08
RATE_MATRIX = 0.05
RATE_OUTPUT = 0.25
RATE_NORMS = 0.75
DECAY_RATE = 0.1
CLIP_LIMIT = 1.0
GELU_COEF = 0.044715

BF = jnp.bfloat16
F32 = jnp.float32
RB = 256
FORWARD_PACE = 2.2
MIDDLE_PACE = 3.0
LAST_PACE = 3.5
PW = 768
MESH_ID = pl.DeviceIdType.MESH
VMEM_LIMIT = 63 * 1024 * 1024


def nn(a, b):
    return lax.dot_general(a, b, (((1,), (0,)), ((), ())), preferred_element_type=F32)


def nt(a, b):
    return lax.dot_general(a, b, (((1,), (1,)), ((), ())), preferred_element_type=F32)


def tn(a, b):
    return lax.dot_general(a, b, (((0,), (0,)), ((), ())), preferred_element_type=F32)


def vm(n=1):
    return [pl.BlockSpec(memory_space=pltpu.VMEM)] * n


def anym(n=1):
    return [pl.BlockSpec(memory_space=pl.ANY)] * n


def sds(shape, dtype):
    return jax.ShapeDtypeStruct(shape, dtype)


def params(**kw):
    return pltpu.CompilerParams(vmem_limit_bytes=VMEM_LIMIT, **kw)


def block(i, size=RB):
    return pl.ds(pl.multiple_of(i * size, size), size)


def gelu_with_slope(values):
    root = math.sqrt(2.0 / math.pi)
    square = values * values
    tangent = jnp.tanh(values * (root + (root * GELU_COEF) * square))
    half = 0.5 + 0.5 * tangent
    output = values * half
    slope = half + 0.5 * output * (1.0 - tangent) * (2.0 * root + (6.0 * root * GELU_COEF) * square)
    return output, slope


def norm_stats(values):
    centre = values - jnp.mean(values, -1, keepdims=True)
    inverse = lax.rsqrt(jnp.mean(centre * centre, -1, keepdims=True) + EPS_NORM)
    return centre * inverse, inverse


def norm_forward(values, gain, shift):
    scaled, _ = norm_stats(values)
    return (scaled * gain + shift).astype(BF)


def norm_backward(upstream, values, gain):
    scaled, inverse = norm_stats(values)
    weighted = upstream * gain
    product = upstream * scaled
    result = inverse * (
        weighted
        - jnp.mean(weighted, -1, keepdims=True)
        - scaled * jnp.mean(weighted * scaled, -1, keepdims=True)
    )
    return result, jnp.sum(product, 0, keepdims=True), jnp.sum(upstream, 0, keepdims=True)


def launch(kernel, name, ins, outs, scratch, macs=0, **compiler):
    names = list(ins) + list(outs) + list(scratch)

    def run(*refs):
        kernel(SimpleNamespace(**dict(zip(names, refs))))

    results = pl.pallas_call(
        run,
        name=name,
        out_shape=[sds(shape, dtype) for shape, dtype, _ in outs.values()],
        in_specs=[(vm() if inside else anym())[0] for _, inside in ins.values()],
        out_specs=[(vm() if inside else anym())[0] for _, _, inside in outs.values()],
        scratch_shapes=list(scratch.values()),
        compiler_params=params(**compiler),
        cost_estimate=pl.CostEstimate(flops=2 * macs, bytes_accessed=20 << 20, transcendentals=0),
    )(*[a for a, _ in ins.values()])
    return SimpleNamespace(**dict(zip(outs, results)))


class Local:
    def __init__(self, sems):
        self.sems, self.count, self.open = sems, 0, {}

    def start(self, name, src, dst):
        copy = pltpu.make_async_copy(src, dst, self.sems.at[self.count])
        self.count += 1
        copy.start()
        self.open[name] = copy

    def row(self, name, src, dst):
        rows = dst.shape[0]
        start = pl.multiple_of(lax.axis_index("ta") * rows, rows)
        self.start(name, src.at[pl.ds(start, rows)], dst)

    def own_row(self, name, src, dst):
        rows = src.shape[0]
        start = pl.multiple_of(lax.axis_index("ta") * rows, rows)
        self.start(name, src, dst.at[pl.ds(start, rows)])

    def wait(self, *names):
        for name in names:
            self.open.pop(name).wait()

    def drain(self):
        self.wait(*list(self.open))


class Steps:
    def __init__(self, pace=0.0):
        self.todo, self.pace, self.credit = [], pace, 0.0

    def spend(self, cost):
        self.credit += cost
        while self.todo and self.credit >= self.pace:
            self.credit -= self.pace
            self.step()

    def add(self, name, fn, *args, **kwargs):
        self.todo.append((name, partial(fn, *args, **kwargs)))

    def step(self, count=1):
        for _ in range(min(count, len(self.todo))):
            self.todo.pop(0)[1]()

    def until(self, name):
        while any(n == name for n, _ in self.todo):
            self.step()

    def drain(self):
        self.step(len(self.todo))


def join_groups(packed, joined):
    rows, width = packed.shape[2], packed.shape[3] // 4

    @pl.loop(0, packed.shape[1])
    def _(i):
        first, second = packed[0, i], packed[1, i]
        pieces = []
        for s in range(4):
            pieces += [first[:, s * width : (s + 1) * width], second[:, s * width : (s + 1) * width]]
        joined[block(i, rows), :] = jnp.concatenate(pieces, axis=1)


def gradient(source, rhs, store):
    product = tn(source, rhs)
    rows = product.shape[0] // 8
    for d in range(8):
        store(d, product[d * rows : (d + 1) * rows])


def head_masks(rows):
    lane = lax.broadcasted_iota(jnp.int32, (rows, 2 * HD), 1)
    return lane < HD


def keep_half(values, low_half, head):
    zero = jnp.zeros_like(values)
    return jnp.where(low_half, values, zero) if head == 0 else jnp.where(low_half, zero, values)


def attend(qkv, bias_of, causal, out, logsum, bias, between, after):
    rows, cols = out.shape
    size = RB if causal else bias.shape[0]

    def one(start, keys, pair):
        q_rows = pl.ds(start, size)
        lanes = slice(pair * 2 * HD, (pair + 1) * 2 * HD)
        key = qkv[0:keys, cols + pair * 2 * HD : cols + (pair + 1) * 2 * HD]
        value = qkv[0:keys, 2 * cols + pair * 2 * HD : 2 * cols + (pair + 1) * 2 * HD]
        query = qkv[q_rows, lanes]
        low_half = head_masks(size)
        outs, sums = [], []
        for head in range(2):
            scores = nt(keep_half(query, low_half, head), key) + bias[0:size, 0:keys]
            peak = jnp.max(scores, -1, keepdims=True)
            shifted = jnp.exp(scores - peak)
            total = jnp.sum(shifted, -1, keepdims=True)
            outs.append(nn(shifted.astype(BF), value) / total)
            sums.append(peak + jnp.log(total))
        out[q_rows, lanes] = jnp.where(low_half, outs[0], outs[1]).astype(BF)
        both = jnp.where(low_half, sums[0], sums[1]).T
        logsum[pair, :, q_rows] = jnp.concatenate([both[0:1], both[HD : HD + 1]], axis=0)

    for i in range(rows // size):
        keys = (i + 1) * size if causal else bias.shape[1]
        bias[0:size, 0:keys] = bias_of(i, size, keys)
        for pair in range(cols // (2 * HD)):
            one(i * size, keys, pair)
            between(size * keys * 3.4e-6)
        for k in range(size // RB):
            after(i * (size // RB) + k)


def attend_back(qkv, attended, grad, logsum, bias_of, causal, dqkv, dk_sum, dv_sum, k_turned, bias, between, after):
    rows, cols = attended.shape
    dk_sum[...] = jnp.zeros(dk_sum.shape, F32)
    dv_sum[...] = jnp.zeros(dv_sum.shape, F32)

    @pl.loop(0, k_turned.shape[1] // RB)
    def _(i):
        k_turned[:, block(i)] = qkv[block(i), cols : 2 * cols].T

    def one(q_rows, keys, pair):
        lanes = slice(pair * 2 * HD, (pair + 1) * 2 * HD)
        k_lanes = slice(cols + pair * 2 * HD, cols + (pair + 1) * 2 * HD)
        v_lanes = slice(2 * cols + pair * 2 * HD, 2 * cols + (pair + 1) * 2 * HD)
        query, key, value = qkv[q_rows, lanes], qkv[0:keys, k_lanes], qkv[0:keys, v_lanes]
        out_grad = grad[q_rows, lanes]
        low_half = head_masks(RB)
        product = (out_grad.astype(F32) * attended[q_rows, lanes].astype(F32)).T
        dk = dv = None
        dq = []
        for head in range(2):
            inner = jnp.sum(product[head * HD : (head + 1) * HD], 0, keepdims=True)
            q_head = keep_half(query, low_half, head)
            g_head = keep_half(out_grad, low_half, head)
            scores = nt(key, q_head) + bias[0:keys, :]
            weights = jnp.exp(scores - logsum[pair, head : head + 1, q_rows])
            weight_grad = nt(value, g_head)
            score_grad = (weights * (weight_grad - inner)).astype(BF)
            dv_part = nn(weights.astype(BF), g_head)
            dk_part = nn(score_grad, q_head)
            turned_rows = slice(pair * 2 * HD + head * HD, pair * 2 * HD + (head + 1) * HD)
            dq.append(nn(k_turned[turned_rows, 0:keys], score_grad))
            dv = dv_part if dv is None else dv + dv_part
            dk = dk_part if dk is None else dk + dk_part
        dqkv[q_rows, lanes] = (jnp.concatenate(dq, axis=0).T * (1.0 / math.sqrt(HD))).astype(BF)
        dk_sum[0:keys, lanes] += dk
        dv_sum[0:keys, lanes] += dv

    def settle(key_rows):
        dqkv[key_rows, cols : 2 * cols] = dk_sum[key_rows, :].astype(BF)
        dqkv[key_rows, 2 * cols : 3 * cols] = dv_sum[key_rows, :].astype(BF)

    for i in reversed(range(rows // RB)):
        keys = (i + 1) * RB if causal else bias.shape[0]
        bias[0:keys, :] = bias_of(i, keys)
        for pair in range(cols // (2 * HD)):
            one(pl.ds(i * RB, RB), keys, pair)
            between(RB * keys * 5.4e-6)
        if causal:
            settle(pl.ds(i * RB, RB))
        after(i)
    if not causal:
        pl.loop(0, dk_sum.shape[0] // RB)(lambda i: settle(block(i)))


def self_bias(q_ids, k_ids, i, rows, keys):
    same = q_ids[i * rows : (i + 1) * rows, :] == k_ids[:, 0:keys]
    q_pos = i * rows + lax.broadcasted_iota(jnp.int32, (rows, keys), 0)
    k_pos = lax.broadcasted_iota(jnp.int32, (rows, keys), 1)
    allowed = (same & (k_pos < q_pos)) | (k_pos == q_pos)
    return jnp.where(allowed, 0.0, NEG_FILL)


def self_bias_turned(q_ids, k_ids, i, keys):
    same = k_ids[0:keys, :] == q_ids[:, i * RB : (i + 1) * RB]
    q_pos = i * RB + lax.broadcasted_iota(jnp.int32, (keys, RB), 1)
    k_pos = lax.broadcasted_iota(jnp.int32, (keys, RB), 0)
    allowed = (same & (k_pos < q_pos)) | (k_pos == q_pos)
    return jnp.where(allowed, 0.0, NEG_FILL)


def cross_bias(q_ids, k_ids, i, rows, keys):
    return jnp.where(q_ids[i * rows : (i + 1) * rows, :] == k_ids[:, 0:keys], 0.0, NEG_FILL)


def cross_bias_turned(q_ids, k_ids, i, keys):
    return jnp.where(k_ids[0:keys, :] == q_ids[:, block(i)], 0.0, NEG_FILL)


def places():
    dp, ta = lax.axis_index("dp"), lax.axis_index("ta")
    return lax.div(dp, 2), lax.rem(dp, 2), ta


class Peers:
    def __init__(self, nz):
        self.nz = nz
        self.z, self.x, self.ta = places()
        self.ox, self.ot = 1 - self.x, 1 - self.ta
        self.x_peer = {"dp": self.z * 2 + self.ox}
        self.y_peer = {"ta": self.ot}
        self.tb = lax.axis_index("tb")
        self.core_peer = {"tb": 1 - self.tb}

    def up(self, j):
        return lax.rem(self.z + j, self.nz)

    def down(self, j):
        return lax.rem(self.z + (self.nz - j), self.nz)

    def z_peer(self, j):
        return {"dp": self.up(j) * 2 + self.x}

    def cube_peer(self, bits):
        turn = [bits >> 2 & 1, bits >> 1 & 1, bits & 1]
        x, ta, tb = [1 - v if t else v for v, t in zip((self.x, self.ta, self.tb), turn)]
        return {"dp": self.z * 2 + x, "ta": ta, "tb": tb}

    def row_peers(self):
        places = [(j, k) for j in range(self.nz) for k in range(2)][1:]
        return [((j, k), {"dp": self.up(j) * 2 + (self.ox if k else self.x)}) for j, k in places]

    def box_peers(self):
        places = [(j, t, k) for j in range(self.nz) for t in range(2) for k in range(2)][1:]
        return [
            ((j, t, k), {"dp": self.up(j) * 2 + (self.ox if k else self.x), "ta": self.ot if t else self.ta})
            for j, t, k in places
        ]

    def greet(self, plane, cube=False):
        others = [self.core_peer] if plane else [self.core_peer, self.y_peer]
        if plane:
            others += [peer for _, peer in self.box_peers()]
        if cube:
            others += [self.cube_peer(bits) for bits in (3, 5, 7)]
        barrier = pltpu.get_barrier_semaphore()
        for other in others:
            pl.semaphore_signal(barrier, inc=1, device_id=other, device_id_type=MESH_ID)
        pl.semaphore_wait(barrier, len(others))


SLOTS = 16


class Route:
    def __init__(self, peers, order, rows):
        self.p, self.order, self.rows = peers, order, rows
        self.sizes = {"z": peers.nz, "y": 2, "x": 2}
        self.places = [(z, y, x) for z in range(peers.nz) for y in range(2) for x in range(2)]
        self.places.sort(key=lambda place: (self.last(place), self.at(place, self.order[0])))

    def at(self, place, axis):
        return place["zyx".index(axis)]

    def last(self, place):
        return max([0] + [i + 1 for i, axis in enumerate(self.order) if self.at(place, axis)])

    def moved(self, place, axis, k):
        return tuple(k if a == axis else self.at(place, a) for a in "zyx")

    def beyond(self, place):
        return [
            (axis, k, self.moved(place, axis, k))
            for axis in self.order[self.last(place) :]
            for k in range(1, self.sizes[axis])
        ]

    def peer(self, axis, k):
        return {"z": self.p.z_peer(k), "y": self.p.y_peer, "x": self.p.x_peer}[axis]

    def index(self, place):
        return place[0] * 4 + place[1] * 2 + place[2]

    def spot(self, place, down):
        p = self.p
        z = p.down(place[0]) if down else p.up(place[0])
        return (p.ot if place[1] else p.ta), z * 2 + (p.ox if place[2] else p.x)


class Gather(Route):
    def __init__(self, peers, order, rows, out, send, recv, own):
        super().__init__(peers, order, rows)
        self.out, self.send, self.recv, self.own = out, send, recv, own

    def copy(self, place, new, peer):
        slot = self.out.at[(*self.spot(place, True), self.rows)]
        return pltpu.make_async_remote_copy(
            src_ref=slot if any(place) else self.own.at[self.rows], dst_ref=slot, send_sem=self.send.at[self.index(new)],
            recv_sem=self.recv.at[self.index(new)], device_id=peer, device_id_type=MESH_ID,
        )

    def arrived(self, place):
        slot = self.out.at[(*self.spot(place, True), self.rows)]
        pltpu.make_async_remote_copy(
            src_ref=slot, dst_ref=slot, send_sem=self.send.at[self.index(place)],
            recv_sem=self.recv.at[self.index(place)], device_id=self.p.y_peer, device_id_type=MESH_ID,
        ).wait_recv()

    def pass_on(self, place):
        if any(place):
            self.arrived(place)
        for axis, k, new in self.beyond(place):
            self.copy(place, new, self.peer(axis, k)).start()

    def finish(self):
        for place in self.places:
            if self.last(place) == 3:
                self.arrived(place)

    def close(self):
        for place in self.places:
            for axis, k, new in self.beyond(place):
                self.copy(place, new, self.peer(axis, k)).wait_send()


class Reduce(Route):
    def __init__(self, peers, order, rows, part, landing, relay, send, recv):
        super().__init__(peers, order, rows)
        self.part, self.landing, self.relay, self.send, self.recv = part, landing, relay, send, recv
        self.relayed = [place for place in self.places if 0 < self.last(place) < 3]

    def copy(self, place):
        axis = self.order[self.last(place) - 1]
        if self.last(place) == 3:
            src = self.part.at[(*self.spot(place, False), self.rows)]
        else:
            src = self.relay.at[self.relayed.index(place), self.rows]
        return pltpu.make_async_remote_copy(
            src_ref=src, dst_ref=self.landing.at[self.index(place), self.rows], send_sem=self.send.at[self.index(place)],
            recv_sem=self.recv.at[self.index(place)], device_id=self.peer(axis, self.at(place, axis)),
            device_id_type=MESH_ID,
        )

    def total(self, place):
        t, d = self.spot(place, False)
        total = self.part[t, d, self.rows, :].astype(F32)
        for _, _, new in self.beyond(place):
            self.copy(new).wait_recv()
            total = total + self.landing[self.index(new), self.rows, :].astype(F32)
        return total

    def start(self):
        for place in self.places:
            if self.last(place) == 3:
                self.copy(place).start()

    def pass_on(self, place):
        self.relay[self.relayed.index(place), self.rows, :] = self.total(place).astype(self.relay.dtype)
        self.copy(place).start()

    def finish(self):
        total = self.total((0, 0, 0))
        for place in self.places:
            if any(place):
                self.copy(place).wait_send()
        return total


class Group:
    def __init__(self, works):
        self.works = works

    def start(self):
        for w in self.works:
            if isinstance(w, Gather):
                w.pass_on((0, 0, 0))
            else:
                w.start()

    def stages(self):
        lists = []
        for w in self.works:
            places = [p for p in w.places if 0 < w.last(p) < 3]
            places.sort(key=w.last, reverse=isinstance(w, Reduce))
            lists.append([(w, p) for p in places])
        count = max(len(places) for places in lists)
        return [[places[i] for places in lists if i < len(places)] for i in range(count)]

    def add_to(self, steps, name, between=None, at=None):
        for i, stage in enumerate(self.stages()):
            if i == at:
                steps.add(name, between)
            steps.add(name, self.run, stage)

    def run(self, stage):
        for w, place in stage:
            w.pass_on(place)

    def finish(self):
        totals = [w.finish() for w in self.works]
        return totals[0] if len(totals) == 1 else jnp.concatenate(totals) if totals[0] is not None else None

    def close(self):
        for w in self.works:
            w.close()


def gather_group(peers, split, out, send, recv, own):
    rows, works = 0, []
    for k, (order, count) in enumerate(split):
        works.append(Gather(peers, order, pl.ds(rows, count), out, send.at[k], recv.at[k], own))
        rows += count
    return Group(works)


def reduce_group(peers, split, part, landing, relay, send, recv):
    rows, works = 0, []
    for k, (order, count) in enumerate(split):
        works.append(Reduce(peers, order, pl.ds(rows, count), part, landing, relay, send.at[k], recv.at[k]))
        rows += count
    return Group(works)


def split_rows(rows, first, second, share):
    count = max(16, int(rows * share) // 16 * 16)
    return ((first, count), (second, rows - count))


class Swap:
    def __init__(self, peers, src, dst, send, recv, rows=RB):
        self.peer, self.src, self.dst, self.send, self.recv, self.rows = peers.core_peer, src, dst, send, recv, rows

    def copy(self, i):
        rows = block(i, self.rows)
        return pltpu.make_async_remote_copy(
            src_ref=self.src.at[rows], dst_ref=self.dst.at[rows], send_sem=self.send.at[i], recv_sem=self.recv.at[i],
            device_id=self.peer, device_id_type=MESH_ID,
        )

    def start(self, i):
        self.copy(i).start()

    def arrived(self, i):
        self.copy(i).wait_recv()

    def drain(self):
        for i in range(self.src.shape[0] // self.rows):
            self.copy(i).wait_send()


class Spread:
    def __init__(self, peers, src, dst, send, recv, parts):
        self.p, self.src, self.dst, self.send, self.recv, self.parts = peers, src, dst, send, recv, parts
        self.half = src.shape[0] // 2
        self.size = self.half // parts

    def rows(self, core, i, ta=None):
        start = core * self.half + i * self.size
        start = start if ta is None else ta * 2 * self.half + start
        return pl.ds(pl.multiple_of(start, self.size), self.size)

    def copy(self, src, dst_ta, core, i, hop, peer):
        return pltpu.make_async_remote_copy(
            src_ref=src, dst_ref=self.dst.at[self.rows(core, i, dst_ta)], send_sem=self.send.at[hop, i],
            recv_sem=self.recv.at[hop, i], device_id=peer, device_id_type=MESH_ID,
        )

    def across(self, i):
        p = self.p
        return self.copy(self.src.at[self.rows(p.tb, i)], p.ta, p.tb, i, 0, p.y_peer)

    def beside(self, i):
        p = self.p
        return self.copy(self.dst.at[self.rows(p.tb, i, p.ot)], p.ot, p.tb, i, 1, p.core_peer)

    def start(self, i):
        self.across(i).start()

    def start_all(self):
        for i in range(self.parts):
            self.start(i)

    def pass_on(self, i):
        p = self.p
        self.copy(self.src.at[self.rows(p.tb, i)], p.ot, p.tb, i, 0, p.y_peer).wait_recv()
        self.beside(i).start()

    def finish(self):
        p = self.p
        for i in range(self.parts):
            self.copy(self.src.at[self.rows(p.tb, i)], p.ot, 1 - p.tb, i, 1, p.core_peer).wait_recv()
            self.across(i).wait_send()
            self.beside(i).wait_send()


def pack_rows(w_in, w_out):
    return jnp.concatenate([w_in[0], w_in[1], w_in[2], w_out[...].T], axis=1).astype(BF)


def forward_kernel(nz, gathers, r):
    peers = Peers(nz)
    local = Local(r.local)
    local.row("x", r.target, r.x)
    local.row("mem", r.memory, r.mem)
    local.row("cot", r.cotangent, r.cot)
    peers.greet(gathers)
    steps = Steps(FORWARD_PACE)
    packs = (r.w_self, r.w_cross, r.w_up, r.w_down)
    if gathers:
        here = peers.ta, peers.z * 2 + peers.x
        split = split_rows(r.stage.shape[1], "zyx", "xzy", 0.67)
        works = [gather_group(peers, split, g, r.g_send.at[k], r.g_recv.at[k], r.stage.at[k]) for k, g in enumerate(packs)]
        mine = peers.z * 2 + peers.x
        r.n_all[mine] = jnp.zeros(r.n_all.shape[1:], BF)
        r.n_all[mine, 0 : r.m_norm.shape[0], 0 : r.m_norm.shape[1]] = r.m_norm[...].astype(BF)

        def norm_copy(place, slot, peer):
            index = place[0] * 2 + place[1]
            return pltpu.make_async_remote_copy(
                src_ref=r.n_all.at[slot], dst_ref=r.n_all.at[slot], send_sem=r.n_send.at[index],
                recv_sem=r.n_recv.at[index], device_id=peer, device_id_type=MESH_ID,
            )

        for place, peer in peers.row_peers():
            norm_copy(place, mine, peer).start()
        r.stage[0] = pack_rows(r.m_self_in, r.m_self_out)
        works[0].start()
        local.start("own0", r.stage.at[0], packs[0].at[here])
        r.stage[1] = pack_rows(r.m_cross_in, r.m_cross_out)
        r.stage[2] = r.m_up[...].astype(BF)
        r.stage[3] = r.m_down[...].astype(BF)
        for k in range(1, 4):
            local.start("own%d" % k, r.stage.at[k], packs[k].at[here])
        first = Steps()
        works[0].add_to(first, "self", works[1].start, 5)
        first.drain()
        finish = Steps()
        for work in works:
            finish.add("close", work.close)
        for place, peer in peers.row_peers():
            slot = peers.down(place[0]) * 2 + (peers.ox if place[1] else peers.x)
            norm_copy(place, slot, peer).wait_recv()
            finish.add("norm", norm_copy(place, mine, peer).wait_send)
        span = r.m_norm.shape[1]
        feature = lax.broadcasted_iota(jnp.int32, (r.n_all.shape[2], r.x.shape[1]), 1)
        lane = lax.broadcasted_iota(jnp.int32, (r.n_all.shape[2], r.x.shape[1]), 0)
        norms = jnp.zeros((r.n_all.shape[1], r.x.shape[1]), F32)
        for d in range(2 * nz):
            norms += nn(r.n_all[d], ((feature == lane + d * span) & (lane < span)).astype(BF))
        r.norms[...] = norms
        for k, name in ((1, "cross"), (2, "up"), (3, "down")):
            works[k].add_to(steps, name, works[k + 1].start if k < 3 else None, 5 if k < 3 else None)
            steps.add(name, works[k].finish)
    norm_ref = r.norms
    blocks = r.x.shape[0] // RB
    cols = r.att_a.shape[1]
    local.wait("x", "mem")

    @pl.loop(0, blocks)
    def _(i):
        r.n_a[block(i), :] = norm_forward(r.x[block(i), :].astype(F32), norm_ref[0:1, :], norm_ref[3:4, :])

    local.start("n_a", r.n_a, r.normed_one)
    if gathers:
        works[0].finish()
        local.wait("own0")
    local.start("raw_a", packs[0], r.raw)
    steps.spend(2.0)
    local.wait("raw_a")
    join_groups(r.raw, r.wj_a)
    steps.spend(2.0)

    wide = 2 * RB

    def project(normed, weights, qkv, i):
        q = nn(normed[block(i, wide), :], weights[:, 0:cols]).astype(BF).astype(F32) * (1.0 / math.sqrt(HD))
        qkv[block(i, wide), 0:cols] = q.astype(BF)

    def project_rest(source, weights, qkv, i):
        qkv[block(i, wide), cols : 3 * cols] = nn(source[block(i, wide), :], weights[:, cols : 3 * cols]).astype(BF)

    for i in range(blocks // 2):
        project(r.n_a, r.wj_a, r.qkv_a, i)
        steps.spend(0.6)
        project_rest(r.n_a, r.wj_a, r.qkv_a, i)
        steps.spend(1.0)
    local.start("qkv_a", r.qkv_a, r.qkv_one)
    swap_a = Swap(peers, r.own_a, r.other_a, r.s_send.at[0], r.s_recv.at[0])
    swap_b = Swap(peers, r.own_b, r.other_b, r.s_send.at[1], r.s_recv.at[1])

    def out_of(att, weights, own, swap, i):
        own[block(i), :] = nt(att[block(i), :], weights[:, 3 * cols : 4 * cols]).astype(BF)
        swap.start(i)
        steps.spend(0.4)

    attend(
        r.qkv_a, partial(self_bias, r.q_ids, r.k_ids), True, r.att_a, r.lse_one, r.bias,
        steps.spend, partial(out_of, r.att_a, r.wj_a, r.own_a, swap_a),
    )
    local.start("att_a", r.att_a, r.att_one)
    steps.until("cross")
    if gathers:
        local.wait("own1")
    local.start("raw_b", packs[1], r.raw)
    local.wait("raw_b")
    join_groups(r.raw, r.wj_b)
    steps.spend(2.0)
    for i in range(blocks // 2):
        project_rest(r.mem, r.wj_b, r.qkv_b, i)
        steps.spend(1.0)
    for i in range(blocks):
        swap_a.arrived(i)
        h = r.x[block(i), :].astype(F32) + (r.own_a[block(i), :].astype(F32) + r.other_a[block(i), :].astype(F32))
        r.h_a[block(i), :] = h
        r.l_a[block(i), :] = h.astype(BF)
        r.n_b[block(i), :] = norm_forward(h, norm_ref[1:2, :], norm_ref[4:5, :])
        if i % 2 == 1:
            project(r.n_b, r.wj_b, r.qkv_b, i // 2)
            steps.spend(2.2)
    local.start("h_a", r.l_a, r.hidden_one)
    local.start("n_b", r.n_b, r.normed_two)
    local.start("qkv_b", r.qkv_b, r.qkv_two)
    attend(
        r.qkv_b, partial(cross_bias, r.q_ids, r.m_ids), False, r.att_b, r.lse_two, r.bias,
        steps.spend, partial(out_of, r.att_b, r.wj_b, r.own_b, swap_b),
    )
    local.start("att_b", r.att_b, r.att_two)
    for i in range(blocks):
        swap_b.arrived(i)
        h = r.h_a[block(i), :] + (r.own_b[block(i), :].astype(F32) + r.other_b[block(i), :].astype(F32))
        r.l_b[block(i), :] = h.astype(BF)
        r.n_c[block(i), :] = norm_forward(h, norm_ref[2:3, :], norm_ref[5:6, :])
        steps.spend(0.7)
    local.start("h_b", r.l_b, r.hidden_two)
    local.start("n_c", r.n_c, r.normed_three)
    steps.until("up")
    if gathers:
        local.wait("own2")
    local.start("up", packs[2], r.raw)
    local.wait("up", "cot")
    depth, hidden = r.x.shape[1], r.active.shape[1] // 2
    for t in range(2):
        half = slice(t * hidden, (t + 1) * hidden)
        for i in range(blocks // 2):
            rows = block(i, wide)
            activated, slope = gelu_with_slope(nn(r.n_c[rows, :], r.raw[t].reshape(depth, hidden)))
            r.active[rows, half] = activated.astype(BF)
            r.slope[rows, half] = slope.astype(BF)
            steps.spend(1.0)
        local.start("active%d" % t, r.active.at[:, half], r.ffn_active.at[:, half])
        local.start("slope%d" % t, r.slope.at[:, half], r.ffn_slope.at[:, half])
        gradient(r.cot[...], r.active[:, half], store_into(r.p_down, t))
        steps.spend(1.5)
    local.start("p_down", r.p_down, r.g_down)
    swap_a.drain()
    swap_b.drain()
    steps.drain()
    if gathers:
        finish.drain()
    local.drain()


def store_into(pack, t):
    def store(d, values):
        pack[t, d] = values.astype(BF)

    return store


def back_in(upstream, values, gain, residual, sums):
    delta, gain_part, shift_part = norm_backward(upstream, values, gain)
    sums[0:1, :] += gain_part
    sums[1:2, :] += shift_part
    return residual + delta


def store_joined(pack, first):
    def store(d, values):
        width = pack.shape[3] // 4
        for s in range(values.shape[1] // (2 * width)):
            for t in range(2):
                piece = values[:, (2 * s + t) * width : (2 * s + t + 1) * width].astype(BF)
                pack[t, d, :, (first + s) * width : (first + s + 1) * width] = piece

    return store


def middle_kernel(nz, reduces, r):
    peers = Peers(nz)
    local = Local(r.local)
    if reduces:
        local.start("p_down", r.g_down, r.p_down)
    local.row("cot", r.cotangent, r.cot)
    local.start("down", r.w_down, r.down)
    peers.greet(reduces)
    local.start("slope", r.ffn_slope, r.slope)
    local.start("up", r.w_up, r.up)
    depth, blocks, cols = r.h.shape[1], r.h.shape[0] // RB, r.k_turned.shape[0]
    qkv, att = r.active.at[:, 0 : 3 * cols], r.active.at[:, 3 * cols : 4 * cols]
    dqkv, grad = r.slope.at[:, 0 : 3 * cols], r.slope.at[:, 3 * cols : 4 * cols]
    dk_sum, dv_sum = r.dkv.at[:, 0:cols], r.dkv.at[:, cols : 2 * cols]
    hidden = r.active.shape[1] // 2
    row_low, own_q, own_m, p_cross = r.n3, r.own_d, r.own_p, r.up
    steps = Steps(MIDDLE_PACE)
    swap_p = Swap(peers, r.own_p, r.other_p, r.s_send.at[0], r.s_recv.at[0])
    swap_d = Swap(peers, r.own_d, r.other_d, r.s_send.at[1], r.s_recv.at[1])
    swap_q = Swap(peers, own_q, r.dn_other, r.s_send.at[2], r.s_recv.at[2])
    swap_m = Swap(peers, own_m, r.other_m, r.s_send.at[3], r.s_recv.at[3])
    spread = Spread(peers, row_low, r.block_rows, r.y_send, r.y_recv, 1)
    works = []
    if reduces:
        split = split_rows(r.landing.shape[2], "zxy", "yzx", 0.34)
        works = [
            reduce_group(peers, split, p, r.landing.at[k], r.relay.at[k], r.r_send.at[k], r.r_recv.at[k])
            for k, p in enumerate((r.p_down, r.p_up))
        ]
        local.wait("p_down")
        works[0].start()
        works[0].add_to(steps, "down")
    r.norm_sums[...] = jnp.zeros_like(r.norm_sums)
    local.wait("cot", "down", "slope", "up")
    local.start("n3", r.normed_three, r.n3)
    local.start("active", r.ffn_active, r.active)
    local.start("h", r.hidden_two, r.h)
    wide = 2 * RB

    @pl.loop(0, blocks // 2)
    def _(i):
        rows = block(i, wide)
        total = None
        for t in range(2):
            half = slice(t * hidden, (t + 1) * hidden)
            up, down = r.up[t].reshape(depth, hidden), r.down[t].reshape(depth, hidden)
            du = (nn(r.cot[rows, :], down) * r.slope[rows, half].astype(F32)).astype(BF)
            r.slope[rows, half] = du
            one = nt(du, up)
            total = one if total is None else total + one
        r.own_d[rows, :] = total.astype(BF)
        swap_d.start(2 * i)
        swap_d.start(2 * i + 1)

    local.start("raw", r.w_cross, r.up)
    steps.spend(6.0)
    local.wait("n3", "active")
    for t in range(2):
        gradient(r.n3[...], r.slope[:, t * hidden : (t + 1) * hidden], store_into(r.p_up, t))
        steps.spend(1.5)
    if reduces:
        works[1].start()
        works[1].add_to(steps, "up")
    else:
        local.start("p_up", r.p_up, r.out_up)

    @pl.loop(0, blocks // 2)
    def _(i):
        rows = block(i, wide)
        total = nt(r.active[rows, 0:hidden], r.down[0].reshape(depth, hidden))
        total += nt(r.active[rows, hidden : 2 * hidden], r.down[1].reshape(depth, hidden))
        r.own_p[rows, :] = total.astype(BF)
        swap_p.start(2 * i)
        swap_p.start(2 * i + 1)

    local.start("qkv", r.qkv_two, qkv)
    local.start("att", r.att_two, att)
    local.start("n", r.normed_two, r.n_in)
    local.row("mem", r.memory, r.mem)
    steps.spend(3.0)
    local.wait("raw", "h")
    join_groups(r.up, r.wj)
    for i in range(blocks):
        swap_d.arrived(i)
        upstream = r.own_d[block(i), :].astype(F32) + r.other_d[block(i), :].astype(F32)
        e = back_in(upstream, r.h[block(i), :].astype(F32), r.norms[2:3, :], r.cot[block(i), :].astype(F32), r.norm_sums)
        r.low[block(i), :] = e.astype(BF)
        grad[block(i), :] = nn(e.astype(BF), r.wj[:, 3 * cols : 4 * cols]).astype(BF)
    local.start("e", r.low, r.residual)
    steps.spend(5.0)
    for i in range(blocks):
        swap_p.arrived(i)
        row = r.h[block(i), :].astype(F32) + (r.own_p[block(i), :].astype(F32) + r.other_p[block(i), :].astype(F32))
        row_low[block(i), :] = row.astype(BF)
    local.own_row("row", row_low, r.block_rows)
    spread.start(0)
    local.wait("qkv", "att", "n", "mem")
    swap_d.drain()

    def after(i):
        own_q[block(i), :] = nt(dqkv[block(i), 0:cols], r.wj[:, 0:cols]).astype(BF)
        swap_q.start(i)
        steps.spend(0.4)

    gradient(r.low[...], att[...], store_joined(p_cross, 3))
    steps.spend(3.0)
    attend_back(
        qkv, att, grad, r.lse_two, partial(cross_bias_turned, r.q_ids, r.m_ids), False, dqkv, dk_sum, dv_sum,
        r.k_turned, r.bias, steps.spend, after,
    )
    spread.pass_on(0)
    swap_p.drain()
    for i in range(blocks):
        own_m[block(i), :] = nt(dqkv[block(i), cols : 3 * cols], r.wj[:, cols : 3 * cols]).astype(BF)
        swap_m.start(i)
    steps.spend(2.0)
    gradient(r.n_in[...], dqkv[:, 0:cols], store_joined(p_cross, 0))
    gradient(r.mem[...], dqkv[:, cols : 3 * cols], store_joined(p_cross, 1))
    local.start("p_cross", p_cross, r.out_cross)
    local.start("own_q", own_q, r.dn_own)
    local.wait("e")
    for i in range(blocks):
        swap_m.arrived(i)
        r.low[block(i), :] = (own_m[block(i), :].astype(F32) + r.other_m[block(i), :].astype(F32)).astype(BF)
    local.start("mem_row", r.low, r.mem_own)
    for i in range(blocks):
        swap_q.arrived(i)
    steps.drain()
    if reduces:
        for k, out in enumerate((r.red_down, r.red_up)):
            out[...] = works[k].finish()
    spread.finish()
    for swap in (swap_q, swap_m):
        swap.drain()
    local.drain()


def last_kernel(nz, reduces, tensor_size, r):
    peers = Peers(nz)
    local = Local(r.local)
    if reduces:
        local.start("p_cross", r.g_cross, r.p_cross)
    local.start("raw", r.w_self, r.raw)
    local.start("e", r.residual, r.e_in)
    local.start("own_d", r.dn_own, r.own_d)
    local.start("other_d", r.dn_other, r.other_d)
    local.start("h", r.hidden_one, r.h)
    peers.greet(reduces, cube=reduces)
    blocks, cols = r.h.shape[0] // RB, r.att.shape[1]
    steps = Steps(LAST_PACE)
    swap_q = Swap(peers, r.own_q, r.other_q, r.s_send.at[0], r.s_recv.at[0])
    spread_m = Spread(peers, r.mem_low, r.mem_rows, r.y_send.at[0], r.y_recv.at[0], 1)
    spread_t = Spread(peers, r.row_low, r.target_rows, r.y_send.at[1], r.y_recv.at[1], 2)
    works = []
    if reduces:
        split = split_rows(r.landing.shape[2], "zxy", "yzx", 0.17)
        works = [
            reduce_group(peers, split, p, r.landing.at[k], r.relay.at[k], r.r_send.at[k], r.r_recv.at[k])
            for k, p in enumerate((r.p_cross, r.p_self))
        ]
        local.wait("p_cross")
        works[0].start()
        works[0].add_to(steps, "cross")
    r.norm_sums[...] = jnp.zeros_like(r.norm_sums)
    local.wait("raw")
    join_groups(r.raw, r.wj)
    local.wait("e", "own_d", "other_d", "h")
    local.start("mem", r.mem_own, r.mem_low)
    local.start("qkv", r.qkv_one, r.qkv)
    local.start("att", r.att_one, r.att)
    local.start("n", r.normed_one, r.n_in)
    local.row("x", r.target, r.x)
    for i in range(blocks):
        upstream = r.own_d[block(i), :].astype(F32) + r.other_d[block(i), :].astype(F32)
        e = back_in(upstream, r.h[block(i), :].astype(F32), r.norms[1:2, :], r.e_in[block(i), :].astype(F32), r.norm_sums)
        r.e[block(i), :] = e
        r.low[block(i), :] = e.astype(BF)
        r.grad[block(i), :] = nn(e.astype(BF), r.wj[:, 3 * cols : 4 * cols]).astype(BF)
    local.wait("mem")
    local.own_row("mem_own", r.mem_low, r.mem_rows)
    spread_m.start(0)
    steps.spend(6.0)
    local.wait("qkv", "att", "n", "x")
    gradient(r.low[...], r.att[...], store_joined(r.p_self, 3))
    steps.spend(1.0)

    def after(i):
        r.own_q[block(i), :] = nt(r.dqkv[block(i), :], r.wj[:, 0 : 3 * cols]).astype(BF)
        swap_q.start(i)
        steps.spend(0.8)

    attend_back(
        r.qkv, r.att, r.grad, r.lse_one, partial(self_bias_turned, r.q_ids, r.k_ids), True, r.dqkv, r.dk_sum, r.dv_sum,
        r.k_turned, r.bias, steps.spend, after,
    )
    gradient(r.n_in[...], r.dqkv[...], store_joined(r.p_self, 0))
    steps.drain()
    if reduces:
        works[1].start()
        works[1].add_to(steps, "self")
    else:
        local.start("p_self", r.p_self, r.out_self)
    spread_m.pass_on(0)
    r.first_sums[...] = jnp.zeros_like(r.first_sums)
    for i in range(blocks):
        swap_q.arrived(i)
        upstream = r.own_q[block(i), :].astype(F32) + r.other_q[block(i), :].astype(F32)
        row = back_in(upstream, r.x[block(i), :].astype(F32), r.norms[0:1, :], r.e[block(i), :], r.first_sums)
        r.row_low[block(i), :] = row.astype(BF)
        if i % 2 == 1:
            pl.when(peers.tb == i // 2)(spread_t.start_all)
    local.own_row("row", r.row_low, r.target_rows)
    if reduces:
        depth, span = r.x.shape[1], r.x.shape[1] // (2 * nz)
        sums = jnp.concatenate(
            [r.first_sums[0:1], r.norm_sums[0:1], r.third_sums[0:1], r.first_sums[1:2], r.norm_sums[1:2]]
            + [r.third_sums[1:2], jnp.zeros((10, depth), F32)]
        ).astype(BF)
        feature = lax.broadcasted_iota(jnp.int32, (r.p_norm.shape[2], depth), 1)
        lane = lax.broadcasted_iota(jnp.int32, (r.p_norm.shape[2], depth), 0)
        for d in range(2 * nz):
            piece = nt(sums, ((feature == lane + d * span) & (lane < span)).astype(BF)).astype(BF)
            r.p_norm[d] = piece

        def norm_copy(place, peer):
            index = place[0] * 4 + place[1] * 2 + place[2]
            return pltpu.make_async_remote_copy(
                src_ref=r.p_norm.at[peer["dp"]], dst_ref=r.n_landing.at[index], send_sem=r.n_send.at[index],
                recv_sem=r.n_recv.at[index], device_id=peer, device_id_type=MESH_ID,
            )

        for place, peer in peers.box_peers():
            norm_copy(place, peer).start()
        steps.drain()
        norm_grad = r.p_norm[peers.z * 2 + peers.x].astype(F32)
        for place, peer in peers.box_peers():
            norm_copy(place, peer).wait_recv()
            norm_grad = norm_grad + r.n_landing[place[0] * 4 + place[1] * 2 + place[2]].astype(F32)
        r.red_norm[...] = norm_grad
        squares = jnp.sum(jnp.sum(norm_grad * norm_grad, -1, keepdims=True), 0, keepdims=True) / tensor_size
        for k, out in enumerate((r.red_cross, r.red_self)):
            total = works[k].finish()
            out[...] = total
            squares = squares + jnp.sum(jnp.sum(total * total, -1, keepdims=True), 0, keepdims=True)
        for place, peer in peers.box_peers():
            norm_copy(place, peer).wait_send()
        for done in (r.red_up, r.red_down):
            squares = squares + jnp.sum(jnp.sum(done[...] * done[...], -1, keepdims=True), 0, keepdims=True)
        r.squares[...] = sum_everywhere(peers, squares, r.heard, r.q_send, r.q_recv)
    for i in range(2):
        spread_t.pass_on(i)
    spread_m.finish()
    spread_t.finish()
    swap_q.drain()
    local.drain()


def sum_everywhere(peers, value, heard, send, recv):
    nz = peers.nz

    def copy(step, src, dst, peer):
        return pltpu.make_async_remote_copy(
            src_ref=heard.at[src], dst_ref=heard.at[dst], send_sem=send.at[step], recv_sem=recv.at[step],
            device_id=peer, device_id_type=MESH_ID,
        )

    heard[peers.z] = jnp.broadcast_to(value, heard.shape[1:])
    for j in range(1, nz):
        copy(j - 1, peers.z, peers.z, peers.z_peer(j)).start()
    for j in range(1, nz):
        copy(j - 1, peers.z, peers.down(j), peers.z_peer(j)).wait_recv()
    total = heard[0]
    for k in range(1, nz):
        total = total + heard[k]

    def place(bits):
        spots = ((peers.x, 4), (peers.ta, 2), (peers.tb, 1))
        return nz + sum((1 - v if bits & weight else v) * weight for v, weight in spots)

    heard[place(0)] = total
    for bits in range(1, 8):
        copy(nz - 2 + bits, place(0), place(0), peers.cube_peer(bits)).start()
    for bits in range(1, 8):
        copy(nz - 2 + bits, place(0), place(bits), peers.cube_peer(bits)).wait_recv()
    for j in range(1, nz):
        copy(j - 1, peers.z, peers.z, peers.z_peer(j)).wait_send()
    for bits in range(1, 8):
        copy(nz - 2 + bits, place(0), place(0), peers.cube_peer(bits)).wait_send()
    total = heard[nz]
    for k in range(1, 8):
        total = total + heard[nz + k]
    return total


def adam_update(weight, gradient, first, second, clip_factor, bias_one, bias_two, rate, decay):
    scaled = gradient * clip_factor
    first_new = BETA_ONE * first + (1.0 - BETA_ONE) * scaled
    second_new = BETA_TWO * second + (1.0 - BETA_TWO) * scaled * scaled
    first_hat = first_new / bias_one
    second_hat = second_new / bias_two
    weight_new = weight - rate * (first_hat / (jnp.sqrt(second_hat) + EPS_ADAM) + decay * weight)
    return weight_new, weight_new.astype(BF), first_new, second_new


RATES = (
    (RATE_MATRIX, DECAY_RATE),
    (RATE_OUTPUT, DECAY_RATE),
    (RATE_MATRIX, DECAY_RATE),
    (RATE_OUTPUT, DECAY_RATE),
    (RATE_MATRIX, DECAY_RATE),
    (RATE_MATRIX, DECAY_RATE),
    (RATE_NORMS, 0.0),
)


def shard_gradients(reduced, width):
    g_self, g_cross, g_up, g_down, g_norms = reduced
    cut = [
        [g[:, s * width : (s + 1) * width] for s in range(4)] for g in (g_self, g_cross)
    ]
    return (cut[0][:3], cut[0][3].T, cut[1][:3], cut[1][3].T, g_up, g_down.T, g_norms)


def adam_kernel(*refs):
    reduced, squares, biases = refs[:5], refs[5], refs[6]
    state, norm_out, outs = refs[7:28], refs[28], refs[29:]
    width = state[3].shape[0]
    norm = jnp.sqrt(squares[...])
    norm_out[...] = norm
    clip = (CLIP_LIMIT / jnp.maximum(norm, CLIP_LIMIT))[0:1, 0:1]
    values = [r[...] for r in reduced]
    shape = state[18].shape
    values[4] = values[4][0 : shape[0], 0 : shape[1]]
    gradients = list(shard_gradients(values, width))
    gradients[5] = values[3]
    for k, (rate, decay) in enumerate(RATES):
        weight, first, second = state[3 * k : 3 * k + 3]
        into = outs[4 * k : 4 * k + 4]
        if isinstance(gradients[k], list):
            for s in range(3):
                new = adam_update(
                    weight[s], gradients[k][s], first[s], second[s], clip, biases[0], biases[1], rate, decay
                )
                for ref, value in zip(into, new):
                    ref[s] = value
        else:
            new = adam_update(
                weight[...], gradients[k], first[...], second[...], clip, biases[0], biases[1], rate, decay
            )
            for ref, value in zip(into, new):
                ref[...] = value


def widen_kernel(*refs):
    count = len(refs) // 2
    for src, dst in zip(refs[:count], refs[count:]):
        dst[...] = src[...].astype(F32)


def widen(*arrays):
    rows, depth = arrays[0].shape
    spec = pl.BlockSpec((RB, depth), lambda i: (i, 0))
    return pl.pallas_call(
        widen_kernel,
        name="widen",
        out_shape=[sds(a.shape, F32) for a in arrays],
        grid=(rows // RB,),
        in_specs=[spec] * len(arrays),
        out_specs=[spec] * len(arrays),
        compiler_params=params(),
    )(*arrays)


def body(target, memory, cotangent, tgt_seg, mem_seg, pad_len, step_count, *state):
    dp_size, tensor_size = lax.axis_size("dp"), lax.axis_size("ta") * lax.axis_size("tb")
    ta = lax.axis_index("ta")
    self_in, self_out, cross_in, cross_out, ffn_in, ffn_out, norm_params = state[::3]
    length, depth = tgt_seg.shape[1], target.shape[1]
    mem_length = mem_seg.shape[1]
    width, span = self_out.shape
    cols, hidden = 2 * width, ffn_in.shape[1]
    fold = depth // 8
    own_transfers = dp_size == 8
    nz = dp_size // 2 if own_transfers else 1
    blocks = length // RB

    tgt_ids = lax.dynamic_slice_in_dim(tgt_seg, ta, 1)
    mem_ids = lax.dynamic_slice_in_dim(mem_seg, ta, 1)
    pad = lax.dynamic_slice_in_dim(pad_len, ta, 1)
    key_ids = jnp.where(jnp.arange(length)[None, :] < length - pad[:, None], tgt_ids, -1)
    tgt_col, mem_col, key_col = tgt_ids.reshape(length, 1), mem_ids.reshape(mem_length, 1), key_ids.reshape(length, 1)

    row, mem_row = (length, depth), (mem_length, depth)
    qkv, att, logsum = (length, 3 * cols), (length, cols), (cols // 128, 2, length)
    pack = (2, 8, fold, 4 * width)
    wide = (2, 8, fold, hidden)
    joined = (depth, 4 * cols)
    dma = pltpu.SemaphoreType.DMA

    def v(shape, dtype=BF):
        return pltpu.VMEM(shape, dtype)

    ins = dict(
        target=(target, 0), memory=(memory, 0), cotangent=(cotangent, 0), q_ids=(tgt_col, 1), k_ids=(key_ids, 1), m_ids=(mem_ids, 1)
    )
    outs = dict(
        hidden_one=(row, BF, 0), hidden_two=(row, BF, 0), normed_one=(row, BF, 0), normed_two=(row, BF, 0),
        qkv_one=(qkv, BF, 0), qkv_two=(qkv, BF, 0), att_one=(att, BF, 0), att_two=(att, BF, 0),
        lse_one=(logsum, F32, 1), lse_two=(logsum, F32, 1), normed_three=(row, BF, 0),
        ffn_active=((length, 2 * hidden), BF, 0), ffn_slope=((length, 2 * hidden), BF, 0), g_down=(wide, BF, 0),
    )
    scratch = dict(
        cot=v(row), n_c=v(row), active=v((length, 2 * hidden)), slope=v((length, 2 * hidden)), p_down=v(wide),
        x=v(row), mem=v(mem_row), raw=v(pack), wj_a=v(joined), wj_b=v(joined), n_a=v(row), n_b=v(row),
        qkv_a=v(qkv), qkv_b=v(qkv), att_a=v(att), att_b=v(att), h_a=v(row, F32), l_a=v(row), l_b=v(row),
        own_a=v(row), other_a=v(row), own_b=v(row), other_b=v(row), bias=v((2 * RB, max(length, mem_length)), F32),
        s_send=dma((2, blocks)), s_recv=dma((2, blocks)), local=dma((24,)),
    )
    if own_transfers:
        ins |= dict(
            m_self_in=(self_in, 1), m_self_out=(self_out, 1), m_cross_in=(cross_in, 1), m_cross_out=(cross_out, 1),
            m_up=(ffn_in, 1), m_down=(ffn_out.T, 1), m_norm=(norm_params, 1),
        )
        outs |= dict(
            w_self=(pack, BF, 0), w_cross=(pack, BF, 0), w_up=(wide, BF, 0), w_down=(wide, BF, 0),
            norms=((16, depth), F32, 1),
        )
        scratch |= dict(
            stage=v((4, fold, 4 * width)), n_all=v((dp_size, 16, 128)), g_send=dma((4, 2, SLOTS)),
            g_recv=dma((4, 2, SLOTS)), n_send=dma((dp_size,)), n_recv=dma((dp_size,)),
        )
    else:
        norm_shard = jnp.zeros((16, span), BF).at[: norm_params.shape[0]].set(norm_params.astype(BF))
        shards = [
            jnp.concatenate([w_in[0], w_in[1], w_in[2], w_out.T], axis=1).astype(BF)
            for w_in, w_out in ((self_in, self_out), (cross_in, cross_out))
        ]
        shards += [ffn_in.astype(BF), ffn_out.T.astype(BF)]
        gathered = [
            lax.all_gather(lax.all_gather(s, "dp", axis=0, tiled=True), "ta", axis=0).reshape(2, 8, fold, s.shape[1])
            for s in shards
        ]
        norms = lax.all_gather(norm_shard, "dp", axis=1, tiled=True).astype(F32)
        ins |= dict(zip(("w_self", "w_cross", "w_up", "w_down"), ((g, 0) for g in gathered))) | dict(norms=(norms, 1))
    f = launch(
        partial(forward_kernel, nz, own_transfers), "forward", ins, outs, scratch, length * depth * 8 * cols,
        collective_id=0, has_side_effects=True,
    )
    if own_transfers:
        w_self, w_cross, w_up, w_down, norms = f.w_self, f.w_cross, f.w_up, f.w_down, f.norms
    else:
        w_self, w_cross, w_up, w_down = gathered

    ins = dict(
        hidden_two=(f.hidden_two, 0), cotangent=(cotangent, 0), w_up=(w_up, 0), w_down=(w_down, 0),
        w_cross=(w_cross, 0), qkv_two=(f.qkv_two, 0), att_two=(f.att_two, 0), normed_two=(f.normed_two, 0),
        memory=(memory, 0), lse_two=(f.lse_two, 1), norms=(norms, 1), q_ids=(tgt_ids, 1), m_ids=(mem_col, 1),
        normed_three=(f.normed_three, 0), ffn_active=(f.ffn_active, 0), ffn_slope=(f.ffn_slope, 0),
    )
    outs = dict(
        residual=(row, BF, 0), dn_own=(row, BF, 0), dn_other=(row, BF, 0),
        block_rows=((2 * length, depth), BF, 0), mem_own=(mem_row, BF, 0), out_cross=(pack, BF, 0), norm_sums=((8, depth), F32, 1),
    )
    back = dict(
        wj=v(joined), low=v(row), n_in=v(row), h=v(row),
        own_d=v(row), other_d=v(row), local=dma((24,)), y_send=dma((2, 2, 2)), y_recv=dma((2, 2, 2)),
    )
    sums_m = dict(dkv=v((mem_length, 2 * cols), F32), bias=v((mem_length, RB), F32), k_turned=v((cols, mem_length)))
    sums_s = dict(
        dk_sum=v((length, cols), F32), dv_sum=v((length, cols), F32), bias=v((length, RB), F32),
        k_turned=v((cols, length)),
    )
    reducing = dict(
        landing=v((2, SLOTS, fold, 4 * width)), relay=v((2, 2 * nz - 1, fold, 4 * width)), r_send=dma((2, 2, SLOTS)),
        r_recv=dma((2, 2, SLOTS)),
    )
    scratch = back | sums_m | dict(
        mem=v(mem_row), up=v(wide), down=v(wide), cot=v(row), n3=v(row), active=v((length, 2 * hidden)),
        slope=v((length, 2 * hidden)), own_p=v(row), other_p=v(row), other_m=v(mem_row),
        p_up=v(wide), p_down=v(wide), s_send=dma((4, blocks)), s_recv=dma((4, blocks)),
        y_send=dma((2, 1)), y_recv=dma((2, 1)),
    )
    if own_transfers:
        ins |= dict(g_down=(f.g_down, 0))
        outs |= dict(red_down=((span, hidden), F32, 1), red_up=((span, hidden), F32, 1))
        scratch |= reducing
    else:
        outs |= dict(out_up=(wide, BF, 0))
    m = launch(
        partial(middle_kernel, nz, own_transfers), "middle", ins, outs, scratch, length * depth * (12 * hidden),
        collective_id=1, has_side_effects=True,
    )

    ins = dict(
        residual=(m.residual, 0), dn_own=(m.dn_own, 0), dn_other=(m.dn_other, 0), hidden_one=(f.hidden_one, 0),
        w_self=(w_self, 0), qkv_one=(f.qkv_one, 0), att_one=(f.att_one, 0), normed_one=(f.normed_one, 0),
        target=(target, 0), mem_own=(m.mem_own, 0), lse_one=(f.lse_one, 1), norms=(norms, 1), q_ids=(tgt_ids, 1),
        k_ids=(key_col, 1), third_sums=(m.norm_sums, 1),
    )
    outs = dict(
        target_rows=((2 * length, depth), BF, 0), mem_rows=((2 * mem_length, depth), BF, 0),
        norm_sums=((8, depth), F32, 1), first_sums=((8, depth), F32, 1),
    )
    scratch = back | sums_s | dict(
        e_in=v(row), e=v(row, F32),        raw=v(pack), x=v(row), mem_low=v(mem_row), other_q=v(row), p_self=v(pack), s_send=dma((1, blocks)),
        s_recv=dma((1, blocks)), qkv=v(qkv), att=v(att), dqkv=v(qkv), grad=v(att), row_low=v(row), own_q=v(row),
    )
    if own_transfers:
        ins |= dict(g_cross=(m.out_cross, 0), red_up=(m.red_up, 1), red_down=(m.red_down, 1))
        shard = ((span, 4 * width), F32, 1)
        outs |= dict(red_cross=shard, red_self=shard, red_norm=((16, 128), F32, 1), squares=((8, 128), F32, 1))
        scratch |= reducing | dict(
            p_cross=v(pack), p_norm=v((dp_size, 16, 128)), n_landing=v((SLOTS, 16, 128)), n_send=dma((SLOTS,)),
            n_recv=dma((SLOTS,)), heard=v((nz + 8, 8, 128), F32), q_send=dma((nz + 6,)),
            q_recv=dma((nz + 6,)),
        )
    else:
        outs |= dict(out_self=(pack, BF, 0))
    b = launch(
        partial(last_kernel, nz, own_transfers, tensor_size), "last", ins, outs, scratch, length * depth * 16 * cols,
        collective_id=2, has_side_effects=True,
    )

    step_float = step_count.astype(F32)
    biases = jnp.stack([1.0 - jnp.power(BETA_ONE, step_float), 1.0 - jnp.power(BETA_TWO, step_float)])
    if own_transfers:
        turn = [a.T if 15 <= k < 18 else a for k, a in enumerate(state)]
        updated = pl.pallas_call(
            adam_kernel,
            name="adam",
            out_shape=[sds((8, 128), F32)]
            + [sds(w.shape, dt) for w in turn[::3] for dt in (F32, BF, F32, F32)],
            in_specs=vm(6) + [pl.BlockSpec(memory_space=pltpu.SMEM)] + vm(21),
            out_specs=vm(29),
            compiler_params=params(),
        )(b.red_self, b.red_cross, m.red_up, m.red_down, b.red_norm, b.squares, biases, *turn)
        global_norm, updated = updated[0][0, 0], list(updated[1:])
        updated[20:24] = [a.T for a in updated[20:24]]
    else:
        sums = (b.first_sums, b.norm_sums, m.norm_sums)
        all_sums = jnp.stack([s[k] for k in range(2) for s in sums]).astype(BF).astype(F32)
        norm_part = lax.psum_scatter(lax.psum(all_sums, "ta"), "dp", scatter_dimension=1, tiled=True)
        reduced = []
        for g in (b.out_self, m.out_cross, m.out_up, f.g_down):
            g = lax.psum_scatter(g.astype(F32), "ta", scatter_dimension=0).reshape(depth, g.shape[3])
            reduced.append(lax.psum_scatter(g, "dp", scatter_dimension=0, tiled=True))
        total = sum(jnp.sum(g * g) for g in reduced) + jnp.sum(norm_part * norm_part) / tensor_size
        global_norm = jnp.sqrt(lax.psum(total, ("dp", "ta", "tb")))
        clip = CLIP_LIMIT / jnp.maximum(global_norm, CLIP_LIMIT)
        updated = []
        for k, g in enumerate(shard_gradients(reduced + [norm_part], width)):
            g = jnp.stack(g) if isinstance(g, list) else g
            weight, first, second = state[3 * k : 3 * k + 3]
            updated += adam_update(weight, g, first, second, clip, biases[0], biases[1], *RATES[k])
    rows = widen(m.block_rows, b.target_rows, b.mem_rows)
    return (global_norm, *rows, *updated)


def solution(mesh):
    dp_size, tensor_size = mesh.shape["dp"], mesh.shape["tensor"]
    grid = Mesh(mesh.devices.reshape(dp_size, 2, tensor_size // 2), ("dp", "ta", "tb"))
    tensor = ("ta", "tb")
    rows = P("dp", None)
    place = (
        P(None, "dp", tensor),
        P(tensor, "dp"),
        P(None, "dp", tensor),
        P(tensor, "dp"),
        P("dp", tensor),
        P(tensor, "dp"),
        P(None, "dp"),
    )
    return jax.shard_map(
        body,
        mesh=grid,
        in_specs=(rows,) * 5 + (P("dp"), P()) + tuple(p for p in place for _ in range(3)),
        out_specs=(P(), rows, rows, rows) + tuple(p for p in place for _ in range(4)),
        check_vma=False,
    )
```

```python
from functools import partial
import math
from types import SimpleNamespace

import jax
import jax.numpy as jnp
from jax import lax
from jax.experimental import pallas as pl
from jax.experimental.pallas import tpu as pltpu
from jax.sharding import Mesh, PartitionSpec as P

HD = 64
EPS_NORM = 1e-05
NEG_FILL = -1000000000.0
BETA_ONE = 0.9
BETA_TWO = 0.999
EPS_ADAM = 1e-08
RATE_MATRIX = 0.05
RATE_OUTPUT = 0.25
RATE_NORMS = 0.75
DECAY_RATE = 0.1
CLIP_LIMIT = 1.0
GELU_COEF = 0.044715

BF = jnp.bfloat16
F32 = jnp.float32
RB = 256
FORWARD_PACE = 2.0
MIDDLE_PACE = 3.0
STRIDE = 5
LAST_PACE = 3.5
WINDOW = 4
FEED = 2
PW = 768
MESH_ID = pl.DeviceIdType.MESH
VMEM_LIMIT = 63 * 1024 * 1024


def nn(a, b):
    return lax.dot_general(a, b, (((1,), (0,)), ((), ())), preferred_element_type=F32)


def nt(a, b):
    return lax.dot_general(a, b, (((1,), (1,)), ((), ())), preferred_element_type=F32)


def tn(a, b):
    return lax.dot_general(a, b, (((0,), (0,)), ((), ())), preferred_element_type=F32)


def vm(n=1):
    return [pl.BlockSpec(memory_space=pltpu.VMEM)] * n


def anym(n=1):
    return [pl.BlockSpec(memory_space=pl.ANY)] * n


def sds(shape, dtype):
    return jax.ShapeDtypeStruct(shape, dtype)


def params(**kw):
    return pltpu.CompilerParams(vmem_limit_bytes=VMEM_LIMIT, **kw)


def block(i, size=RB):
    return pl.ds(pl.multiple_of(i * size, size), size)


def gelu_with_slope(values):
    root = math.sqrt(2.0 / math.pi)
    square = values * values
    tangent = jnp.tanh(values * (root + (root * GELU_COEF) * square))
    half = 0.5 + 0.5 * tangent
    output = values * half
    slope = half + 0.5 * output * (1.0 - tangent) * (2.0 * root + (6.0 * root * GELU_COEF) * square)
    return output, slope


def norm_stats(values):
    centre = values - jnp.mean(values, -1, keepdims=True)
    inverse = lax.rsqrt(jnp.mean(centre * centre, -1, keepdims=True) + EPS_NORM)
    return centre * inverse, inverse


def norm_forward(values, gain, shift):
    scaled, _ = norm_stats(values)
    return (scaled * gain + shift).astype(BF)


def norm_backward(upstream, values, gain):
    scaled, inverse = norm_stats(values)
    weighted = upstream * gain
    product = upstream * scaled
    result = inverse * (
        weighted
        - jnp.mean(weighted, -1, keepdims=True)
        - scaled * jnp.mean(weighted * scaled, -1, keepdims=True)
    )
    return result, jnp.sum(product, 0, keepdims=True), jnp.sum(upstream, 0, keepdims=True)


def launch(kernel, name, ins, outs, scratch, macs=0, **compiler):
    names = list(ins) + list(outs) + list(scratch)

    def run(*refs):
        kernel(SimpleNamespace(**dict(zip(names, refs))))

    results = pl.pallas_call(
        run,
        name=name,
        out_shape=[sds(shape, dtype) for shape, dtype, _ in outs.values()],
        in_specs=[pl.BlockSpec(memory_space=(pl.ANY, pltpu.VMEM, pltpu.SMEM)[where]) for _, where in ins.values()],
        out_specs=[(vm() if inside else anym())[0] for _, _, inside in outs.values()],
        scratch_shapes=list(scratch.values()),
        compiler_params=params(**compiler),
        cost_estimate=pl.CostEstimate(flops=2 * macs, bytes_accessed=20 << 20, transcendentals=0),
    )(*[a for a, _ in ins.values()])
    return SimpleNamespace(**dict(zip(outs, results)))


class Local:
    def __init__(self, sems):
        self.sems, self.count, self.open = sems, 0, {}

    def start(self, name, src, dst):
        copy = pltpu.make_async_copy(src, dst, self.sems.at[self.count])
        self.count += 1
        copy.start()
        self.open[name] = copy

    def row(self, name, src, dst):
        rows = dst.shape[0]
        start = pl.multiple_of(lax.axis_index("ta") * rows, rows)
        self.start(name, src.at[pl.ds(start, rows)], dst)

    def own_row(self, name, src, dst):
        rows = src.shape[0]
        start = pl.multiple_of(lax.axis_index("ta") * rows, rows)
        self.start(name, src, dst.at[pl.ds(start, rows)])

    def wait(self, *names):
        for name in names:
            self.open.pop(name).wait()

    def drain(self):
        self.wait(*list(self.open))


class Steps:
    def __init__(self, pace=0.0):
        self.todo, self.pace, self.credit = [], pace, 0.0

    def spend(self, cost):
        self.credit += cost
        while self.todo and self.credit >= self.pace:
            self.credit -= self.pace
            self.step()

    def add(self, name, fn, *args, **kwargs):
        self.todo.append((name, partial(fn, *args, **kwargs)))

    def step(self, count=1):
        for _ in range(min(count, len(self.todo))):
            self.todo.pop(0)[1]()

    def until(self, name):
        while any(n == name for n, _ in self.todo):
            self.step()

    def drain(self):
        self.step(len(self.todo))


def join_groups(packed, joined):
    rows, width = packed.shape[2], packed.shape[3] // 4

    @pl.loop(0, packed.shape[1])
    def _(i):
        first, second = packed[0, i], packed[1, i]
        pieces = []
        for s in range(4):
            pieces += [first[:, s * width : (s + 1) * width], second[:, s * width : (s + 1) * width]]
        joined[block(i, rows), :] = jnp.concatenate(pieces, axis=1)


def gradient(source, rhs, store):
    product = tn(source, rhs)
    rows = product.shape[0] // 8
    for d in range(8):
        store(d, product[d * rows : (d + 1) * rows])


def head_masks(rows):
    lane = lax.broadcasted_iota(jnp.int32, (rows, 2 * HD), 1)
    return lane < HD


def keep_half(values, low_half, head):
    zero = jnp.zeros_like(values)
    return jnp.where(low_half, values, zero) if head == 0 else jnp.where(low_half, zero, values)


def attend(qkv, bias_of, causal, out, logsum, bias, between, after):
    rows, cols = out.shape
    size = RB if causal else bias.shape[0]

    def one(start, keys, pair):
        q_rows = pl.ds(start, size)
        lanes = slice(pair * 2 * HD, (pair + 1) * 2 * HD)
        key = qkv[0:keys, cols + pair * 2 * HD : cols + (pair + 1) * 2 * HD]
        value = qkv[0:keys, 2 * cols + pair * 2 * HD : 2 * cols + (pair + 1) * 2 * HD]
        query = qkv[q_rows, lanes]
        low_half = head_masks(size)
        outs, sums = [], []
        for head in range(2):
            scores = nt(keep_half(query, low_half, head), key) + bias[0:size, 0:keys]
            peak = jnp.max(scores, -1, keepdims=True)
            shifted = jnp.exp(scores - peak)
            total = jnp.sum(shifted, -1, keepdims=True)
            outs.append(nn(shifted.astype(BF), value) / total)
            sums.append(peak + jnp.log(total))
        out[q_rows, lanes] = jnp.where(low_half, outs[0], outs[1]).astype(BF)
        both = jnp.where(low_half, sums[0], sums[1]).T
        logsum[pair, :, q_rows] = jnp.concatenate([both[0:1], both[HD : HD + 1]], axis=0)

    for i in range(rows // size):
        keys = (i + 1) * size if causal else bias.shape[1]
        bias[0:size, 0:keys] = bias_of(i, size, keys)
        for pair in range(cols // (2 * HD)):
            one(i * size, keys, pair)
            between(size * keys * 3.4e-6)
        for k in range(size // RB):
            after(i * (size // RB) + k)


def attend_back(qkv, attended, grad, logsum, bias_of, causal, dqkv, dk_sum, dv_sum, k_turned, bias, between, after):
    rows, cols = attended.shape
    dk_sum[...] = jnp.zeros(dk_sum.shape, F32)
    dv_sum[...] = jnp.zeros(dv_sum.shape, F32)

    @pl.loop(0, k_turned.shape[1] // RB)
    def _(i):
        k_turned[:, block(i)] = qkv[block(i), cols : 2 * cols].T

    def one(q_rows, keys, pair):
        lanes = slice(pair * 2 * HD, (pair + 1) * 2 * HD)
        k_lanes = slice(cols + pair * 2 * HD, cols + (pair + 1) * 2 * HD)
        v_lanes = slice(2 * cols + pair * 2 * HD, 2 * cols + (pair + 1) * 2 * HD)
        query, key, value = qkv[q_rows, lanes], qkv[0:keys, k_lanes], qkv[0:keys, v_lanes]
        out_grad = grad[q_rows, lanes]
        low_half = head_masks(RB)
        product = (out_grad.astype(F32) * attended[q_rows, lanes].astype(F32)).T
        dk = dv = None
        dq = []
        for head in range(2):
            inner = jnp.sum(product[head * HD : (head + 1) * HD], 0, keepdims=True)
            q_head = keep_half(query, low_half, head)
            g_head = keep_half(out_grad, low_half, head)
            scores = nt(key, q_head) + bias[0:keys, :]
            weights = jnp.exp(scores - logsum[pair, head : head + 1, q_rows])
            weight_grad = nt(value, g_head)
            score_grad = (weights * (weight_grad - inner)).astype(BF)
            dv_part = nn(weights.astype(BF), g_head)
            dk_part = nn(score_grad, q_head)
            turned_rows = slice(pair * 2 * HD + head * HD, pair * 2 * HD + (head + 1) * HD)
            dq.append(nn(k_turned[turned_rows, 0:keys], score_grad))
            dv = dv_part if dv is None else dv + dv_part
            dk = dk_part if dk is None else dk + dk_part
        dqkv[q_rows, lanes] = (jnp.concatenate(dq, axis=0).T * (1.0 / math.sqrt(HD))).astype(BF)
        dk_sum[0:keys, lanes] += dk
        dv_sum[0:keys, lanes] += dv

    def settle(key_rows):
        dqkv[key_rows, cols : 2 * cols] = dk_sum[key_rows, :].astype(BF)
        dqkv[key_rows, 2 * cols : 3 * cols] = dv_sum[key_rows, :].astype(BF)

    for i in reversed(range(rows // RB)):
        keys = (i + 1) * RB if causal else bias.shape[0]
        bias[0:keys, :] = bias_of(i, keys)
        for pair in range(cols // (2 * HD)):
            one(pl.ds(i * RB, RB), keys, pair)
            between(RB * keys * 5.4e-6)
        if causal:
            settle(pl.ds(i * RB, RB))
        after(i)
    if not causal:
        pl.loop(0, dk_sum.shape[0] // RB)(lambda i: settle(block(i)))


def id_rows(seg, pad_len=None):
    ids = seg[pl.ds(lax.axis_index("ta"), 1), :]
    if pad_len is not None:
        live = ids.shape[1] - pad_len[lax.axis_index("ta")]
        ids = jnp.where(lax.broadcasted_iota(jnp.int32, ids.shape, 1) < live, ids, -1)
    return ids, jnp.broadcast_to(ids.astype(F32), (128, ids.shape[1])).T[:, 0:1].astype(jnp.int32)


def self_bias(q_ids, k_ids, i, rows, keys):
    same = q_ids[i * rows : (i + 1) * rows, :] == k_ids[:, 0:keys]
    q_pos = i * rows + lax.broadcasted_iota(jnp.int32, (rows, keys), 0)
    k_pos = lax.broadcasted_iota(jnp.int32, (rows, keys), 1)
    allowed = (same & (k_pos < q_pos)) | (k_pos == q_pos)
    return jnp.where(allowed, 0.0, NEG_FILL)


def self_bias_turned(q_ids, k_ids, i, keys):
    same = k_ids[0:keys, :] == q_ids[:, i * RB : (i + 1) * RB]
    q_pos = i * RB + lax.broadcasted_iota(jnp.int32, (keys, RB), 1)
    k_pos = lax.broadcasted_iota(jnp.int32, (keys, RB), 0)
    allowed = (same & (k_pos < q_pos)) | (k_pos == q_pos)
    return jnp.where(allowed, 0.0, NEG_FILL)


def cross_bias(q_ids, k_ids, i, rows, keys):
    return jnp.where(q_ids[i * rows : (i + 1) * rows, :] == k_ids[:, 0:keys], 0.0, NEG_FILL)


def cross_bias_turned(q_ids, k_ids, i, keys):
    return jnp.where(k_ids[0:keys, :] == q_ids[:, i * RB : (i + 1) * RB], 0.0, NEG_FILL)


def places():
    dp, ta = lax.axis_index("dp"), lax.axis_index("ta")
    return lax.div(dp, 2), lax.rem(dp, 2), ta


class Peers:
    def __init__(self, nz):
        self.nz = nz
        self.z, self.x, self.ta = places()
        self.ox, self.ot = 1 - self.x, 1 - self.ta
        self.x_peer = {"dp": self.z * 2 + self.ox}
        self.y_peer = {"ta": self.ot}
        self.tb = lax.axis_index("tb")
        self.core_peer = {"tb": 1 - self.tb}

    def up(self, j):
        return lax.rem(self.z + j, self.nz)

    def down(self, j):
        return lax.rem(self.z + (self.nz - j), self.nz)

    def z_peer(self, j):
        return {"dp": self.up(j) * 2 + self.x}

    def cube_peer(self, bits):
        turn = [bits >> 2 & 1, bits >> 1 & 1, bits & 1]
        x, ta, tb = [1 - v if t else v for v, t in zip((self.x, self.ta, self.tb), turn)]
        return {"dp": self.z * 2 + x, "ta": ta, "tb": tb}

    def row_peers(self):
        places = [(j, k) for j in range(self.nz) for k in range(2)][1:]
        return [((j, k), {"dp": self.up(j) * 2 + (self.ox if k else self.x)}) for j, k in places]

    def box_peers(self):
        places = [(j, t, k) for j in range(self.nz) for t in range(2) for k in range(2)][1:]
        return [
            ((j, t, k), {"dp": self.up(j) * 2 + (self.ox if k else self.x), "ta": self.ot if t else self.ta})
            for j, t, k in places
        ]

    def greet(self, plane, cube=False):
        others = [self.core_peer] if plane else [self.core_peer, self.y_peer]
        if plane:
            others += [peer for _, peer in self.box_peers()]
        if cube:
            others += [self.cube_peer(bits) for bits in (3, 5, 7)]
        barrier = pltpu.get_barrier_semaphore()
        for other in others:
            pl.semaphore_signal(barrier, inc=1, device_id=other, device_id_type=MESH_ID)
        pl.semaphore_wait(barrier, len(others))


SLOTS = 16


class Route:
    def __init__(self, peers, order, rows):
        self.p, self.order, self.rows = peers, order, rows
        self.sizes = {"z": peers.nz, "y": 2, "x": 2}
        self.places = [(z, y, x) for z in range(peers.nz) for y in range(2) for x in range(2)]
        self.places.sort(key=lambda place: (self.last(place), self.at(place, self.order[0])))

    def at(self, place, axis):
        return place["zyx".index(axis)]

    def last(self, place):
        return max([0] + [i + 1 for i, axis in enumerate(self.order) if self.at(place, axis)])

    def moved(self, place, axis, k):
        return tuple(k if a == axis else self.at(place, a) for a in "zyx")

    def beyond(self, place):
        return [
            (axis, k, self.moved(place, axis, k))
            for axis in self.order[self.last(place) :]
            for k in range(1, self.sizes[axis])
        ]

    def peer(self, axis, k):
        return {"z": self.p.z_peer(k), "y": self.p.y_peer, "x": self.p.x_peer}[axis]

    def index(self, place):
        return place[0] * 4 + place[1] * 2 + place[2]

    def spot(self, place, down):
        p = self.p
        z = p.down(place[0]) if down else p.up(place[0])
        return (p.ot if place[1] else p.ta), z * 2 + (p.ox if place[2] else p.x)


class Gather(Route):
    def __init__(self, peers, order, rows, out, send, recv, own):
        super().__init__(peers, order, rows)
        self.out, self.send, self.recv, self.own = out, send, recv, own

    def copy(self, place, new, peer):
        slot = self.out.at[(*self.spot(place, True), self.rows)]
        return pltpu.make_async_remote_copy(
            src_ref=slot if any(place) else self.own.at[self.rows], dst_ref=slot, send_sem=self.send.at[self.index(new)],
            recv_sem=self.recv.at[self.index(new)], device_id=peer, device_id_type=MESH_ID,
        )

    def arrived(self, place):
        slot = self.out.at[(*self.spot(place, True), self.rows)]
        pltpu.make_async_remote_copy(
            src_ref=slot, dst_ref=slot, send_sem=self.send.at[self.index(place)],
            recv_sem=self.recv.at[self.index(place)], device_id=self.p.y_peer, device_id_type=MESH_ID,
        ).wait_recv()

    def pass_on(self, place):
        if any(place):
            self.arrived(place)
        for axis, k, new in self.beyond(place):
            self.copy(place, new, self.peer(axis, k)).start()

    def finish(self):
        for place in self.places:
            if self.last(place) == 3:
                self.arrived(place)

    def close(self):
        for place in self.places:
            for axis, k, new in self.beyond(place):
                self.copy(place, new, self.peer(axis, k)).wait_send()


class Reduce(Route):
    def __init__(self, peers, order, rows, part, landing, relay, send, recv):
        super().__init__(peers, order, rows)
        self.part, self.landing, self.relay, self.send, self.recv = part, landing, relay, send, recv
        self.relayed = sorted([place for place in self.places if 0 < self.last(place) < 3], key=self.last, reverse=True)
        order = self.relayed + [(0, 0, 0)]
        firsts = [place for place in self.places if self.last(place) == 3]
        self.queue = sorted(firsts, key=lambda place: order.index(self.moved(place, self.order[2], 0)))

    def copy(self, place):
        axis = self.order[self.last(place) - 1]
        if self.last(place) == 3:
            src = self.part.at[(*self.spot(place, False), self.rows)]
        else:
            src = self.relay.at[self.relayed.index(place), self.rows]
        return pltpu.make_async_remote_copy(
            src_ref=src, dst_ref=self.landing.at[self.index(place), self.rows], send_sem=self.send.at[self.index(place)],
            recv_sem=self.recv.at[self.index(place)], device_id=self.peer(axis, self.at(place, axis)),
            device_id_type=MESH_ID,
        )

    def total(self, place):
        t, d = self.spot(place, False)
        total = self.part[t, d, self.rows, :].astype(F32)
        for _, _, new in self.beyond(place):
            self.copy(new).wait_recv()
            total = total + self.landing[self.index(new), self.rows, :].astype(F32)
        return total

    def start(self):
        self.feed(WINDOW)

    def feed(self, count):
        for _ in range(min(count, len(self.queue))):
            self.copy(self.queue.pop(0)).start()

    def pass_on(self, place):
        self.relay[self.relayed.index(place), self.rows, :] = self.total(place).astype(self.relay.dtype)
        self.copy(place).start()
        self.feed(FEED)

    def finish(self):
        self.feed(len(self.queue))
        total = self.total((0, 0, 0))
        for place in self.places:
            if any(place):
                self.copy(place).wait_send()
        return total


class Group:
    def __init__(self, works):
        self.works = works

    def start(self):
        for w in self.works:
            if isinstance(w, Gather):
                w.pass_on((0, 0, 0))
            else:
                w.start()

    def stages(self):
        lists = []
        for w in self.works:
            places = w.relayed if isinstance(w, Reduce) else [p for p in w.places if 0 < w.last(p) < 3]
            lists.append([(w, p) for p in places])
        count = max(len(places) for places in lists)
        return [[places[i] for places in lists if i < len(places)] for i in range(count)]

    def add_to(self, steps, name, between=None, at=None):
        for i, stage in enumerate(self.stages()):
            if i == at:
                steps.add(name, between)
            steps.add(name, self.run, stage)

    def run(self, stage):
        for w, place in stage:
            w.pass_on(place)

    def finish(self):
        totals = [w.finish() for w in self.works]
        return totals[0] if len(totals) == 1 else jnp.concatenate(totals) if totals[0] is not None else None

    def close(self):
        for w in self.works:
            w.close()


def gather_group(peers, split, out, send, recv, own):
    rows, works = 0, []
    for k, (order, count) in enumerate(split):
        works.append(Gather(peers, order, pl.ds(rows, count), out, send.at[k], recv.at[k], own))
        rows += count
    return Group(works)


def reduce_group(peers, split, part, landing, relay, send, recv):
    rows, works = 0, []
    for k, (order, count) in enumerate(split):
        works.append(Reduce(peers, order, pl.ds(rows, count), part, landing, relay, send.at[k], recv.at[k]))
        rows += count
    return Group(works)


def split_rows(rows, first, second, share):
    count = max(16, int(rows * share) // 16 * 16)
    return ((first, count), (second, rows - count))


class Swap:
    def __init__(self, peers, src, dst, send, recv, rows=RB):
        self.peer, self.src, self.dst, self.send, self.recv, self.rows = peers.core_peer, src, dst, send, recv, rows

    def copy(self, i):
        rows = block(i, self.rows)
        return pltpu.make_async_remote_copy(
            src_ref=self.src.at[rows], dst_ref=self.dst.at[rows], send_sem=self.send.at[i], recv_sem=self.recv.at[i],
            device_id=self.peer, device_id_type=MESH_ID,
        )

    def start(self, i):
        self.copy(i).start()

    def arrived(self, i):
        self.copy(i).wait_recv()

    def drain(self):
        for i in range(self.src.shape[0] // self.rows):
            self.copy(i).wait_send()


class Spread:
    def __init__(self, peers, src, dst, send, recv, parts):
        self.p, self.src, self.dst, self.send, self.recv, self.parts = peers, src, dst, send, recv, parts
        self.size = src.shape[0] // (2 * parts)

    def rows(self, core, i, ta=None):
        start = (2 * i + core) * self.size
        start = start if ta is None else ta * self.src.shape[0] + start
        return pl.ds(pl.multiple_of(start, self.size), self.size)

    def copy(self, src, dst_ta, core, i, hop, peer):
        return pltpu.make_async_remote_copy(
            src_ref=src, dst_ref=self.dst.at[self.rows(core, i, dst_ta)], send_sem=self.send.at[hop, i],
            recv_sem=self.recv.at[hop, i], device_id=peer, device_id_type=MESH_ID,
        )

    def across(self, i):
        p = self.p
        return self.copy(self.src.at[self.rows(p.tb, i)], p.ta, p.tb, i, 0, p.y_peer)

    def beside(self, i):
        p = self.p
        return self.copy(self.dst.at[self.rows(p.tb, i, p.ot)], p.ot, p.tb, i, 1, p.core_peer)

    def start(self, i):
        self.across(i).start()

    def pass_on(self, i):
        p = self.p
        self.copy(self.src.at[self.rows(p.tb, i)], p.ot, p.tb, i, 0, p.y_peer).wait_recv()
        self.beside(i).start()

    def finish(self):
        p = self.p
        for i in range(self.parts):
            self.copy(self.src.at[self.rows(p.tb, i)], p.ot, 1 - p.tb, i, 1, p.core_peer).wait_recv()
            self.across(i).wait_send()
            self.beside(i).wait_send()


def pack_rows(w_in, w_out):
    return jnp.concatenate([w_in[0], w_in[1], w_in[2], w_out[...].T], axis=1).astype(BF)


def forward_kernel(nz, gathers, r):
    peers = Peers(nz)
    local = Local(r.local)
    local.row("x", r.target, r.x)
    local.row("mem", r.memory, r.mem)
    local.row("cot", r.cotangent, r.cot)
    peers.greet(gathers)
    steps = Steps(FORWARD_PACE)
    packs = (r.w_self, r.w_cross, r.w_up, r.w_down)
    if gathers:
        here = peers.ta, peers.z * 2 + peers.x
        split = split_rows(r.stage.shape[1], "zyx", "xzy", 0.67)
        works = [gather_group(peers, split, g, r.g_send.at[k], r.g_recv.at[k], r.stage.at[k]) for k, g in enumerate(packs)]
        mine = peers.z * 2 + peers.x
        r.n_all[mine] = jnp.zeros(r.n_all.shape[1:], BF)
        r.n_all[mine, 0 : r.m_norm.shape[0], 0 : r.m_norm.shape[1]] = r.m_norm[...].astype(BF)

        def norm_copy(place, slot, peer):
            index = place[0] * 2 + place[1]
            return pltpu.make_async_remote_copy(
                src_ref=r.n_all.at[slot], dst_ref=r.n_all.at[slot], send_sem=r.n_send.at[index],
                recv_sem=r.n_recv.at[index], device_id=peer, device_id_type=MESH_ID,
            )

        for place, peer in peers.row_peers():
            norm_copy(place, mine, peer).start()
        r.stage[0] = pack_rows(r.m_self_in, r.m_self_out)
        works[0].start()
        local.start("own0", r.stage.at[0], packs[0].at[here])
        r.stage[1] = pack_rows(r.m_cross_in, r.m_cross_out)
        r.stage[2] = r.m_up[...].astype(BF)
        r.stage[3] = r.m_down[...].astype(BF)
        for k in range(1, 4):
            local.start("own%d" % k, r.stage.at[k], packs[k].at[here])
        first = Steps()
        works[0].add_to(first, "self", works[1].start, 5)
        first.drain()
        finish = Steps()
        for work in works:
            finish.add("close", work.close)
        for place, peer in peers.row_peers():
            slot = peers.down(place[0]) * 2 + (peers.ox if place[1] else peers.x)
            norm_copy(place, slot, peer).wait_recv()
            finish.add("norm", norm_copy(place, mine, peer).wait_send)
        span = r.m_norm.shape[1]
        feature = lax.broadcasted_iota(jnp.int32, (r.n_all.shape[2], r.x.shape[1]), 1)
        lane = lax.broadcasted_iota(jnp.int32, (r.n_all.shape[2], r.x.shape[1]), 0)
        norms = jnp.zeros((r.n_all.shape[1], r.x.shape[1]), F32)
        for d in range(2 * nz):
            norms += nn(r.n_all[d], ((feature == lane + d * span) & (lane < span)).astype(BF))
        r.norms[...] = norms
        timed = []
        for k, name in ((1, "cross"), (2, "up"), (3, "down")):
            begin = (k - 1) * STRIDE
            if k < 3:
                timed.append((begin + STRIDE - 3.5, name, works[k + 1].start))
            for i, stage in enumerate(works[k].stages()):
                timed.append((begin + i, name, partial(works[k].run, stage)))
        for _, name, fn in sorted(timed, key=lambda item: item[0]):
            steps.add(name, fn)
    norm_ref = r.norms
    blocks = r.x.shape[0] // RB
    cols = r.att_a.shape[1]
    local.wait("x", "mem")
    q_col, k_row, m_row = id_rows(r.tgt_seg)[1], id_rows(r.tgt_seg, r.pad_len)[0], id_rows(r.mem_seg)[0]

    @pl.loop(0, blocks)
    def _(i):
        r.n_a[block(i), :] = norm_forward(r.x[block(i), :].astype(F32), norm_ref[0:1, :], norm_ref[3:4, :])

    local.start("n_a", r.n_a, r.normed_one)
    if gathers:
        works[0].finish()
        local.wait("own0")
    local.start("raw_a", packs[0], r.raw)
    steps.spend(2.0)
    local.wait("raw_a")
    join_groups(r.raw, r.wj_a)
    steps.spend(2.0)

    wide = 2 * RB

    def project(normed, weights, qkv, i):
        q = nn(normed[block(i, wide), :], weights[:, 0:cols]).astype(BF).astype(F32) * (1.0 / math.sqrt(HD))
        qkv[block(i, wide), 0:cols] = q.astype(BF)

    def project_rest(source, weights, qkv, i):
        qkv[block(i, wide), cols : 3 * cols] = nn(source[block(i, wide), :], weights[:, cols : 3 * cols]).astype(BF)

    for i in range(blocks // 2):
        project(r.n_a, r.wj_a, r.qkv_a, i)
        steps.spend(0.6)
        project_rest(r.n_a, r.wj_a, r.qkv_a, i)
        steps.spend(1.0)
    local.start("qkv_a", r.qkv_a, r.qkv_one)
    swap_a = Swap(peers, r.own_a, r.other_a, r.s_send.at[0], r.s_recv.at[0])
    swap_b = Swap(peers, r.own_b, r.other_b, r.s_send.at[1], r.s_recv.at[1])

    def out_of(att, weights, own, swap, i):
        own[block(i), :] = nt(att[block(i), :], weights[:, 3 * cols : 4 * cols]).astype(BF)
        swap.start(i)
        steps.spend(0.4)

    attend(
        r.qkv_a, partial(self_bias, q_col, k_row), True, r.att_a, r.lse_one, r.bias,
        steps.spend, partial(out_of, r.att_a, r.wj_a, r.own_a, swap_a),
    )
    local.start("att_a", r.att_a, r.att_one)
    steps.until("cross")
    if gathers:
        works[1].finish()
        local.wait("own1")
    local.start("raw_b", packs[1], r.raw)
    local.wait("raw_b")
    join_groups(r.raw, r.wj_b)
    steps.spend(2.0)
    for i in range(blocks // 2):
        project_rest(r.mem, r.wj_b, r.qkv_b, i)
        steps.spend(1.0)
    for i in range(blocks):
        swap_a.arrived(i)
        h = r.x[block(i), :].astype(F32) + (r.own_a[block(i), :].astype(F32) + r.other_a[block(i), :].astype(F32))
        r.h_a[block(i), :] = h
        r.l_a[block(i), :] = h.astype(BF)
        r.n_b[block(i), :] = norm_forward(h, norm_ref[1:2, :], norm_ref[4:5, :])
        if i % 2 == 1:
            project(r.n_b, r.wj_b, r.qkv_b, i // 2)
            steps.spend(2.2)
    local.start("h_a", r.l_a, r.hidden_one)
    local.start("n_b", r.n_b, r.normed_two)
    local.start("qkv_b", r.qkv_b, r.qkv_two)
    attend(
        r.qkv_b, partial(cross_bias, q_col, m_row), False, r.att_b, r.lse_two, r.bias,
        steps.spend, partial(out_of, r.att_b, r.wj_b, r.own_b, swap_b),
    )
    local.start("att_b", r.att_b, r.att_two)
    for i in range(blocks):
        swap_b.arrived(i)
        h = r.h_a[block(i), :] + (r.own_b[block(i), :].astype(F32) + r.other_b[block(i), :].astype(F32))
        r.l_b[block(i), :] = h.astype(BF)
        r.n_c[block(i), :] = norm_forward(h, norm_ref[2:3, :], norm_ref[5:6, :])
        steps.spend(0.7)
    local.start("h_b", r.l_b, r.hidden_two)
    local.start("n_c", r.n_c, r.normed_three)
    steps.until("up")
    if gathers:
        works[2].finish()
        local.wait("own2")
    local.start("up", packs[2], r.raw)
    local.wait("up", "cot")
    depth, hidden = r.x.shape[1], r.active.shape[1] // 2
    for t in range(2):
        half = slice(t * hidden, (t + 1) * hidden)
        for i in range(blocks // 2):
            rows = block(i, wide)
            activated, slope = gelu_with_slope(nn(r.n_c[rows, :], r.raw[t].reshape(depth, hidden)))
            r.active[rows, half] = activated.astype(BF)
            r.slope[rows, half] = slope.astype(BF)
            steps.spend(1.0)
        local.start("active%d" % t, r.active.at[:, half], r.ffn_active.at[:, half])
        local.start("slope%d" % t, r.slope.at[:, half], r.ffn_slope.at[:, half])
        gradient(r.cot[...], r.active[:, half], store_into(r.p_down, t))
        steps.spend(1.5)
    local.start("p_down", r.p_down, r.g_down)
    swap_a.drain()
    swap_b.drain()
    steps.drain()
    if gathers:
        works[3].finish()
        finish.drain()
    local.drain()


def store_into(pack, t):
    def store(d, values):
        pack[t, d] = values.astype(BF)

    return store


def back_in(upstream, values, gain, residual, sums):
    delta, gain_part, shift_part = norm_backward(upstream, values, gain)
    sums[0:1, :] += gain_part
    sums[1:2, :] += shift_part
    return residual + delta


def store_joined(pack, first):
    def store(d, values):
        width = pack.shape[3] // 4
        for s in range(values.shape[1] // (2 * width)):
            for t in range(2):
                piece = values[:, (2 * s + t) * width : (2 * s + t + 1) * width].astype(BF)
                pack[t, d, :, (first + s) * width : (first + s + 1) * width] = piece

    return store


def middle_kernel(nz, reduces, r):
    peers = Peers(nz)
    local = Local(r.local)
    if reduces:
        local.start("p_down", r.g_down, r.p_down)
    local.row("cot", r.cotangent, r.cot)
    local.start("down", r.w_down, r.down)
    peers.greet(reduces)
    local.start("slope", r.ffn_slope, r.slope)
    local.start("up", r.w_up, r.up)
    depth, blocks, cols = r.h.shape[1], r.h.shape[0] // RB, r.k_turned.shape[0]
    qkv, att = r.active.at[:, 0 : 3 * cols], r.active.at[:, 3 * cols : 4 * cols]
    dqkv, grad = r.slope.at[:, 0 : 3 * cols], r.slope.at[:, 3 * cols : 4 * cols]
    dk_sum, dv_sum = r.dkv.at[:, 0:cols], r.dkv.at[:, cols : 2 * cols]
    hidden = r.active.shape[1] // 2
    row_low, own_q, own_m, p_cross = r.n3, r.own_d, r.own_p, r.up
    steps = Steps(MIDDLE_PACE)
    swap_p = Swap(peers, r.own_p, r.other_p, r.s_send.at[0], r.s_recv.at[0])
    swap_d = Swap(peers, r.own_d, r.other_d, r.s_send.at[1], r.s_recv.at[1])
    swap_q = Swap(peers, own_q, r.dn_other, r.s_send.at[2], r.s_recv.at[2])
    swap_m = Swap(peers, own_m, r.other_m, r.s_send.at[3], r.s_recv.at[3])
    spread = Spread(peers, row_low, r.block_rows, r.y_send, r.y_recv, 1)
    works = []
    if reduces:
        split = split_rows(r.landing.shape[2], "zxy", "yzx", 0.5)
        works = [
            reduce_group(peers, split, p, r.landing.at[k], r.relay.at[k], r.r_send.at[k], r.r_recv.at[k])
            for k, p in enumerate((r.p_down, r.p_up))
        ]
        local.wait("p_down")
        works[0].start()
        works[0].add_to(steps, "down")
    r.norm_sums[...] = jnp.zeros_like(r.norm_sums)
    local.wait("cot", "down", "slope", "up")
    local.start("n3", r.normed_three, r.n3)
    local.start("active", r.ffn_active, r.active)
    local.start("h", r.hidden_two, r.h)
    wide = 2 * RB

    @pl.loop(0, blocks // 2)
    def _(i):
        rows = block(i, wide)
        total = None
        for t in range(2):
            half = slice(t * hidden, (t + 1) * hidden)
            up, down = r.up[t].reshape(depth, hidden), r.down[t].reshape(depth, hidden)
            du = (nn(r.cot[rows, :], down) * r.slope[rows, half].astype(F32)).astype(BF)
            r.slope[rows, half] = du
            one = nt(du, up)
            total = one if total is None else total + one
        r.own_d[rows, :] = total.astype(BF)
        swap_d.start(2 * i)
        swap_d.start(2 * i + 1)

    local.start("raw", r.w_cross, r.up)
    steps.spend(6.0)
    local.wait("n3", "active")
    for t in range(2):
        gradient(r.n3[...], r.slope[:, t * hidden : (t + 1) * hidden], store_into(r.p_up, t))
        steps.spend(1.5)
    if reduces:
        works[1].start()
        works[1].add_to(steps, "up")
    else:
        local.start("p_up", r.p_up, r.out_up)

    @pl.loop(0, blocks // 2)
    def _(i):
        rows = block(i, wide)
        total = nt(r.active[rows, 0:hidden], r.down[0].reshape(depth, hidden))
        total += nt(r.active[rows, hidden : 2 * hidden], r.down[1].reshape(depth, hidden))
        r.own_p[rows, :] = total.astype(BF)
        swap_p.start(2 * i)
        swap_p.start(2 * i + 1)

    local.start("qkv", r.qkv_two, qkv)
    local.start("att", r.att_two, att)
    local.start("n", r.normed_two, r.n_in)
    local.row("mem", r.memory, r.mem)
    steps.spend(3.0)
    local.wait("raw", "h")
    join_groups(r.up, r.wj)
    for i in range(blocks):
        swap_d.arrived(i)
        upstream = r.own_d[block(i), :].astype(F32) + r.other_d[block(i), :].astype(F32)
        e = back_in(upstream, r.h[block(i), :].astype(F32), r.norms[2:3, :], r.cot[block(i), :].astype(F32), r.norm_sums)
        r.low[block(i), :] = e.astype(BF)
        grad[block(i), :] = nn(e.astype(BF), r.wj[:, 3 * cols : 4 * cols]).astype(BF)
    local.start("e", r.low, r.residual)
    steps.spend(5.0)
    for i in range(blocks):
        swap_p.arrived(i)
        row = r.h[block(i), :].astype(F32) + (r.own_p[block(i), :].astype(F32) + r.other_p[block(i), :].astype(F32))
        row_low[block(i), :] = row.astype(BF)
    local.own_row("row", row_low, r.block_rows)
    spread.start(0)
    local.wait("qkv", "att", "n", "mem")
    swap_d.drain()

    def after(i):
        own_q[block(i), :] = nt(dqkv[block(i), 0:cols], r.wj[:, 0:cols]).astype(BF)
        swap_q.start(i)
        steps.spend(0.4)

    gradient(r.low[...], att[...], store_joined(p_cross, 3))
    steps.spend(3.0)
    attend_back(
        qkv, att, grad, r.lse_two, partial(cross_bias_turned, id_rows(r.tgt_seg)[0], id_rows(r.mem_seg)[1]), False, dqkv, dk_sum, dv_sum,
        r.k_turned, r.bias, steps.spend, after,
    )
    spread.pass_on(0)
    swap_p.drain()
    for i in range(blocks):
        own_m[block(i), :] = nt(dqkv[block(i), cols : 3 * cols], r.wj[:, cols : 3 * cols]).astype(BF)
        swap_m.start(i)
    steps.spend(2.0)
    gradient(r.n_in[...], dqkv[:, 0:cols], store_joined(p_cross, 0))
    gradient(r.mem[...], dqkv[:, cols : 3 * cols], store_joined(p_cross, 1))
    local.start("p_cross", p_cross, r.out_cross)
    local.start("own_q", own_q, r.dn_own)
    local.wait("e")
    for i in range(blocks):
        swap_m.arrived(i)
        r.low[block(i), :] = (own_m[block(i), :].astype(F32) + r.other_m[block(i), :].astype(F32)).astype(BF)
    local.start("mem_row", r.low, r.mem_own)
    for i in range(blocks):
        swap_q.arrived(i)
    steps.drain()
    if reduces:
        for k, out in enumerate((r.red_down, r.red_up)):
            out[...] = works[k].finish()
    spread.finish()
    for swap in (swap_q, swap_m):
        swap.drain()
    local.drain()


def last_kernel(nz, reduces, tensor_size, r):
    peers = Peers(nz)
    local = Local(r.local)
    if reduces:
        local.start("p_cross", r.g_cross, r.p_cross)
    local.start("raw", r.w_self, r.raw)
    local.start("e", r.residual, r.e_in)
    local.start("own_d", r.dn_own, r.own_d)
    local.start("other_d", r.dn_other, r.other_d)
    local.start("h", r.hidden_one, r.h)
    peers.greet(reduces, cube=reduces)
    blocks, cols = r.h.shape[0] // RB, r.att.shape[1]
    steps = Steps(LAST_PACE)
    swap_q = Swap(peers, r.own_q, r.other_q, r.s_send.at[0], r.s_recv.at[0])
    spread_m = Spread(peers, r.mem_low, r.mem_rows, r.y_send.at[0], r.y_recv.at[0], 1)
    spread_t = Spread(peers, r.row_low, r.target_rows, r.y_send.at[1], r.y_recv.at[1], blocks)
    works = []
    if reduces:
        split = split_rows(r.landing.shape[2], "zxy", "yzx", 0.17)
        even = split_rows(r.landing.shape[2], "zxy", "yzx", 0.17)
        works = [
            reduce_group(peers, split, p, r.landing.at[k], r.relay.at[k], r.r_send.at[k], r.r_recv.at[k])
            for k, (p, split) in enumerate(((r.p_cross, split), (r.p_self, even)))
        ]
        local.wait("p_cross")
        works[0].start()
        works[0].add_to(steps, "cross")
    r.norm_sums[...] = jnp.zeros_like(r.norm_sums)
    local.wait("raw")
    join_groups(r.raw, r.wj)
    local.wait("e", "own_d", "other_d", "h")
    local.start("mem", r.mem_own, r.mem_low)
    local.start("qkv", r.qkv_one, r.qkv)
    local.start("att", r.att_one, r.att)
    local.start("n", r.normed_one, r.n_in)
    local.row("x", r.target, r.x)
    for i in range(blocks):
        upstream = r.own_d[block(i), :].astype(F32) + r.other_d[block(i), :].astype(F32)
        e = back_in(upstream, r.h[block(i), :].astype(F32), r.norms[1:2, :], r.e_in[block(i), :].astype(F32), r.norm_sums)
        r.e[block(i), :] = e
        r.low[block(i), :] = e.astype(BF)
        r.grad[block(i), :] = nn(e.astype(BF), r.wj[:, 3 * cols : 4 * cols]).astype(BF)
    local.wait("mem")
    local.own_row("mem_own", r.mem_low, r.mem_rows)
    spread_m.start(0)
    steps.spend(6.0)
    local.wait("qkv", "att", "n", "x")
    gradient(r.low[...], r.att[...], store_joined(r.p_self, 3))
    steps.spend(1.0)

    r.first_sums[...] = jnp.zeros_like(r.first_sums)

    def settle(i):
        swap_q.arrived(i)
        upstream = r.own_q[block(i), :].astype(F32) + r.other_q[block(i), :].astype(F32)
        row = back_in(upstream, r.x[block(i), :].astype(F32), r.norms[0:1, :], r.e[block(i), :], r.first_sums)
        r.row_low[block(i), :] = row.astype(BF)
        spread_t.start(i)

    def after(i):
        r.own_q[block(i), :] = nt(r.dqkv[block(i), :], r.wj[:, 0 : 3 * cols]).astype(BF)
        swap_q.start(i)
        if i + 1 < blocks:
            settle(i + 1)
        steps.spend(1.5)

    attend_back(
        r.qkv, r.att, r.grad, r.lse_one, partial(self_bias_turned, id_rows(r.tgt_seg)[0], id_rows(r.tgt_seg, r.pad_len)[1]), True, r.dqkv, r.dk_sum, r.dv_sum,
        r.k_turned, r.bias, steps.spend, after,
    )
    gradient(r.n_in[...], r.dqkv[...], store_joined(r.p_self, 0))
    if reduces:
        works[1].start()
        works[1].add_to(steps, "self")
    else:
        local.start("p_self", r.p_self, r.out_self)
    settle(0)
    local.own_row("row", r.row_low, r.target_rows)
    if reduces:
        depth, span = r.x.shape[1], r.x.shape[1] // (2 * nz)
        sums = jnp.concatenate(
            [r.first_sums[0:1], r.norm_sums[0:1], r.third_sums[0:1], r.first_sums[1:2], r.norm_sums[1:2]]
            + [r.third_sums[1:2], jnp.zeros((10, depth), F32)]
        ).astype(BF)
        feature = lax.broadcasted_iota(jnp.int32, (r.p_norm.shape[2], depth), 1)
        lane = lax.broadcasted_iota(jnp.int32, (r.p_norm.shape[2], depth), 0)
        for d in range(2 * nz):
            piece = nt(sums, ((feature == lane + d * span) & (lane < span)).astype(BF)).astype(BF)
            r.p_norm[d] = piece

        def norm_copy(place, peer):
            index = place[0] * 4 + place[1] * 2 + place[2]
            return pltpu.make_async_remote_copy(
                src_ref=r.p_norm.at[peer["dp"]], dst_ref=r.n_landing.at[index], send_sem=r.n_send.at[index],
                recv_sem=r.n_recv.at[index], device_id=peer, device_id_type=MESH_ID,
            )

        for place, peer in peers.box_peers():
            norm_copy(place, peer).start()
        spread_m.pass_on(0)
        for i in reversed(range(1, blocks)):
            spread_t.pass_on(i)
        steps.drain()
        norm_grad = r.p_norm[peers.z * 2 + peers.x].astype(F32)
        for place, peer in peers.box_peers():
            norm_copy(place, peer).wait_recv()
            norm_grad = norm_grad + r.n_landing[place[0] * 4 + place[1] * 2 + place[2]].astype(F32)
        r.red_norm[...] = norm_grad
        squares = jnp.sum(jnp.sum(norm_grad * norm_grad, -1, keepdims=True), 0, keepdims=True) / tensor_size
        for k, out in enumerate((r.red_cross, r.red_self)):
            total = works[k].finish()
            out[...] = total
            squares = squares + jnp.sum(jnp.sum(total * total, -1, keepdims=True), 0, keepdims=True)
        for place, peer in peers.box_peers():
            norm_copy(place, peer).wait_send()
        for done in (r.red_up, r.red_down):
            squares = squares + jnp.sum(jnp.sum(done[...] * done[...], -1, keepdims=True), 0, keepdims=True)
        r.squares[...] = sum_everywhere(peers, squares, r.heard, r.q_send, r.q_recv)
    else:
        spread_m.pass_on(0)
        for i in reversed(range(1, blocks)):
            spread_t.pass_on(i)
    spread_t.pass_on(0)
    spread_m.finish()
    spread_t.finish()
    swap_q.drain()
    local.drain()


def sum_everywhere(peers, value, heard, send, recv):
    nz = peers.nz

    def copy(step, src, dst, peer):
        return pltpu.make_async_remote_copy(
            src_ref=heard.at[src], dst_ref=heard.at[dst], send_sem=send.at[step], recv_sem=recv.at[step],
            device_id=peer, device_id_type=MESH_ID,
        )

    heard[peers.z] = jnp.broadcast_to(value, heard.shape[1:])
    for j in range(1, nz):
        copy(j - 1, peers.z, peers.z, peers.z_peer(j)).start()
    for j in range(1, nz):
        copy(j - 1, peers.z, peers.down(j), peers.z_peer(j)).wait_recv()
    total = heard[0]
    for k in range(1, nz):
        total = total + heard[k]

    def place(bits):
        spots = ((peers.x, 4), (peers.ta, 2), (peers.tb, 1))
        return nz + sum((1 - v if bits & weight else v) * weight for v, weight in spots)

    heard[place(0)] = total
    for bits in range(1, 8):
        copy(nz - 2 + bits, place(0), place(0), peers.cube_peer(bits)).start()
    for bits in range(1, 8):
        copy(nz - 2 + bits, place(0), place(bits), peers.cube_peer(bits)).wait_recv()
    for j in range(1, nz):
        copy(j - 1, peers.z, peers.z, peers.z_peer(j)).wait_send()
    for bits in range(1, 8):
        copy(nz - 2 + bits, place(0), place(0), peers.cube_peer(bits)).wait_send()
    total = heard[nz]
    for k in range(1, 8):
        total = total + heard[nz + k]
    return total


def adam_update(weight, gradient, first, second, clip_factor, bias_one, bias_two, rate, decay):
    scaled = gradient * clip_factor
    first_new = BETA_ONE * first + (1.0 - BETA_ONE) * scaled
    second_new = BETA_TWO * second + (1.0 - BETA_TWO) * scaled * scaled
    first_hat = first_new / bias_one
    second_hat = second_new / bias_two
    weight_new = weight - rate * (first_hat / (jnp.sqrt(second_hat) + EPS_ADAM) + decay * weight)
    return weight_new, weight_new.astype(BF), first_new, second_new


RATES = (
    (RATE_MATRIX, DECAY_RATE),
    (RATE_OUTPUT, DECAY_RATE),
    (RATE_MATRIX, DECAY_RATE),
    (RATE_OUTPUT, DECAY_RATE),
    (RATE_MATRIX, DECAY_RATE),
    (RATE_MATRIX, DECAY_RATE),
    (RATE_NORMS, 0.0),
)


def shard_gradients(reduced, width):
    g_self, g_cross, g_up, g_down, g_norms = reduced
    cut = [
        [g[:, s * width : (s + 1) * width] for s in range(4)] for g in (g_self, g_cross)
    ]
    return (cut[0][:3], cut[0][3].T, cut[1][:3], cut[1][3].T, g_up, g_down.T, g_norms)


def adam_kernel(*refs):
    reduced, squares, biases = refs[:5], refs[5], refs[6]
    state, norm_out, outs = refs[7:28], refs[28], refs[29:]
    width = state[3].shape[0]
    norm = jnp.sqrt(squares[...])
    norm_out[...] = norm
    clip = (CLIP_LIMIT / jnp.maximum(norm, CLIP_LIMIT))[0:1, 0:1]
    values = [r[...] for r in reduced]
    shape = state[18].shape
    values[4] = values[4][0 : shape[0], 0 : shape[1]]
    gradients = list(shard_gradients(values, width))
    gradients[5] = values[3]
    for k, (rate, decay) in enumerate(RATES):
        weight, first, second = state[3 * k : 3 * k + 3]
        into = outs[4 * k : 4 * k + 4]
        if isinstance(gradients[k], list):
            for s in range(3):
                new = adam_update(
                    weight[s], gradients[k][s], first[s], second[s], clip, biases[0], biases[1], rate, decay
                )
                for ref, value in zip(into, new):
                    ref[s] = value
        else:
            new = adam_update(
                weight[...], gradients[k], first[...], second[...], clip, biases[0], biases[1], rate, decay
            )
            for ref, value in zip(into, new):
                ref[...] = value


def closing_kernel(count, *refs):
    ins, outs = refs[:31], refs[31:63]
    held, made, came, went = refs[63:90], refs[90:119], refs[119], refs[120]
    step = pl.program_id(0)
    sources = ins[3:9] + ins[10:]

    def bring(k):
        return pltpu.make_async_copy(sources[k], held[k], came.at[k])

    def put(k):
        return pltpu.make_async_copy(made[k], outs[3 + k], went.at[k])

    @pl.when(step == 0)
    def _():
        for k in range(len(held)):
            bring(k).start()

    @pl.when(step == 2)
    def _():
        for k in range(len(held)):
            bring(k).wait()
        adam_kernel(*held[:6], ins[9], *held[6:], *made)
        for k in range(len(made)):
            put(k).start()

    for src, dst in zip(ins[:3], outs[:3]):
        dst[...] = src[...].astype(F32)

    @pl.when(step == count - 1)
    def _():
        for k in range(len(made)):
            put(k).wait()


def closing(rows, reduced, squares, biases, state):
    count, depth = rows[0].shape
    spec = pl.BlockSpec((RB, depth), lambda i: (i, 0))
    out_shape = [sds((count, depth), F32)] * 3 + [sds((8, 128), F32)]
    out_shape += [sds(w.shape, dt) for w in state[::3] for dt in (F32, BF, F32, F32)]
    held = (*reduced, squares, *state)
    outs = pl.pallas_call(
        partial(closing_kernel, count // RB),
        name="closing",
        out_shape=out_shape,
        grid=(count // RB,),
        in_specs=[spec] * 3 + anym(6) + [pl.BlockSpec(memory_space=pltpu.SMEM)] + anym(21),
        out_specs=[spec] * 3 + anym(29),
        scratch_shapes=[pltpu.VMEM(a.shape, a.dtype) for a in (*held, *out_shape[3:])]
        + [pltpu.SemaphoreType.DMA((len(held),)), pltpu.SemaphoreType.DMA((29,))],
        compiler_params=params(),
    )(*rows, *reduced, squares, biases, *state)
    return outs[:3], outs[3][0, 0], list(outs[4:])


def body(target, memory, cotangent, tgt_seg, mem_seg, pad_len, step_count, *state):
    dp_size, tensor_size = lax.axis_size("dp"), lax.axis_size("ta") * lax.axis_size("tb")
    self_in, self_out, cross_in, cross_out, ffn_in, ffn_out, norm_params = state[::3]
    length, depth = tgt_seg.shape[1], target.shape[1]
    mem_length = mem_seg.shape[1]
    width, span = self_out.shape
    cols, hidden = 2 * width, ffn_in.shape[1]
    fold = depth // 8
    own_transfers = dp_size == 8
    nz = dp_size // 2 if own_transfers else 1
    blocks = length // RB

    row, mem_row = (length, depth), (mem_length, depth)
    qkv, att, logsum = (length, 3 * cols), (length, cols), (cols // 128, 2, length)
    pack = (2, 8, fold, 4 * width)
    wide = (2, 8, fold, hidden)
    joined = (depth, 4 * cols)
    dma = pltpu.SemaphoreType.DMA

    def v(shape, dtype=BF):
        return pltpu.VMEM(shape, dtype)

    ins = dict(
        target=(target, 0), memory=(memory, 0), cotangent=(cotangent, 0), tgt_seg=(tgt_seg, 1), mem_seg=(mem_seg, 1),
        pad_len=(pad_len, 2),
    )
    outs = dict(
        hidden_one=(row, BF, 0), hidden_two=(row, BF, 0), normed_one=(row, BF, 0), normed_two=(row, BF, 0),
        qkv_one=(qkv, BF, 0), qkv_two=(qkv, BF, 0), att_one=(att, BF, 0), att_two=(att, BF, 0),
        lse_one=(logsum, F32, 1), lse_two=(logsum, F32, 1), normed_three=(row, BF, 0),
        ffn_active=((length, 2 * hidden), BF, 0), ffn_slope=((length, 2 * hidden), BF, 0), g_down=(wide, BF, 0),
    )
    scratch = dict(
        cot=v(row), n_c=v(row), active=v((length, 2 * hidden)), slope=v((length, 2 * hidden)), p_down=v(wide),
        x=v(row), mem=v(mem_row), raw=v(pack), wj_a=v(joined), wj_b=v(joined), n_a=v(row), n_b=v(row),
        qkv_a=v(qkv), qkv_b=v(qkv), att_a=v(att), att_b=v(att), h_a=v(row, F32), l_a=v(row), l_b=v(row),
        own_a=v(row), other_a=v(row), own_b=v(row), other_b=v(row), bias=v((2 * RB, max(length, mem_length)), F32),
        s_send=dma((2, blocks)), s_recv=dma((2, blocks)), local=dma((24,)),
    )
    if own_transfers:
        ins |= dict(
            m_self_in=(self_in, 1), m_self_out=(self_out, 1), m_cross_in=(cross_in, 1), m_cross_out=(cross_out, 1),
            m_up=(ffn_in, 1), m_down=(ffn_out.T, 1), m_norm=(norm_params, 1),
        )
        outs |= dict(
            w_self=(pack, BF, 0), w_cross=(pack, BF, 0), w_up=(wide, BF, 0), w_down=(wide, BF, 0),
            norms=((16, depth), F32, 1),
        )
        scratch |= dict(
            stage=v((4, fold, 4 * width)), n_all=v((dp_size, 16, 128)), g_send=dma((4, 2, SLOTS)),
            g_recv=dma((4, 2, SLOTS)), n_send=dma((dp_size,)), n_recv=dma((dp_size,)),
        )
    else:
        norm_shard = jnp.zeros((16, span), BF).at[: norm_params.shape[0]].set(norm_params.astype(BF))
        shards = [
            jnp.concatenate([w_in[0], w_in[1], w_in[2], w_out.T], axis=1).astype(BF)
            for w_in, w_out in ((self_in, self_out), (cross_in, cross_out))
        ]
        shards += [ffn_in.astype(BF), ffn_out.T.astype(BF)]
        gathered = [
            lax.all_gather(lax.all_gather(s, "dp", axis=0, tiled=True), "ta", axis=0).reshape(2, 8, fold, s.shape[1])
            for s in shards
        ]
        norms = lax.all_gather(norm_shard, "dp", axis=1, tiled=True).astype(F32)
        ins |= dict(zip(("w_self", "w_cross", "w_up", "w_down"), ((g, 0) for g in gathered))) | dict(norms=(norms, 1))
    f = launch(
        partial(forward_kernel, nz, own_transfers), "forward", ins, outs, scratch, length * depth * 8 * cols,
        collective_id=0, has_side_effects=True,
    )
    if own_transfers:
        w_self, w_cross, w_up, w_down, norms = f.w_self, f.w_cross, f.w_up, f.w_down, f.norms
    else:
        w_self, w_cross, w_up, w_down = gathered

    ins = dict(
        hidden_two=(f.hidden_two, 0), cotangent=(cotangent, 0), w_up=(w_up, 0), w_down=(w_down, 0),
        w_cross=(w_cross, 0), qkv_two=(f.qkv_two, 0), att_two=(f.att_two, 0), normed_two=(f.normed_two, 0),
        memory=(memory, 0), lse_two=(f.lse_two, 1), norms=(norms, 1), tgt_seg=(tgt_seg, 1), mem_seg=(mem_seg, 1),
        normed_three=(f.normed_three, 0), ffn_active=(f.ffn_active, 0), ffn_slope=(f.ffn_slope, 0),
    )
    outs = dict(
        residual=(row, BF, 0), dn_own=(row, BF, 0), dn_other=(row, BF, 0),
        block_rows=((2 * length, depth), BF, 0), mem_own=(mem_row, BF, 0), out_cross=(pack, BF, 0), norm_sums=((8, depth), F32, 1),
    )
    back = dict(
        wj=v(joined), low=v(row), n_in=v(row), h=v(row),
        own_d=v(row), other_d=v(row), local=dma((24,)), y_send=dma((2, 2, blocks)), y_recv=dma((2, 2, blocks)),
    )
    sums_m = dict(dkv=v((mem_length, 2 * cols), F32), bias=v((mem_length, RB), F32), k_turned=v((cols, mem_length)))
    sums_s = dict(
        dk_sum=v((length, cols), F32), dv_sum=v((length, cols), F32), bias=v((length, RB), F32),
        k_turned=v((cols, length)),
    )
    reducing = dict(
        landing=v((2, SLOTS, fold, 4 * width)), relay=v((2, 2 * nz - 1, fold, 4 * width)), r_send=dma((2, 2, SLOTS)),
        r_recv=dma((2, 2, SLOTS)),
    )
    scratch = back | sums_m | dict(
        mem=v(mem_row), up=v(wide), down=v(wide), cot=v(row), n3=v(row), active=v((length, 2 * hidden)),
        slope=v((length, 2 * hidden)), own_p=v(row), other_p=v(row), other_m=v(mem_row),
        p_up=v(wide), p_down=v(wide), s_send=dma((4, blocks)), s_recv=dma((4, blocks)),
        y_send=dma((2, 1)), y_recv=dma((2, 1)),
    )
    if own_transfers:
        ins |= dict(g_down=(f.g_down, 0))
        outs |= dict(red_down=((span, hidden), F32, 1), red_up=((span, hidden), F32, 1))
        scratch |= reducing
    else:
        outs |= dict(out_up=(wide, BF, 0))
    m = launch(
        partial(middle_kernel, nz, own_transfers), "middle", ins, outs, scratch, length * depth * (12 * hidden),
        collective_id=1, has_side_effects=True,
    )

    ins = dict(
        residual=(m.residual, 0), dn_own=(m.dn_own, 0), dn_other=(m.dn_other, 0), hidden_one=(f.hidden_one, 0),
        w_self=(w_self, 0), qkv_one=(f.qkv_one, 0), att_one=(f.att_one, 0), normed_one=(f.normed_one, 0),
        target=(target, 0), mem_own=(m.mem_own, 0), lse_one=(f.lse_one, 1), norms=(norms, 1), tgt_seg=(tgt_seg, 1),
        pad_len=(pad_len, 2), third_sums=(m.norm_sums, 1),
    )
    outs = dict(
        target_rows=((2 * length, depth), BF, 0), mem_rows=((2 * mem_length, depth), BF, 0),
        norm_sums=((8, depth), F32, 1), first_sums=((8, depth), F32, 1),
    )
    scratch = back | sums_s | dict(
        e_in=v(row), e=v(row, F32),        raw=v(pack), x=v(row), mem_low=v(mem_row), other_q=v(row), p_self=v(pack), s_send=dma((1, blocks)),
        s_recv=dma((1, blocks)), qkv=v(qkv), att=v(att), dqkv=v(qkv), grad=v(att), row_low=v(row), own_q=v(row),
    )
    if own_transfers:
        ins |= dict(g_cross=(m.out_cross, 0), red_up=(m.red_up, 1), red_down=(m.red_down, 1))
        shard = ((span, 4 * width), F32, 1)
        outs |= dict(red_cross=shard, red_self=shard, red_norm=((16, 128), F32, 1), squares=((8, 128), F32, 1))
        scratch |= reducing | dict(
            p_cross=v(pack), p_norm=v((dp_size, 16, 128)), n_landing=v((SLOTS, 16, 128)), n_send=dma((SLOTS,)),
            n_recv=dma((SLOTS,)), heard=v((nz + 8, 8, 128), F32), q_send=dma((nz + 6,)),
            q_recv=dma((nz + 6,)),
        )
    else:
        outs |= dict(out_self=(pack, BF, 0))
    b = launch(
        partial(last_kernel, nz, own_transfers, tensor_size), "last", ins, outs, scratch, length * depth * 16 * cols,
        collective_id=2, has_side_effects=True,
    )

    step_float = step_count.astype(F32)
    biases = jnp.stack([1.0 - jnp.power(BETA_ONE, step_float), 1.0 - jnp.power(BETA_TWO, step_float)])
    if own_transfers:
        turn = [a.T if 15 <= k < 18 else a for k, a in enumerate(state)]
        rows, global_norm, updated = closing(
            (m.block_rows, b.target_rows, b.mem_rows),
            (b.red_self, b.red_cross, m.red_up, m.red_down, b.red_norm), b.squares, biases, turn,
        )
        updated[20:24] = [a.T for a in updated[20:24]]
    else:
        sums = (b.first_sums, b.norm_sums, m.norm_sums)
        all_sums = jnp.stack([s[k] for k in range(2) for s in sums]).astype(BF).astype(F32)
        norm_part = lax.psum_scatter(lax.psum(all_sums, "ta"), "dp", scatter_dimension=1, tiled=True)
        reduced = []
        for g in (b.out_self, m.out_cross, m.out_up, f.g_down):
            g = lax.psum_scatter(g.astype(F32), "ta", scatter_dimension=0).reshape(depth, g.shape[3])
            reduced.append(lax.psum_scatter(g, "dp", scatter_dimension=0, tiled=True))
        total = sum(jnp.sum(g * g) for g in reduced) + jnp.sum(norm_part * norm_part) / tensor_size
        global_norm = jnp.sqrt(lax.psum(total, ("dp", "ta", "tb")))
        clip = CLIP_LIMIT / jnp.maximum(global_norm, CLIP_LIMIT)
        updated = []
        for k, g in enumerate(shard_gradients(reduced + [norm_part], width)):
            g = jnp.stack(g) if isinstance(g, list) else g
            weight, first, second = state[3 * k : 3 * k + 3]
            updated += adam_update(weight, g, first, second, clip, biases[0], biases[1], *RATES[k])
        rows = [a.astype(F32) for a in (m.block_rows, b.target_rows, b.mem_rows)]
    return (global_norm, *rows, *updated)


def solution(mesh):
    dp_size, tensor_size = mesh.shape["dp"], mesh.shape["tensor"]
    grid = Mesh(mesh.devices.reshape(dp_size, 2, tensor_size // 2), ("dp", "ta", "tb"))
    tensor = ("ta", "tb")
    rows = P("dp", None)
    place = (
        P(None, "dp", tensor),
        P(tensor, "dp"),
        P(None, "dp", tensor),
        P(tensor, "dp"),
        P("dp", tensor),
        P(tensor, "dp"),
        P(None, "dp"),
    )
    return jax.shard_map(
        body,
        mesh=grid,
        in_specs=(rows,) * 5 + (P("dp"), P()) + tuple(p for p in place for _ in range(3)),
        out_specs=(P(), rows, rows, rows) + tuple(p for p in place for _ in range(4)),
        check_vma=False,
    )
```

```python
from functools import partial
import math
from types import SimpleNamespace

import jax
import jax.numpy as jnp
from jax import lax
from jax.experimental import pallas as pl
from jax.experimental.pallas import tpu as pltpu
from jax.sharding import Mesh, PartitionSpec as P

HD = 64
EPS_NORM = 1e-05
NEG_FILL = -1000000000.0
BETA_ONE = 0.9
BETA_TWO = 0.999
EPS_ADAM = 1e-08
RATE_MATRIX = 0.05
RATE_OUTPUT = 0.25
RATE_NORMS = 0.75
DECAY_RATE = 0.1
CLIP_LIMIT = 1.0
GELU_COEF = 0.044715

BF = jnp.bfloat16
F32 = jnp.float32
RB = 256
FORWARD_PACE = 2.0
MIDDLE_PACE = 3.0
STRIDE = 5
LAST_PACE = 3.5
WINDOW = 4
FEED = 2
PW = 768
MESH_ID = pl.DeviceIdType.MESH
VMEM_LIMIT = 63 * 1024 * 1024


def nn(a, b):
    return lax.dot_general(a, b, (((1,), (0,)), ((), ())), preferred_element_type=F32)


def nt(a, b):
    return lax.dot_general(a, b, (((1,), (1,)), ((), ())), preferred_element_type=F32)


def tn(a, b):
    return lax.dot_general(a, b, (((0,), (0,)), ((), ())), preferred_element_type=F32)


def vm(n=1):
    return [pl.BlockSpec(memory_space=pltpu.VMEM)] * n


def anym(n=1):
    return [pl.BlockSpec(memory_space=pl.ANY)] * n


def sds(shape, dtype):
    return jax.ShapeDtypeStruct(shape, dtype)


def params(**kw):
    return pltpu.CompilerParams(vmem_limit_bytes=VMEM_LIMIT, **kw)


def block(i, size=RB):
    return pl.ds(pl.multiple_of(i * size, size), size)


def gelu_with_slope(values):
    root = math.sqrt(2.0 / math.pi)
    square = values * values
    tangent = jnp.tanh(values * (root + (root * GELU_COEF) * square))
    half = 0.5 + 0.5 * tangent
    output = values * half
    slope = half + 0.5 * output * (1.0 - tangent) * (2.0 * root + (6.0 * root * GELU_COEF) * square)
    return output, slope


def norm_stats(values):
    centre = values - jnp.mean(values, -1, keepdims=True)
    inverse = lax.rsqrt(jnp.mean(centre * centre, -1, keepdims=True) + EPS_NORM)
    return centre * inverse, inverse


def norm_forward(values, gain, shift):
    scaled, _ = norm_stats(values)
    return (scaled * gain + shift).astype(BF)


def norm_backward(upstream, values, gain):
    scaled, inverse = norm_stats(values)
    weighted = upstream * gain
    product = upstream * scaled
    result = inverse * (
        weighted
        - jnp.mean(weighted, -1, keepdims=True)
        - scaled * jnp.mean(weighted * scaled, -1, keepdims=True)
    )
    return result, jnp.sum(product, 0, keepdims=True), jnp.sum(upstream, 0, keepdims=True)


def launch(kernel, name, ins, outs, scratch, macs=0, **compiler):
    names = list(ins) + list(outs) + list(scratch)

    def run(*refs):
        kernel(SimpleNamespace(**dict(zip(names, refs))))

    results = pl.pallas_call(
        run,
        name=name,
        out_shape=[sds(shape, dtype) for shape, dtype, _ in outs.values()],
        in_specs=[pl.BlockSpec(memory_space=(pl.ANY, pltpu.VMEM, pltpu.SMEM)[where]) for _, where in ins.values()],
        out_specs=[(vm() if inside else anym())[0] for _, _, inside in outs.values()],
        scratch_shapes=list(scratch.values()),
        compiler_params=params(**compiler),
        cost_estimate=pl.CostEstimate(flops=2 * macs, bytes_accessed=20 << 20, transcendentals=0),
    )(*[a for a, _ in ins.values()])
    return SimpleNamespace(**dict(zip(outs, results)))


class Local:
    def __init__(self, sems):
        self.sems, self.count, self.open = sems, 0, {}

    def start(self, name, src, dst):
        copy = pltpu.make_async_copy(src, dst, self.sems.at[self.count])
        self.count += 1
        copy.start()
        self.open[name] = copy

    def row(self, name, src, dst):
        rows = dst.shape[0]
        start = pl.multiple_of(lax.axis_index("ta") * rows, rows)
        self.start(name, src.at[pl.ds(start, rows)], dst)

    def own_row(self, name, src, dst):
        rows = src.shape[0]
        start = pl.multiple_of(lax.axis_index("ta") * rows, rows)
        self.start(name, src, dst.at[pl.ds(start, rows)])

    def wait(self, *names):
        for name in names:
            self.open.pop(name).wait()

    def drain(self):
        self.wait(*list(self.open))


class Steps:
    def __init__(self, pace=0.0):
        self.todo, self.pace, self.credit = [], pace, 0.0

    def spend(self, cost):
        self.credit += cost
        while self.todo and self.credit >= self.pace:
            self.credit -= self.pace
            self.step()

    def add(self, name, fn, *args, **kwargs):
        self.todo.append((name, partial(fn, *args, **kwargs)))

    def step(self, count=1):
        for _ in range(min(count, len(self.todo))):
            self.todo.pop(0)[1]()

    def until(self, name):
        while any(n == name for n, _ in self.todo):
            self.step()

    def drain(self):
        self.step(len(self.todo))


def join_groups(packed, joined):
    rows, width = packed.shape[2], packed.shape[3] // 4

    @pl.loop(0, packed.shape[1])
    def _(i):
        first, second = packed[0, i], packed[1, i]
        pieces = []
        for s in range(4):
            pieces += [first[:, s * width : (s + 1) * width], second[:, s * width : (s + 1) * width]]
        joined[block(i, rows), :] = jnp.concatenate(pieces, axis=1)


def gradient(source, rhs, store):
    product = tn(source, rhs)
    rows = product.shape[0] // 8
    for d in range(8):
        store(d, product[d * rows : (d + 1) * rows])


def head_masks(rows):
    lane = lax.broadcasted_iota(jnp.int32, (rows, 2 * HD), 1)
    return lane < HD


def keep_half(values, low_half, head):
    zero = jnp.zeros_like(values)
    return jnp.where(low_half, values, zero) if head == 0 else jnp.where(low_half, zero, values)


def attend(qkv, bias_of, causal, out, logsum, bias, between, after):
    rows, cols = out.shape
    size = RB if causal else bias.shape[0]

    def one(start, keys, pair):
        q_rows = pl.ds(start, size)
        lanes = slice(pair * 2 * HD, (pair + 1) * 2 * HD)
        key = qkv[0:keys, cols + pair * 2 * HD : cols + (pair + 1) * 2 * HD]
        value = qkv[0:keys, 2 * cols + pair * 2 * HD : 2 * cols + (pair + 1) * 2 * HD]
        query = qkv[q_rows, lanes]
        low_half = head_masks(size)
        outs, sums = [], []
        for head in range(2):
            scores = nt(keep_half(query, low_half, head), key) + bias[0:size, 0:keys]
            peak = jnp.max(scores, -1, keepdims=True)
            shifted = jnp.exp(scores - peak)
            total = jnp.sum(shifted, -1, keepdims=True)
            outs.append(nn(shifted.astype(BF), value) / total)
            sums.append(peak + jnp.log(total))
        out[q_rows, lanes] = jnp.where(low_half, outs[0], outs[1]).astype(BF)
        both = jnp.where(low_half, sums[0], sums[1]).T
        logsum[pair, :, q_rows] = jnp.concatenate([both[0:1], both[HD : HD + 1]], axis=0)

    for i in range(rows // size):
        keys = (i + 1) * size if causal else bias.shape[1]
        bias[0:size, 0:keys] = bias_of(i, size, keys)
        for pair in range(cols // (2 * HD)):
            one(i * size, keys, pair)
            between(size * keys * 3.4e-6)
        for k in range(size // RB):
            after(i * (size // RB) + k)


def attend_back(qkv, attended, grad, logsum, bias_of, causal, dqkv, dk_sum, dv_sum, k_turned, bias, between, after):
    rows, cols = attended.shape
    dk_sum[...] = jnp.zeros(dk_sum.shape, F32)
    dv_sum[...] = jnp.zeros(dv_sum.shape, F32)

    @pl.loop(0, k_turned.shape[1] // RB)
    def _(i):
        k_turned[:, block(i)] = qkv[block(i), cols : 2 * cols].T

    def one(q_rows, keys, pair):
        lanes = slice(pair * 2 * HD, (pair + 1) * 2 * HD)
        k_lanes = slice(cols + pair * 2 * HD, cols + (pair + 1) * 2 * HD)
        v_lanes = slice(2 * cols + pair * 2 * HD, 2 * cols + (pair + 1) * 2 * HD)
        query, key, value = qkv[q_rows, lanes], qkv[0:keys, k_lanes], qkv[0:keys, v_lanes]
        out_grad = grad[q_rows, lanes]
        low_half = head_masks(RB)
        product = (out_grad.astype(F32) * attended[q_rows, lanes].astype(F32)).T
        dk = dv = None
        dq = []
        for head in range(2):
            inner = jnp.sum(product[head * HD : (head + 1) * HD], 0, keepdims=True)
            q_head = keep_half(query, low_half, head)
            g_head = keep_half(out_grad, low_half, head)
            scores = nt(key, q_head) + bias[0:keys, :]
            weights = jnp.exp(scores - logsum[pair, head : head + 1, q_rows])
            weight_grad = nt(value, g_head)
            score_grad = (weights * (weight_grad - inner)).astype(BF)
            dv_part = nn(weights.astype(BF), g_head)
            dk_part = nn(score_grad, q_head)
            turned_rows = slice(pair * 2 * HD + head * HD, pair * 2 * HD + (head + 1) * HD)
            dq.append(nn(k_turned[turned_rows, 0:keys], score_grad))
            dv = dv_part if dv is None else dv + dv_part
            dk = dk_part if dk is None else dk + dk_part
        dqkv[q_rows, lanes] = (jnp.concatenate(dq, axis=0).T * (1.0 / math.sqrt(HD))).astype(BF)
        dk_sum[0:keys, lanes] += dk
        dv_sum[0:keys, lanes] += dv

    def settle(key_rows):
        dqkv[key_rows, cols : 2 * cols] = dk_sum[key_rows, :].astype(BF)
        dqkv[key_rows, 2 * cols : 3 * cols] = dv_sum[key_rows, :].astype(BF)

    for i in reversed(range(rows // RB)):
        keys = (i + 1) * RB if causal else bias.shape[0]
        bias[0:keys, :] = bias_of(i, keys)
        for pair in range(cols // (2 * HD)):
            one(pl.ds(i * RB, RB), keys, pair)
            between(RB * keys * 5.4e-6)
        if causal:
            settle(pl.ds(i * RB, RB))
        after(i)
    if not causal:
        pl.loop(0, dk_sum.shape[0] // RB)(lambda i: settle(block(i)))


def id_rows(seg, pad_len=None):
    ids = seg[pl.ds(lax.axis_index("ta"), 1), :]
    if pad_len is not None:
        live = ids.shape[1] - pad_len[lax.axis_index("ta")]
        ids = jnp.where(lax.broadcasted_iota(jnp.int32, ids.shape, 1) < live, ids, -1)
    return ids, jnp.broadcast_to(ids.astype(F32), (128, ids.shape[1])).T[:, 0:1].astype(jnp.int32)


def self_bias(q_ids, k_ids, i, rows, keys):
    same = q_ids[i * rows : (i + 1) * rows, :] == k_ids[:, 0:keys]
    q_pos = i * rows + lax.broadcasted_iota(jnp.int32, (rows, keys), 0)
    k_pos = lax.broadcasted_iota(jnp.int32, (rows, keys), 1)
    allowed = (same & (k_pos < q_pos)) | (k_pos == q_pos)
    return jnp.where(allowed, 0.0, NEG_FILL)


def self_bias_turned(q_ids, k_ids, i, keys):
    same = k_ids[0:keys, :] == q_ids[:, i * RB : (i + 1) * RB]
    q_pos = i * RB + lax.broadcasted_iota(jnp.int32, (keys, RB), 1)
    k_pos = lax.broadcasted_iota(jnp.int32, (keys, RB), 0)
    allowed = (same & (k_pos < q_pos)) | (k_pos == q_pos)
    return jnp.where(allowed, 0.0, NEG_FILL)


def cross_bias(q_ids, k_ids, i, rows, keys):
    return jnp.where(q_ids[i * rows : (i + 1) * rows, :] == k_ids[:, 0:keys], 0.0, NEG_FILL)


def cross_bias_turned(q_ids, k_ids, i, keys):
    return jnp.where(k_ids[0:keys, :] == q_ids[:, i * RB : (i + 1) * RB], 0.0, NEG_FILL)


def places():
    dp, ta = lax.axis_index("dp"), lax.axis_index("ta")
    return lax.div(dp, 2), lax.rem(dp, 2), ta


class Peers:
    def __init__(self, nz):
        self.nz = nz
        self.z, self.x, self.ta = places()
        self.ox, self.ot = 1 - self.x, 1 - self.ta
        self.x_peer = {"dp": self.z * 2 + self.ox}
        self.y_peer = {"ta": self.ot}
        self.tb = lax.axis_index("tb")
        self.core_peer = {"tb": 1 - self.tb}

    def up(self, j):
        return lax.rem(self.z + j, self.nz)

    def down(self, j):
        return lax.rem(self.z + (self.nz - j), self.nz)

    def z_peer(self, j):
        return {"dp": self.up(j) * 2 + self.x}

    def cube_peer(self, bits):
        turn = [bits >> 2 & 1, bits >> 1 & 1, bits & 1]
        x, ta, tb = [1 - v if t else v for v, t in zip((self.x, self.ta, self.tb), turn)]
        return {"dp": self.z * 2 + x, "ta": ta, "tb": tb}

    def row_peers(self):
        places = [(j, k) for j in range(self.nz) for k in range(2)][1:]
        return [((j, k), {"dp": self.up(j) * 2 + (self.ox if k else self.x)}) for j, k in places]

    def box_peers(self):
        places = [(j, t, k) for j in range(self.nz) for t in range(2) for k in range(2)][1:]
        return [
            ((j, t, k), {"dp": self.up(j) * 2 + (self.ox if k else self.x), "ta": self.ot if t else self.ta})
            for j, t, k in places
        ]

    def greet(self, plane, cube=False):
        others = [self.core_peer] if plane else [self.core_peer, self.y_peer]
        if plane:
            others += [peer for _, peer in self.box_peers()]
        if cube:
            others += [self.cube_peer(bits) for bits in (3, 5, 7)]
        barrier = pltpu.get_barrier_semaphore()
        for other in others:
            pl.semaphore_signal(barrier, inc=1, device_id=other, device_id_type=MESH_ID)
        pl.semaphore_wait(barrier, len(others))


SLOTS = 16


class Route:
    def __init__(self, peers, order, rows):
        self.p, self.order, self.rows = peers, order, rows
        self.sizes = {"z": peers.nz, "y": 2, "x": 2}
        self.places = [(z, y, x) for z in range(peers.nz) for y in range(2) for x in range(2)]
        self.places.sort(key=lambda place: (self.last(place), self.at(place, self.order[0])))

    def at(self, place, axis):
        return place["zyx".index(axis)]

    def last(self, place):
        return max([0] + [i + 1 for i, axis in enumerate(self.order) if self.at(place, axis)])

    def moved(self, place, axis, k):
        return tuple(k if a == axis else self.at(place, a) for a in "zyx")

    def beyond(self, place):
        return [
            (axis, k, self.moved(place, axis, k))
            for axis in self.order[self.last(place) :]
            for k in range(1, self.sizes[axis])
        ]

    def peer(self, axis, k):
        return {"z": self.p.z_peer(k), "y": self.p.y_peer, "x": self.p.x_peer}[axis]

    def index(self, place):
        return place[0] * 4 + place[1] * 2 + place[2]

    def spot(self, place, down):
        p = self.p
        z = p.down(place[0]) if down else p.up(place[0])
        return (p.ot if place[1] else p.ta), z * 2 + (p.ox if place[2] else p.x)


class Gather(Route):
    def __init__(self, peers, order, rows, out, send, recv, own):
        super().__init__(peers, order, rows)
        self.out, self.send, self.recv, self.own = out, send, recv, own

    def copy(self, place, new, peer):
        slot = self.out.at[(*self.spot(place, True), self.rows)]
        return pltpu.make_async_remote_copy(
            src_ref=slot if any(place) else self.own.at[self.rows], dst_ref=slot, send_sem=self.send.at[self.index(new)],
            recv_sem=self.recv.at[self.index(new)], device_id=peer, device_id_type=MESH_ID,
        )

    def arrived(self, place):
        slot = self.out.at[(*self.spot(place, True), self.rows)]
        pltpu.make_async_remote_copy(
            src_ref=slot, dst_ref=slot, send_sem=self.send.at[self.index(place)],
            recv_sem=self.recv.at[self.index(place)], device_id=self.p.y_peer, device_id_type=MESH_ID,
        ).wait_recv()

    def pass_on(self, place):
        if any(place):
            self.arrived(place)
        for axis, k, new in self.beyond(place):
            self.copy(place, new, self.peer(axis, k)).start()

    def finish(self):
        for place in self.places:
            if self.last(place) == 3:
                self.arrived(place)

    def close(self):
        for place in self.places:
            for axis, k, new in self.beyond(place):
                self.copy(place, new, self.peer(axis, k)).wait_send()


class Reduce(Route):
    def __init__(self, peers, order, rows, part, landing, relay, send, recv):
        super().__init__(peers, order, rows)
        self.part, self.landing, self.relay, self.send, self.recv = part, landing, relay, send, recv
        self.relayed = sorted([place for place in self.places if 0 < self.last(place) < 3], key=self.last, reverse=True)
        order = self.relayed + [(0, 0, 0)]
        firsts = [place for place in self.places if self.last(place) == 3]
        self.queue = sorted(firsts, key=lambda place: order.index(self.moved(place, self.order[2], 0)))

    def copy(self, place):
        axis = self.order[self.last(place) - 1]
        if self.last(place) == 3:
            src = self.part.at[(*self.spot(place, False), self.rows)]
        else:
            src = self.relay.at[self.relayed.index(place), self.rows]
        return pltpu.make_async_remote_copy(
            src_ref=src, dst_ref=self.landing.at[self.index(place), self.rows], send_sem=self.send.at[self.index(place)],
            recv_sem=self.recv.at[self.index(place)], device_id=self.peer(axis, self.at(place, axis)),
            device_id_type=MESH_ID,
        )

    def total(self, place):
        t, d = self.spot(place, False)
        total = self.part[t, d, self.rows, :].astype(F32)
        for _, _, new in self.beyond(place):
            self.copy(new).wait_recv()
            total = total + self.landing[self.index(new), self.rows, :].astype(F32)
        return total

    def start(self):
        self.feed(WINDOW)

    def feed(self, count):
        for _ in range(min(count, len(self.queue))):
            self.copy(self.queue.pop(0)).start()

    def pass_on(self, place):
        self.relay[self.relayed.index(place), self.rows, :] = self.total(place).astype(self.relay.dtype)
        self.copy(place).start()
        self.feed(FEED)

    def finish(self):
        self.feed(len(self.queue))
        total = self.total((0, 0, 0))
        for place in self.places:
            if any(place):
                self.copy(place).wait_send()
        return total


class Group:
    def __init__(self, works):
        self.works = works

    def start(self):
        for w in self.works:
            if isinstance(w, Gather):
                w.pass_on((0, 0, 0))
            else:
                w.start()

    def stages(self):
        lists = []
        for w in self.works:
            places = w.relayed if isinstance(w, Reduce) else [p for p in w.places if 0 < w.last(p) < 3]
            lists.append([(w, p) for p in places])
        count = max(len(places) for places in lists)
        return [[places[i] for places in lists if i < len(places)] for i in range(count)]

    def add_to(self, steps, name, between=None, at=None):
        for i, stage in enumerate(self.stages()):
            if i == at:
                steps.add(name, between)
            steps.add(name, self.run, stage)

    def run(self, stage):
        for w, place in stage:
            w.pass_on(place)

    def finish(self):
        totals = [w.finish() for w in self.works]
        return totals[0] if len(totals) == 1 else jnp.concatenate(totals) if totals[0] is not None else None

    def close(self):
        for w in self.works:
            w.close()


def gather_group(peers, split, out, send, recv, own):
    rows, works = 0, []
    for k, (order, count) in enumerate(split):
        works.append(Gather(peers, order, pl.ds(rows, count), out, send.at[k], recv.at[k], own))
        rows += count
    return Group(works)


def reduce_group(peers, split, part, landing, relay, send, recv):
    rows, works = 0, []
    for k, (order, count) in enumerate(split):
        works.append(Reduce(peers, order, pl.ds(rows, count), part, landing, relay, send.at[k], recv.at[k]))
        rows += count
    return Group(works)


def split_rows(rows, first, second, share):
    count = max(16, int(rows * share) // 16 * 16)
    return ((first, count), (second, rows - count))


class Swap:
    def __init__(self, peers, src, dst, send, recv, rows=RB):
        self.peer, self.src, self.dst, self.send, self.recv, self.rows = peers.core_peer, src, dst, send, recv, rows

    def copy(self, i):
        rows = block(i, self.rows)
        return pltpu.make_async_remote_copy(
            src_ref=self.src.at[rows], dst_ref=self.dst.at[rows], send_sem=self.send.at[i], recv_sem=self.recv.at[i],
            device_id=self.peer, device_id_type=MESH_ID,
        )

    def start(self, i):
        self.copy(i).start()

    def arrived(self, i):
        self.copy(i).wait_recv()

    def drain(self):
        for i in range(self.src.shape[0] // self.rows):
            self.copy(i).wait_send()


class Spread:
    def __init__(self, peers, src, dst, send, recv, parts):
        self.p, self.src, self.dst, self.send, self.recv, self.parts = peers, src, dst, send, recv, parts
        self.size = src.shape[0] // (2 * parts)

    def rows(self, core, i, ta=None):
        start = (2 * i + core) * self.size
        start = start if ta is None else ta * self.src.shape[0] + start
        return pl.ds(pl.multiple_of(start, self.size), self.size)

    def copy(self, src, dst_ta, core, i, hop, peer):
        return pltpu.make_async_remote_copy(
            src_ref=src, dst_ref=self.dst.at[self.rows(core, i, dst_ta)], send_sem=self.send.at[hop, i],
            recv_sem=self.recv.at[hop, i], device_id=peer, device_id_type=MESH_ID,
        )

    def across(self, i):
        p = self.p
        return self.copy(self.src.at[self.rows(p.tb, i)], p.ta, p.tb, i, 0, p.y_peer)

    def beside(self, i):
        p = self.p
        return self.copy(self.dst.at[self.rows(p.tb, i, p.ot)], p.ot, p.tb, i, 1, p.core_peer)

    def start(self, i):
        self.across(i).start()

    def pass_on(self, i):
        p = self.p
        self.copy(self.src.at[self.rows(p.tb, i)], p.ot, p.tb, i, 0, p.y_peer).wait_recv()
        self.beside(i).start()

    def finish(self):
        p = self.p
        for i in range(self.parts):
            self.copy(self.src.at[self.rows(p.tb, i)], p.ot, 1 - p.tb, i, 1, p.core_peer).wait_recv()
            self.across(i).wait_send()
            self.beside(i).wait_send()


def pack_rows(w_in, w_out):
    return jnp.concatenate([w_in[0], w_in[1], w_in[2], w_out[...].T], axis=1).astype(BF)


def forward_kernel(nz, gathers, r):
    peers = Peers(nz)
    local = Local(r.local)
    local.row("x", r.target, r.x)
    local.row("mem", r.memory, r.mem)
    local.row("cot", r.cotangent, r.cot)
    peers.greet(gathers)
    steps = Steps(FORWARD_PACE)
    packs = (r.w_self, r.w_cross, r.w_up, r.w_down)
    if gathers:
        here = peers.ta, peers.z * 2 + peers.x
        split = split_rows(r.stage.shape[1], "zyx", "xzy", 0.67)
        works = [gather_group(peers, split, g, r.g_send.at[k], r.g_recv.at[k], r.stage.at[k]) for k, g in enumerate(packs)]
        mine = peers.z * 2 + peers.x
        r.n_all[mine] = jnp.zeros(r.n_all.shape[1:], BF)
        r.n_all[mine, 0 : r.m_norm.shape[0], 0 : r.m_norm.shape[1]] = r.m_norm[...].astype(BF)

        def norm_copy(place, slot, peer):
            index = place[0] * 2 + place[1]
            return pltpu.make_async_remote_copy(
                src_ref=r.n_all.at[slot], dst_ref=r.n_all.at[slot], send_sem=r.n_send.at[index],
                recv_sem=r.n_recv.at[index], device_id=peer, device_id_type=MESH_ID,
            )

        for place, peer in peers.row_peers():
            norm_copy(place, mine, peer).start()
        r.stage[0] = pack_rows(r.m_self_in, r.m_self_out)
        works[0].start()
        local.start("own0", r.stage.at[0], packs[0].at[here])
        r.stage[1] = pack_rows(r.m_cross_in, r.m_cross_out)
        r.stage[2] = r.m_up[...].astype(BF)
        r.stage[3] = r.m_down[...].astype(BF)
        for k in range(1, 4):
            local.start("own%d" % k, r.stage.at[k], packs[k].at[here])
        first = Steps()
        works[0].add_to(first, "self", works[1].start, 5)
        first.drain()
        finish = Steps()
        for work in works:
            finish.add("close", work.close)
        for place, peer in peers.row_peers():
            slot = peers.down(place[0]) * 2 + (peers.ox if place[1] else peers.x)
            norm_copy(place, slot, peer).wait_recv()
            finish.add("norm", norm_copy(place, mine, peer).wait_send)
        span = r.m_norm.shape[1]
        feature = lax.broadcasted_iota(jnp.int32, (r.n_all.shape[2], r.x.shape[1]), 1)
        lane = lax.broadcasted_iota(jnp.int32, (r.n_all.shape[2], r.x.shape[1]), 0)
        norms = jnp.zeros((r.n_all.shape[1], r.x.shape[1]), F32)
        for d in range(2 * nz):
            norms += nn(r.n_all[d], ((feature == lane + d * span) & (lane < span)).astype(BF))
        r.norms[...] = norms
        timed = []
        for k, name in ((1, "cross"), (2, "up"), (3, "down")):
            begin = (k - 1) * STRIDE
            if k < 3:
                timed.append((begin + STRIDE - 3.5, name, works[k + 1].start))
            for i, stage in enumerate(works[k].stages()):
                timed.append((begin + i, name, partial(works[k].run, stage)))
        for _, name, fn in sorted(timed, key=lambda item: item[0]):
            steps.add(name, fn)
    norm_ref = r.norms
    blocks = r.x.shape[0] // RB
    cols = r.att_a.shape[1]
    local.wait("x", "mem")
    q_col, k_row, m_row = id_rows(r.tgt_seg)[1], id_rows(r.tgt_seg, r.pad_len)[0], id_rows(r.mem_seg)[0]

    @pl.loop(0, blocks)
    def _(i):
        r.n_a[block(i), :] = norm_forward(r.x[block(i), :].astype(F32), norm_ref[0:1, :], norm_ref[3:4, :])

    local.start("n_a", r.n_a, r.normed_one)
    if gathers:
        works[0].finish()
        local.wait("own0")
    local.start("raw_a", packs[0], r.raw)
    steps.spend(2.0)
    local.wait("raw_a")
    join_groups(r.raw, r.wj_a)
    steps.spend(2.0)

    wide = 2 * RB

    def project(normed, weights, qkv, i):
        q = nn(normed[block(i, wide), :], weights[:, 0:cols]).astype(BF).astype(F32) * (1.0 / math.sqrt(HD))
        qkv[block(i, wide), 0:cols] = q.astype(BF)

    def project_rest(source, weights, qkv, i):
        qkv[block(i, wide), cols : 3 * cols] = nn(source[block(i, wide), :], weights[:, cols : 3 * cols]).astype(BF)

    for i in range(blocks // 2):
        project(r.n_a, r.wj_a, r.qkv_a, i)
        steps.spend(0.6)
        project_rest(r.n_a, r.wj_a, r.qkv_a, i)
        steps.spend(1.0)
    local.start("qkv_a", r.qkv_a, r.qkv_one)
    swap_a = Swap(peers, r.own_a, r.other_a, r.s_send.at[0], r.s_recv.at[0])
    swap_b = Swap(peers, r.own_b, r.other_b, r.s_send.at[1], r.s_recv.at[1])

    def out_of(att, weights, own, swap, i):
        own[block(i), :] = nt(att[block(i), :], weights[:, 3 * cols : 4 * cols]).astype(BF)
        swap.start(i)
        steps.spend(0.4)

    attend(
        r.qkv_a, partial(self_bias, q_col, k_row), True, r.att_a, r.lse_one, r.bias,
        steps.spend, partial(out_of, r.att_a, r.wj_a, r.own_a, swap_a),
    )
    local.start("att_a", r.att_a, r.att_one)
    steps.until("cross")
    if gathers:
        works[1].finish()
        local.wait("own1")
    local.start("raw_b", packs[1], r.raw)
    local.wait("raw_b")
    join_groups(r.raw, r.wj_b)
    steps.spend(2.0)
    for i in range(blocks // 2):
        project_rest(r.mem, r.wj_b, r.qkv_b, i)
        steps.spend(1.0)
    for i in range(blocks):
        swap_a.arrived(i)
        h = r.x[block(i), :].astype(F32) + (r.own_a[block(i), :].astype(F32) + r.other_a[block(i), :].astype(F32))
        r.h_a[block(i), :] = h
        r.l_a[block(i), :] = h.astype(BF)
        r.n_b[block(i), :] = norm_forward(h, norm_ref[1:2, :], norm_ref[4:5, :])
        if i % 2 == 1:
            project(r.n_b, r.wj_b, r.qkv_b, i // 2)
            steps.spend(2.2)
    local.start("h_a", r.l_a, r.hidden_one)
    local.start("n_b", r.n_b, r.normed_two)
    local.start("qkv_b", r.qkv_b, r.qkv_two)
    attend(
        r.qkv_b, partial(cross_bias, q_col, m_row), False, r.att_b, r.lse_two, r.bias,
        steps.spend, partial(out_of, r.att_b, r.wj_b, r.own_b, swap_b),
    )
    local.start("att_b", r.att_b, r.att_two)
    for i in range(blocks):
        swap_b.arrived(i)
        h = r.h_a[block(i), :] + (r.own_b[block(i), :].astype(F32) + r.other_b[block(i), :].astype(F32))
        r.l_b[block(i), :] = h.astype(BF)
        r.n_c[block(i), :] = norm_forward(h, norm_ref[2:3, :], norm_ref[5:6, :])
        steps.spend(0.7)
    local.start("h_b", r.l_b, r.hidden_two)
    local.start("n_c", r.n_c, r.normed_three)
    steps.until("up")
    if gathers:
        works[2].finish()
        local.wait("own2")
    local.start("up", packs[2], r.raw)
    local.wait("up", "cot")
    depth, hidden = r.x.shape[1], r.active.shape[1] // 2
    for t in range(2):
        half = slice(t * hidden, (t + 1) * hidden)
        for i in range(blocks // 2):
            rows = block(i, wide)
            activated, slope = gelu_with_slope(nn(r.n_c[rows, :], r.raw[t].reshape(depth, hidden)))
            r.active[rows, half] = activated.astype(BF)
            r.slope[rows, half] = slope.astype(BF)
            steps.spend(1.0)
        local.start("active%d" % t, r.active.at[:, half], r.ffn_active.at[:, half])
        local.start("slope%d" % t, r.slope.at[:, half], r.ffn_slope.at[:, half])
        gradient(r.cot[...], r.active[:, half], store_into(r.p_down, t))
        steps.spend(1.5)
    local.start("p_down", r.p_down, r.g_down)
    swap_a.drain()
    swap_b.drain()
    steps.drain()
    if gathers:
        works[3].finish()
        finish.drain()
    local.drain()


def store_into(pack, t):
    def store(d, values):
        pack[t, d] = values.astype(BF)

    return store


def back_in(upstream, values, gain, residual, sums):
    delta, gain_part, shift_part = norm_backward(upstream, values, gain)
    sums[0:1, :] += gain_part
    sums[1:2, :] += shift_part
    return residual + delta


def store_joined(pack, first):
    def store(d, values):
        width = pack.shape[3] // 4
        for s in range(values.shape[1] // (2 * width)):
            for t in range(2):
                piece = values[:, (2 * s + t) * width : (2 * s + t + 1) * width].astype(BF)
                pack[t, d, :, (first + s) * width : (first + s + 1) * width] = piece

    return store


def middle_kernel(nz, reduces, r):
    peers = Peers(nz)
    local = Local(r.local)
    if reduces:
        local.start("p_down", r.g_down, r.p_down)
    local.row("cot", r.cotangent, r.cot)
    local.start("down", r.w_down, r.down)
    peers.greet(reduces)
    local.start("slope", r.ffn_slope, r.slope)
    local.start("up", r.w_up, r.up)
    depth, blocks, cols = r.h.shape[1], r.h.shape[0] // RB, r.k_turned.shape[0]
    qkv, att = r.active.at[:, 0 : 3 * cols], r.active.at[:, 3 * cols : 4 * cols]
    dqkv, grad = r.slope.at[:, 0 : 3 * cols], r.slope.at[:, 3 * cols : 4 * cols]
    dk_sum, dv_sum = r.dkv.at[:, 0:cols], r.dkv.at[:, cols : 2 * cols]
    hidden = r.active.shape[1] // 2
    row_low, own_q, own_m, p_cross = r.n3, r.own_d, r.own_p, r.up
    steps = Steps(MIDDLE_PACE)
    swap_p = Swap(peers, r.own_p, r.other_p, r.s_send.at[0], r.s_recv.at[0])
    swap_d = Swap(peers, r.own_d, r.other_d, r.s_send.at[1], r.s_recv.at[1])
    swap_q = Swap(peers, own_q, r.dn_other, r.s_send.at[2], r.s_recv.at[2])
    swap_m = Swap(peers, own_m, r.other_m, r.s_send.at[3], r.s_recv.at[3])
    spread = Spread(peers, row_low, r.block_rows, r.y_send, r.y_recv, 1)
    works = []
    if reduces:
        split = split_rows(r.landing.shape[2], "zxy", "yzx", 0.5)
        works = [
            reduce_group(peers, split, p, r.landing.at[k], r.relay.at[k], r.r_send.at[k], r.r_recv.at[k])
            for k, p in enumerate((r.p_down, r.p_up))
        ]
        local.wait("p_down")
        works[0].start()
        works[0].add_to(steps, "down")
    r.norm_sums[...] = jnp.zeros_like(r.norm_sums)
    local.wait("cot", "down", "slope", "up")
    local.start("n3", r.normed_three, r.n3)
    local.start("active", r.ffn_active, r.active)
    local.start("h", r.hidden_two, r.h)
    wide = 2 * RB

    @pl.loop(0, blocks // 2)
    def _(i):
        rows = block(i, wide)
        total = None
        for t in range(2):
            half = slice(t * hidden, (t + 1) * hidden)
            up, down = r.up[t].reshape(depth, hidden), r.down[t].reshape(depth, hidden)
            du = (nn(r.cot[rows, :], down) * r.slope[rows, half].astype(F32)).astype(BF)
            r.slope[rows, half] = du
            one = nt(du, up)
            total = one if total is None else total + one
        r.own_d[rows, :] = total.astype(BF)
        swap_d.start(2 * i)
        swap_d.start(2 * i + 1)

    local.start("raw", r.w_cross, r.up)
    steps.spend(6.0)
    local.wait("n3", "active")
    for t in range(2):
        gradient(r.n3[...], r.slope[:, t * hidden : (t + 1) * hidden], store_into(r.p_up, t))
        steps.spend(1.5)
    if reduces:
        works[1].start()
        works[1].add_to(steps, "up")
    else:
        local.start("p_up", r.p_up, r.out_up)

    @pl.loop(0, blocks // 2)
    def _(i):
        rows = block(i, wide)
        total = nt(r.active[rows, 0:hidden], r.down[0].reshape(depth, hidden))
        total += nt(r.active[rows, hidden : 2 * hidden], r.down[1].reshape(depth, hidden))
        r.own_p[rows, :] = total.astype(BF)
        swap_p.start(2 * i)
        swap_p.start(2 * i + 1)

    local.start("qkv", r.qkv_two, qkv)
    local.start("att", r.att_two, att)
    local.start("n", r.normed_two, r.n_in)
    local.row("mem", r.memory, r.mem)
    steps.spend(3.0)
    local.wait("raw", "h")
    join_groups(r.up, r.wj)
    for i in range(blocks):
        swap_d.arrived(i)
        upstream = r.own_d[block(i), :].astype(F32) + r.other_d[block(i), :].astype(F32)
        e = back_in(upstream, r.h[block(i), :].astype(F32), r.norms[2:3, :], r.cot[block(i), :].astype(F32), r.norm_sums)
        r.low[block(i), :] = e.astype(BF)
        grad[block(i), :] = nn(e.astype(BF), r.wj[:, 3 * cols : 4 * cols]).astype(BF)
    local.start("e", r.low, r.residual)
    steps.spend(5.0)
    for i in range(blocks):
        swap_p.arrived(i)
        row = r.h[block(i), :].astype(F32) + (r.own_p[block(i), :].astype(F32) + r.other_p[block(i), :].astype(F32))
        row_low[block(i), :] = row.astype(BF)
    local.own_row("row", row_low, r.block_rows)
    spread.start(0)
    local.wait("qkv", "att", "n", "mem")
    swap_d.drain()

    def after(i):
        own_q[block(i), :] = nt(dqkv[block(i), 0:cols], r.wj[:, 0:cols]).astype(BF)
        swap_q.start(i)
        steps.spend(0.4)

    gradient(r.low[...], att[...], store_joined(p_cross, 3))
    steps.spend(3.0)
    attend_back(
        qkv, att, grad, r.lse_two, partial(cross_bias_turned, id_rows(r.tgt_seg)[0], id_rows(r.mem_seg)[1]), False, dqkv, dk_sum, dv_sum,
        r.k_turned, r.bias, steps.spend, after,
    )
    spread.pass_on(0)
    swap_p.drain()
    for i in range(blocks):
        own_m[block(i), :] = nt(dqkv[block(i), cols : 3 * cols], r.wj[:, cols : 3 * cols]).astype(BF)
        swap_m.start(i)
    steps.spend(2.0)
    gradient(r.n_in[...], dqkv[:, 0:cols], store_joined(p_cross, 0))
    gradient(r.mem[...], dqkv[:, cols : 3 * cols], store_joined(p_cross, 1))
    local.start("p_cross", p_cross, r.out_cross)
    local.start("own_q", own_q, r.dn_own)
    local.wait("e")
    for i in range(blocks):
        swap_m.arrived(i)
        r.low[block(i), :] = (own_m[block(i), :].astype(F32) + r.other_m[block(i), :].astype(F32)).astype(BF)
    local.start("mem_row", r.low, r.mem_own)
    for i in range(blocks):
        swap_q.arrived(i)
    steps.drain()
    if reduces:
        for k, out in enumerate((r.red_down, r.red_up)):
            out[...] = works[k].finish()
    spread.finish()
    for swap in (swap_q, swap_m):
        swap.drain()
    local.drain()


def last_kernel(nz, reduces, tensor_size, r):
    peers = Peers(nz)
    local = Local(r.local)
    if reduces:
        local.start("p_cross", r.g_cross, r.p_cross)
    local.start("raw", r.w_self, r.raw)
    local.start("e", r.residual, r.e_in)
    local.start("own_d", r.dn_own, r.own_d)
    local.start("other_d", r.dn_other, r.other_d)
    local.start("h", r.hidden_one, r.h)
    peers.greet(reduces, cube=reduces)
    blocks, cols = r.h.shape[0] // RB, r.att.shape[1]
    steps = Steps(LAST_PACE)
    swap_q = Swap(peers, r.own_q, r.other_q, r.s_send.at[0], r.s_recv.at[0])
    spread_m = Spread(peers, r.mem_low, r.mem_rows, r.y_send.at[0], r.y_recv.at[0], 1)
    spread_t = Spread(peers, r.row_low, r.target_rows, r.y_send.at[1], r.y_recv.at[1], blocks)
    works = []
    if reduces:
        split = split_rows(r.landing.shape[2], "zxy", "yzx", 0.17)
        even = split_rows(r.landing.shape[2], "zxy", "yzx", 0.17)
        works = [
            reduce_group(peers, split, p, r.landing.at[k], r.relay.at[k], r.r_send.at[k], r.r_recv.at[k])
            for k, (p, split) in enumerate(((r.p_cross, split), (r.p_self, even)))
        ]
        local.wait("p_cross")
        works[0].start()
        works[0].add_to(steps, "cross")
    r.norm_sums[...] = jnp.zeros_like(r.norm_sums)
    local.wait("raw")
    join_groups(r.raw, r.wj)
    local.wait("e", "own_d", "other_d", "h")
    local.start("mem", r.mem_own, r.mem_low)
    local.start("qkv", r.qkv_one, r.qkv)
    local.start("att", r.att_one, r.att)
    local.start("n", r.normed_one, r.n_in)
    local.row("x", r.target, r.x)
    for i in range(blocks):
        upstream = r.own_d[block(i), :].astype(F32) + r.other_d[block(i), :].astype(F32)
        e = back_in(upstream, r.h[block(i), :].astype(F32), r.norms[1:2, :], r.e_in[block(i), :].astype(F32), r.norm_sums)
        r.e[block(i), :] = e
        r.low[block(i), :] = e.astype(BF)
        r.grad[block(i), :] = nn(e.astype(BF), r.wj[:, 3 * cols : 4 * cols]).astype(BF)
    local.wait("mem")
    local.own_row("mem_own", r.mem_low, r.mem_rows)
    spread_m.start(0)
    steps.spend(6.0)
    local.wait("qkv", "att", "n", "x")
    gradient(r.low[...], r.att[...], store_joined(r.p_self, 3))
    steps.spend(1.0)

    r.first_sums[...] = jnp.zeros_like(r.first_sums)

    def settle(i):
        swap_q.arrived(i)
        upstream = r.own_q[block(i), :].astype(F32) + r.other_q[block(i), :].astype(F32)
        row = back_in(upstream, r.x[block(i), :].astype(F32), r.norms[0:1, :], r.e[block(i), :], r.first_sums)
        r.row_low[block(i), :] = row.astype(BF)
        spread_t.start(i)

    def after(i):
        r.own_q[block(i), :] = nt(r.dqkv[block(i), :], r.wj[:, 0 : 3 * cols]).astype(BF)
        swap_q.start(i)
        if i + 1 < blocks:
            settle(i + 1)
        steps.spend(1.5)

    attend_back(
        r.qkv, r.att, r.grad, r.lse_one, partial(self_bias_turned, id_rows(r.tgt_seg)[0], id_rows(r.tgt_seg, r.pad_len)[1]), True, r.dqkv, r.dk_sum, r.dv_sum,
        r.k_turned, r.bias, steps.spend, after,
    )
    gradient(r.n_in[...], r.dqkv[...], store_joined(r.p_self, 0))
    if reduces:
        works[1].start()
        works[1].add_to(steps, "self")
    else:
        local.start("p_self", r.p_self, r.out_self)
    settle(0)
    local.own_row("row", r.row_low, r.target_rows)
    if reduces:
        depth, span = r.x.shape[1], r.x.shape[1] // (2 * nz)
        sums = jnp.concatenate(
            [r.first_sums[0:1], r.norm_sums[0:1], r.third_sums[0:1], r.first_sums[1:2], r.norm_sums[1:2]]
            + [r.third_sums[1:2], jnp.zeros((10, depth), F32)]
        ).astype(BF)
        feature = lax.broadcasted_iota(jnp.int32, (r.p_norm.shape[2], depth), 1)
        lane = lax.broadcasted_iota(jnp.int32, (r.p_norm.shape[2], depth), 0)
        for d in range(2 * nz):
            piece = nt(sums, ((feature == lane + d * span) & (lane < span)).astype(BF)).astype(BF)
            r.p_norm[d] = piece

        def norm_copy(place, peer):
            index = place[0] * 4 + place[1] * 2 + place[2]
            return pltpu.make_async_remote_copy(
                src_ref=r.p_norm.at[peer["dp"]], dst_ref=r.n_landing.at[index], send_sem=r.n_send.at[index],
                recv_sem=r.n_recv.at[index], device_id=peer, device_id_type=MESH_ID,
            )

        for place, peer in peers.box_peers():
            norm_copy(place, peer).start()
        spread_m.pass_on(0)
        for i in reversed(range(1, blocks)):
            spread_t.pass_on(i)
        steps.drain()
        norm_grad = r.p_norm[peers.z * 2 + peers.x].astype(F32)
        for place, peer in peers.box_peers():
            norm_copy(place, peer).wait_recv()
            norm_grad = norm_grad + r.n_landing[place[0] * 4 + place[1] * 2 + place[2]].astype(F32)
        r.red_norm[...] = norm_grad
        squares = jnp.sum(jnp.sum(norm_grad * norm_grad, -1, keepdims=True), 0, keepdims=True) / tensor_size
        for k, out in enumerate((r.red_cross, r.red_self)):
            total = works[k].finish()
            out[...] = total
            squares = squares + jnp.sum(jnp.sum(total * total, -1, keepdims=True), 0, keepdims=True)
        for place, peer in peers.box_peers():
            norm_copy(place, peer).wait_send()
        for done in (r.red_up, r.red_down):
            squares = squares + jnp.sum(jnp.sum(done[...] * done[...], -1, keepdims=True), 0, keepdims=True)
        r.squares[...] = sum_everywhere(peers, squares, r.heard, r.q_send, r.q_recv)
    else:
        spread_m.pass_on(0)
        for i in reversed(range(1, blocks)):
            spread_t.pass_on(i)
    spread_t.pass_on(0)
    spread_m.finish()
    spread_t.finish()
    swap_q.drain()
    local.drain()


def sum_everywhere(peers, value, heard, send, recv):
    nz = peers.nz

    def copy(step, src, dst, peer):
        return pltpu.make_async_remote_copy(
            src_ref=heard.at[src], dst_ref=heard.at[dst], send_sem=send.at[step], recv_sem=recv.at[step],
            device_id=peer, device_id_type=MESH_ID,
        )

    heard[peers.z] = jnp.broadcast_to(value, heard.shape[1:])
    for j in range(1, nz):
        copy(j - 1, peers.z, peers.z, peers.z_peer(j)).start()
    for j in range(1, nz):
        copy(j - 1, peers.z, peers.down(j), peers.z_peer(j)).wait_recv()
    total = heard[0]
    for k in range(1, nz):
        total = total + heard[k]

    def place(bits):
        spots = ((peers.x, 4), (peers.ta, 2), (peers.tb, 1))
        return nz + sum((1 - v if bits & weight else v) * weight for v, weight in spots)

    heard[place(0)] = total
    for bits in range(1, 8):
        copy(nz - 2 + bits, place(0), place(0), peers.cube_peer(bits)).start()
    for bits in range(1, 8):
        copy(nz - 2 + bits, place(0), place(bits), peers.cube_peer(bits)).wait_recv()
    for j in range(1, nz):
        copy(j - 1, peers.z, peers.z, peers.z_peer(j)).wait_send()
    for bits in range(1, 8):
        copy(nz - 2 + bits, place(0), place(0), peers.cube_peer(bits)).wait_send()
    total = heard[nz]
    for k in range(1, 8):
        total = total + heard[nz + k]
    return total


def adam_update(weight, gradient, first, second, clip_factor, bias_one, bias_two, rate, decay):
    scaled = gradient * clip_factor
    first_new = BETA_ONE * first + (1.0 - BETA_ONE) * scaled
    second_new = BETA_TWO * second + (1.0 - BETA_TWO) * scaled * scaled
    first_hat = first_new / bias_one
    second_hat = second_new / bias_two
    weight_new = weight - rate * (first_hat / (jnp.sqrt(second_hat) + EPS_ADAM) + decay * weight)
    return weight_new, weight_new.astype(BF), first_new, second_new


RATES = (
    (RATE_MATRIX, DECAY_RATE),
    (RATE_OUTPUT, DECAY_RATE),
    (RATE_MATRIX, DECAY_RATE),
    (RATE_OUTPUT, DECAY_RATE),
    (RATE_MATRIX, DECAY_RATE),
    (RATE_MATRIX, DECAY_RATE),
    (RATE_NORMS, 0.0),
)


def shard_gradients(reduced, width):
    g_self, g_cross, g_up, g_down, g_norms = reduced
    cut = [
        [g[:, s * width : (s + 1) * width] for s in range(4)] for g in (g_self, g_cross)
    ]
    return (cut[0][:3], cut[0][3].T, cut[1][:3], cut[1][3].T, g_up, g_down.T, g_norms)


def adam_kernel(*refs):
    reduced, squares, biases = refs[:5], refs[5], refs[6]
    state, norm_out, outs = refs[7:28], refs[28], refs[29:]
    width = state[3].shape[0]
    norm = jnp.sqrt(squares[...])
    norm_out[...] = norm
    clip = (CLIP_LIMIT / jnp.maximum(norm, CLIP_LIMIT))[0:1, 0:1]
    values = [r[...] for r in reduced]
    shape = state[18].shape
    values[4] = values[4][0 : shape[0], 0 : shape[1]]
    gradients = list(shard_gradients(values, width))
    gradients[5] = values[3]
    for k, (rate, decay) in enumerate(RATES):
        weight, first, second = state[3 * k : 3 * k + 3]
        into = outs[4 * k : 4 * k + 4]
        if isinstance(gradients[k], list):
            for s in range(3):
                new = adam_update(
                    weight[s], gradients[k][s], first[s], second[s], clip, biases[0], biases[1], rate, decay
                )
                for ref, value in zip(into, new):
                    ref[s] = value
        else:
            new = adam_update(
                weight[...], gradients[k], first[...], second[...], clip, biases[0], biases[1], rate, decay
            )
            for ref, value in zip(into, new):
                ref[...] = value


def closing_kernel(count, *refs):
    ins, outs = refs[:31], refs[31:63]
    held, made, came, went = refs[63:90], refs[90:119], refs[119], refs[120]
    step = pl.program_id(0)
    sources = ins[3:9] + ins[10:]

    def bring(k):
        return pltpu.make_async_copy(sources[k], held[k], came.at[k])

    def put(k):
        return pltpu.make_async_copy(made[k], outs[3 + k], went.at[k])

    @pl.when(step == 0)
    def _():
        for k in range(len(held)):
            bring(k).start()

    @pl.when(step == 1)
    def _():
        for k in range(len(held)):
            bring(k).wait()
        adam_kernel(*held[:6], ins[9], *held[6:], *made)
        for k in range(len(made)):
            put(k).start()

    for src, dst in zip(ins[:3], outs[:3]):
        dst[...] = src[...].astype(F32)

    @pl.when(step == count - 1)
    def _():
        for k in range(len(made)):
            put(k).wait()


def closing(rows, reduced, squares, biases, state):
    count, depth = rows[0].shape
    spec = pl.BlockSpec((2 * RB, depth), lambda i: (i, 0))
    out_shape = [sds((count, depth), F32)] * 3 + [sds((8, 128), F32)]
    out_shape += [sds(w.shape, dt) for w in state[::3] for dt in (F32, BF, F32, F32)]
    held = (*reduced, squares, *state)
    outs = pl.pallas_call(
        partial(closing_kernel, count // (2 * RB)),
        name="closing",
        out_shape=out_shape,
        grid=(count // (2 * RB),),
        in_specs=[spec] * 3 + anym(6) + [pl.BlockSpec(memory_space=pltpu.SMEM)] + anym(21),
        out_specs=[spec] * 3 + anym(29),
        scratch_shapes=[pltpu.VMEM(a.shape, a.dtype) for a in (*held, *out_shape[3:])]
        + [pltpu.SemaphoreType.DMA((len(held),)), pltpu.SemaphoreType.DMA((29,))],
        compiler_params=params(),
    )(*rows, *reduced, squares, biases, *state)
    return outs[:3], outs[3][0, 0], list(outs[4:])


def body(target, memory, cotangent, tgt_seg, mem_seg, pad_len, step_count, *state):
    dp_size, tensor_size = lax.axis_size("dp"), lax.axis_size("ta") * lax.axis_size("tb")
    self_in, self_out, cross_in, cross_out, ffn_in, ffn_out, norm_params = state[::3]
    length, depth = tgt_seg.shape[1], target.shape[1]
    mem_length = mem_seg.shape[1]
    width, span = self_out.shape
    cols, hidden = 2 * width, ffn_in.shape[1]
    fold = depth // 8
    own_transfers = dp_size == 8
    nz = dp_size // 2 if own_transfers else 1
    blocks = length // RB

    row, mem_row = (length, depth), (mem_length, depth)
    qkv, att, logsum = (length, 3 * cols), (length, cols), (cols // 128, 2, length)
    pack = (2, 8, fold, 4 * width)
    wide = (2, 8, fold, hidden)
    joined = (depth, 4 * cols)
    dma = pltpu.SemaphoreType.DMA

    def v(shape, dtype=BF):
        return pltpu.VMEM(shape, dtype)

    ins = dict(
        target=(target, 0), memory=(memory, 0), cotangent=(cotangent, 0), tgt_seg=(tgt_seg, 1), mem_seg=(mem_seg, 1),
        pad_len=(pad_len, 2),
    )
    outs = dict(
        hidden_one=(row, BF, 0), hidden_two=(row, BF, 0), normed_one=(row, BF, 0), normed_two=(row, BF, 0),
        qkv_one=(qkv, BF, 0), qkv_two=(qkv, BF, 0), att_one=(att, BF, 0), att_two=(att, BF, 0),
        lse_one=(logsum, F32, 1), lse_two=(logsum, F32, 1), normed_three=(row, BF, 0),
        ffn_active=((length, 2 * hidden), BF, 0), ffn_slope=((length, 2 * hidden), BF, 0), g_down=(wide, BF, 0),
    )
    scratch = dict(
        cot=v(row), n_c=v(row), active=v((length, 2 * hidden)), slope=v((length, 2 * hidden)), p_down=v(wide),
        x=v(row), mem=v(mem_row), raw=v(pack), wj_a=v(joined), wj_b=v(joined), n_a=v(row), n_b=v(row),
        qkv_a=v(qkv), qkv_b=v(qkv), att_a=v(att), att_b=v(att), h_a=v(row, F32), l_a=v(row), l_b=v(row),
        own_a=v(row), other_a=v(row), own_b=v(row), other_b=v(row), bias=v((2 * RB, max(length, mem_length)), F32),
        s_send=dma((2, blocks)), s_recv=dma((2, blocks)), local=dma((24,)),
    )
    if own_transfers:
        ins |= dict(
            m_self_in=(self_in, 1), m_self_out=(self_out, 1), m_cross_in=(cross_in, 1), m_cross_out=(cross_out, 1),
            m_up=(ffn_in, 1), m_down=(ffn_out.T, 1), m_norm=(norm_params, 1),
        )
        outs |= dict(
            w_self=(pack, BF, 0), w_cross=(pack, BF, 0), w_up=(wide, BF, 0), w_down=(wide, BF, 0),
            norms=((16, depth), F32, 1),
        )
        scratch |= dict(
            stage=v((4, fold, 4 * width)), n_all=v((dp_size, 16, 128)), g_send=dma((4, 2, SLOTS)),
            g_recv=dma((4, 2, SLOTS)), n_send=dma((dp_size,)), n_recv=dma((dp_size,)),
        )
    else:
        norm_shard = jnp.zeros((16, span), BF).at[: norm_params.shape[0]].set(norm_params.astype(BF))
        shards = [
            jnp.concatenate([w_in[0], w_in[1], w_in[2], w_out.T], axis=1).astype(BF)
            for w_in, w_out in ((self_in, self_out), (cross_in, cross_out))
        ]
        shards += [ffn_in.astype(BF), ffn_out.T.astype(BF)]
        gathered = [
            lax.all_gather(lax.all_gather(s, "dp", axis=0, tiled=True), "ta", axis=0).reshape(2, 8, fold, s.shape[1])
            for s in shards
        ]
        norms = lax.all_gather(norm_shard, "dp", axis=1, tiled=True).astype(F32)
        ins |= dict(zip(("w_self", "w_cross", "w_up", "w_down"), ((g, 0) for g in gathered))) | dict(norms=(norms, 1))
    f = launch(
        partial(forward_kernel, nz, own_transfers), "forward", ins, outs, scratch, length * depth * 8 * cols,
        collective_id=0, has_side_effects=True,
    )
    if own_transfers:
        w_self, w_cross, w_up, w_down, norms = f.w_self, f.w_cross, f.w_up, f.w_down, f.norms
    else:
        w_self, w_cross, w_up, w_down = gathered

    ins = dict(
        hidden_two=(f.hidden_two, 0), cotangent=(cotangent, 0), w_up=(w_up, 0), w_down=(w_down, 0),
        w_cross=(w_cross, 0), qkv_two=(f.qkv_two, 0), att_two=(f.att_two, 0), normed_two=(f.normed_two, 0),
        memory=(memory, 0), lse_two=(f.lse_two, 1), norms=(norms, 1), tgt_seg=(tgt_seg, 1), mem_seg=(mem_seg, 1),
        normed_three=(f.normed_three, 0), ffn_active=(f.ffn_active, 0), ffn_slope=(f.ffn_slope, 0),
    )
    outs = dict(
        residual=(row, BF, 0), dn_own=(row, BF, 0), dn_other=(row, BF, 0),
        block_rows=((2 * length, depth), BF, 0), mem_own=(mem_row, BF, 0), out_cross=(pack, BF, 0), norm_sums=((8, depth), F32, 1),
    )
    back = dict(
        wj=v(joined), low=v(row), n_in=v(row), h=v(row),
        own_d=v(row), other_d=v(row), local=dma((24,)), y_send=dma((2, 2, blocks)), y_recv=dma((2, 2, blocks)),
    )
    sums_m = dict(dkv=v((mem_length, 2 * cols), F32), bias=v((mem_length, RB), F32), k_turned=v((cols, mem_length)))
    sums_s = dict(
        dk_sum=v((length, cols), F32), dv_sum=v((length, cols), F32), bias=v((length, RB), F32),
        k_turned=v((cols, length)),
    )
    reducing = dict(
        landing=v((2, SLOTS, fold, 4 * width)), relay=v((2, 2 * nz - 1, fold, 4 * width)), r_send=dma((2, 2, SLOTS)),
        r_recv=dma((2, 2, SLOTS)),
    )
    scratch = back | sums_m | dict(
        mem=v(mem_row), up=v(wide), down=v(wide), cot=v(row), n3=v(row), active=v((length, 2 * hidden)),
        slope=v((length, 2 * hidden)), own_p=v(row), other_p=v(row), other_m=v(mem_row),
        p_up=v(wide), p_down=v(wide), s_send=dma((4, blocks)), s_recv=dma((4, blocks)),
        y_send=dma((2, 1)), y_recv=dma((2, 1)),
    )
    if own_transfers:
        ins |= dict(g_down=(f.g_down, 0))
        outs |= dict(red_down=((span, hidden), F32, 1), red_up=((span, hidden), F32, 1))
        scratch |= reducing
    else:
        outs |= dict(out_up=(wide, BF, 0))
    m = launch(
        partial(middle_kernel, nz, own_transfers), "middle", ins, outs, scratch, length * depth * (12 * hidden),
        collective_id=1, has_side_effects=True,
    )

    ins = dict(
        residual=(m.residual, 0), dn_own=(m.dn_own, 0), dn_other=(m.dn_other, 0), hidden_one=(f.hidden_one, 0),
        w_self=(w_self, 0), qkv_one=(f.qkv_one, 0), att_one=(f.att_one, 0), normed_one=(f.normed_one, 0),
        target=(target, 0), mem_own=(m.mem_own, 0), lse_one=(f.lse_one, 1), norms=(norms, 1), tgt_seg=(tgt_seg, 1),
        pad_len=(pad_len, 2), third_sums=(m.norm_sums, 1),
    )
    outs = dict(
        target_rows=((2 * length, depth), BF, 0), mem_rows=((2 * mem_length, depth), BF, 0),
        norm_sums=((8, depth), F32, 1), first_sums=((8, depth), F32, 1),
    )
    scratch = back | sums_s | dict(
        e_in=v(row), e=v(row, F32),        raw=v(pack), x=v(row), mem_low=v(mem_row), other_q=v(row), p_self=v(pack), s_send=dma((1, blocks)),
        s_recv=dma((1, blocks)), qkv=v(qkv), att=v(att), dqkv=v(qkv), grad=v(att), row_low=v(row), own_q=v(row),
    )
    if own_transfers:
        ins |= dict(g_cross=(m.out_cross, 0), red_up=(m.red_up, 1), red_down=(m.red_down, 1))
        shard = ((span, 4 * width), F32, 1)
        outs |= dict(red_cross=shard, red_self=shard, red_norm=((16, 128), F32, 1), squares=((8, 128), F32, 1))
        scratch |= reducing | dict(
            p_cross=v(pack), p_norm=v((dp_size, 16, 128)), n_landing=v((SLOTS, 16, 128)), n_send=dma((SLOTS,)),
            n_recv=dma((SLOTS,)), heard=v((nz + 8, 8, 128), F32), q_send=dma((nz + 6,)),
            q_recv=dma((nz + 6,)),
        )
    else:
        outs |= dict(out_self=(pack, BF, 0))
    b = launch(
        partial(last_kernel, nz, own_transfers, tensor_size), "last", ins, outs, scratch, length * depth * 16 * cols,
        collective_id=2, has_side_effects=True,
    )

    step_float = step_count.astype(F32)
    biases = jnp.stack([1.0 - jnp.power(BETA_ONE, step_float), 1.0 - jnp.power(BETA_TWO, step_float)])
    if own_transfers:
        turn = [a.T if 15 <= k < 18 else a for k, a in enumerate(state)]
        rows, global_norm, updated = closing(
            (m.block_rows, b.target_rows, b.mem_rows),
            (b.red_self, b.red_cross, m.red_up, m.red_down, b.red_norm), b.squares, biases, turn,
        )
        updated[20:24] = [a.T for a in updated[20:24]]
    else:
        sums = (b.first_sums, b.norm_sums, m.norm_sums)
        all_sums = jnp.stack([s[k] for k in range(2) for s in sums]).astype(BF).astype(F32)
        norm_part = lax.psum_scatter(lax.psum(all_sums, "ta"), "dp", scatter_dimension=1, tiled=True)
        reduced = []
        for g in (b.out_self, m.out_cross, m.out_up, f.g_down):
            g = lax.psum_scatter(g.astype(F32), "ta", scatter_dimension=0).reshape(depth, g.shape[3])
            reduced.append(lax.psum_scatter(g, "dp", scatter_dimension=0, tiled=True))
        total = sum(jnp.sum(g * g) for g in reduced) + jnp.sum(norm_part * norm_part) / tensor_size
        global_norm = jnp.sqrt(lax.psum(total, ("dp", "ta", "tb")))
        clip = CLIP_LIMIT / jnp.maximum(global_norm, CLIP_LIMIT)
        updated = []
        for k, g in enumerate(shard_gradients(reduced + [norm_part], width)):
            g = jnp.stack(g) if isinstance(g, list) else g
            weight, first, second = state[3 * k : 3 * k + 3]
            updated += adam_update(weight, g, first, second, clip, biases[0], biases[1], *RATES[k])
        rows = [a.astype(F32) for a in (m.block_rows, b.target_rows, b.mem_rows)]
    return (global_norm, *rows, *updated)


def solution(mesh):
    dp_size, tensor_size = mesh.shape["dp"], mesh.shape["tensor"]
    grid = Mesh(mesh.devices.reshape(dp_size, 2, tensor_size // 2), ("dp", "ta", "tb"))
    tensor = ("ta", "tb")
    rows = P("dp", None)
    place = (
        P(None, "dp", tensor),
        P(tensor, "dp"),
        P(None, "dp", tensor),
        P(tensor, "dp"),
        P("dp", tensor),
        P(tensor, "dp"),
        P(None, "dp"),
    )
    return jax.shard_map(
        body,
        mesh=grid,
        in_specs=(rows,) * 5 + (P("dp"), P()) + tuple(p for p in place for _ in range(3)),
        out_specs=(P(), rows, rows, rows) + tuple(p for p in place for _ in range(4)),
        check_vma=False,
    )
```
